128 devices in a mesh: inst: 4 (over z), seq: 32 (over y, x, core).
Axes of the slice: x: 4, y: 4, z: 4, core: 2. Of those that a mesh axis runs over, the one named last changes fastest.
Arguments:
- kv_pool: bfloat16 [4096, 128, 2048], P(('inst', 'seq')), may hold values from -6 to 6
- queries: bfloat16 [2, 32, 8192], P(None, 'inst', 'seq'), may hold values from -260 to 260
- new_kv: bfloat16 [2, 32, 2048], P(None, 'inst', 'seq'), may hold values from -6 to 6
- lengths: int32 [32], replicated, may hold values from 4097 to 16384, as said below
- block_dev: int32 [32, 128], replicated, may hold values from -1 to 127, as said below
- block_slot: int32 [32, 128], replicated, may hold values from -1 to 31, as said below
- owner_dev: int32 [2, 32], replicated, may hold values from 0 to 127, as said below
- owner_row: int32 [2, 32], replicated, may hold values from 0 to 3, as said below
Outputs:
- attn_out: bfloat16 [2, 32, 8192], P(None, 'inst', 'seq')
- tail_kv: bfloat16 [512, 2048], P(('inst', 'seq'))
The draws below stay inside these ranges and needn't reach their ends.
Inputs may be any that keep to these rules, and one draw needn't show every extreme that they name: `lengths`: in each index of inst one request of the instance has exactly 16384 tokens. `block_dev`: entries b < ceil(lengths[r] / 128) name distinct (device, slot) pairs with block_slot, on any device of the slice; all later entries are -1 in both tables. `block_slot`: see block_dev. No two new rows share a pair (owner_dev, owner_row). `owner_row`: see owner_dev.
All inputs are finite; a program needn't handle non-finite values.
Results may differ from the reference program's by a relative error of at most 0.0027.
Values may be sent and summed in bfloat16 or wider, within the bound.
A program may use at most 128 MiB of HBM per device.

```python
import math
import jax
import jax.numpy as jnp
from jax import lax

H = 64
KVH = 8
HD = 128
BLOCK = 128
STEPS = 2
TAIL = 4
SLOTS_DEV = 32
REQ_INST = 8
REQS = 32
MAXBLK = 128
N_INST = 4
N_SEQ = 32


def shared_lengths(key):
    key = jax.random.fold_in(key, 101)
    first_key, second_key = jax.random.split(key)
    low_len = BLOCK * (MAXBLK // 4) + 1
    high_len = BLOCK * MAXBLK
    raw_len = jax.random.randint(first_key, (N_INST, REQ_INST), low_len, high_len + 1)
    longest = jax.random.randint(second_key, (N_INST, 1), 0, REQ_INST)
    column = jnp.arange(REQ_INST)[None, :]
    return jnp.where(column == longest, high_len, raw_len).reshape(REQS).astype(jnp.int32)


def shared_places(key):
    lengths = shared_lengths(key)
    key = jax.random.fold_in(key, 102)
    total = N_INST * N_SEQ * SLOTS_DEV
    picked = jax.random.permutation(key, total)[:REQS * MAXBLK].reshape(REQS, MAXBLK)
    device = picked // SLOTS_DEV
    slot_index = picked % SLOTS_DEV
    block_index = jnp.arange(MAXBLK)[None, :]
    needed = (lengths + BLOCK - 1) // BLOCK
    used_mask = block_index < needed[:, None]
    device = jnp.where(used_mask, device, -1).astype(jnp.int32)
    slot_index = jnp.where(used_mask, slot_index, -1).astype(jnp.int32)
    return (device, slot_index)


def shared_owners(key):
    key = jax.random.fold_in(key, 103)
    picked = jax.random.permutation(key, N_INST * N_SEQ * TAIL)[:STEPS * REQS].reshape(STEPS, REQS)
    return ((picked // TAIL).astype(jnp.int32), (picked % TAIL).astype(jnp.int32))


def draw_lengths(key, part):
    values = shared_lengths(key)
    return values


def draw_block_dev(key, part):
    places = shared_places(key)
    return places[0]


def draw_block_slot(key, part):
    places = shared_places(key)
    return places[1]


def draw_owner_dev(key, part):
    owners = shared_owners(key)
    return owners[0]


def draw_owner_row(key, part):
    owners = shared_owners(key)
    return owners[1]


def draw_queries(key, part):
    key = jax.random.fold_in(key, 7)
    first_key, second_key, third_key = jax.random.split(key, 3)
    shape = (STEPS, REQS, H, HD)
    base_draw = jnp.clip(jax.random.normal(first_key, shape, jnp.float32), -6.0, 6.0)
    head_scale = jnp.exp(jax.random.uniform(second_key, (1, REQS, H, 1), jnp.float32, math.log(1.5), math.log(3.5)))
    sharp_mask = jax.random.bernoulli(third_key, 0.125, (1, REQS, H, 1))
    head_scale = jnp.where(sharp_mask, head_scale * 12.0, head_scale)
    return (base_draw * head_scale).reshape(STEPS, REQS, H * HD).astype(jnp.bfloat16)


def block_scale(own_key, dims, pieces, low, largest):
    def one(dim, parts):
        heights = jax.random.uniform(jax.random.fold_in(jax.random.fold_in(own_key, 6), dim), (parts,), jnp.float32, low / len(pieces), largest / len(pieces))
        return jnp.repeat(jnp.exp(heights), dims[dim] // parts).reshape((-1,) + (1,) * (len(dims) - dim - 1))

    factor_of = one(*pieces[0])
    for cut in pieces[1:]:
        factor_of = factor_of * one(*cut)
    return factor_of


def gaussian(own_key, shape, width, most, pieces=(), held_as=jnp.bfloat16):
    result = jax.random.normal(own_key, shape, jnp.float32) * width
    if len(pieces) > 0:
        result = block_scale(own_key, shape, pieces, -0.22, 0.18) * result
    return jnp.clip(result, min=-most, max=most).astype(held_as)


def setup_inputs(seed: int = 0) -> dict:
    key_of = jax.random.split(jax.random.key(seed), 9)
    return {
        "kv_pool": gaussian(key_of[0], (N_INST * N_SEQ * SLOTS_DEV, BLOCK, 2 * KVH * HD), 1.0, 6.0, ((0, 128),)),
        "queries": draw_queries(jax.random.fold_in(key_of[8], 71), 0),
        "new_kv": gaussian(key_of[2], (STEPS, REQS, 2 * KVH * HD), 1.0, 6.0, ((1, 4), (2, 32))),
        "lengths": draw_lengths(jax.random.fold_in(key_of[8], 71), 0),
        "block_dev": draw_block_dev(jax.random.fold_in(key_of[8], 71), 0),
        "block_slot": draw_block_slot(jax.random.fold_in(key_of[8], 71), 0),
        "owner_dev": draw_owner_dev(jax.random.fold_in(key_of[8], 71), 0),
        "owner_row": draw_owner_row(jax.random.fold_in(key_of[8], 71), 0),
    }


masked_low = -1e+30

def group_terms(scores, valid_mask):
    masked = jnp.where(valid_mask, scores, masked_low)
    peak_value = lax.optimization_barrier(jnp.max(masked, axis=-1))
    weights = jnp.where(valid_mask, jnp.exp(masked - peak_value[..., None]), 0.0).astype(jnp.bfloat16)
    totals = lax.optimization_barrier(jnp.sum(weights.astype(jnp.float32), axis=-1))
    return (peak_value, weights, totals)

def reference(kv_pool, queries, new_kv, lengths, block_dev, block_slot, owner_dev, owner_row):
    groups = H // KVH
    head_scale = 1.0 / math.sqrt(HD)
    highest = lax.Precision.HIGHEST
    q_all = queries.astype(jnp.float32).reshape(STEPS, REQS, KVH, groups, HD)
    new_rows = new_kv.astype(jnp.float32).reshape(STEPS, REQS, 2, KVH, HD)
    flat_index = jnp.where(block_dev >= 0, block_dev * SLOTS_DEV + block_slot, 0).astype(jnp.int32)
    step_order = jnp.arange(STEPS, dtype=jnp.int32)
    reach_mask = step_order[None, :] <= step_order[:, None]
    position = jnp.arange(MAXBLK, dtype=jnp.int32)[:, None] * BLOCK + jnp.arange(BLOCK, dtype=jnp.int32)[None, :]

    def one_request(request):
        cache_rows = jnp.take(kv_pool, flat_index[request], axis=0).astype(jnp.float32)
        key_rows = cache_rows[..., :KVH * HD].reshape(MAXBLK, BLOCK, KVH, HD)
        value_rows = cache_rows[..., KVH * HD:].reshape(MAXBLK, BLOCK, KVH, HD)
        query_rows = q_all[:, request]
        scores = jnp.einsum('sgqd,btgd->sgqbt', query_rows, key_rows, precision=highest) * head_scale
        valid_mask = position < lengths[request]
        peak_block, weights, totals = group_terms(scores, valid_mask)
        num_block = jnp.einsum('sgqbt,btgd->sgqbd', weights.astype(jnp.float32), value_rows, precision=highest)
        new_keys = new_rows[:, request, 0]
        new_values = new_rows[:, request, 1]
        scores_new = jnp.einsum('sgqd,jgd->sgqj', query_rows, new_keys, precision=highest) * head_scale
        peak_new, weights_new, totals_new = group_terms(scores_new, reach_mask[:, None, None, :])
        num_new = jnp.einsum('sgqj,jgd->sgqd', weights_new.astype(jnp.float32), new_values, precision=highest)
        top_peak = jnp.maximum(lax.optimization_barrier(jnp.max(peak_block, axis=-1)), peak_new)
        factor = jnp.exp(peak_block - top_peak[..., None])
        factor_new = jnp.exp(peak_new - top_peak)
        den_sum = lax.optimization_barrier(jnp.sum(totals * factor, axis=-1)) + totals_new * factor_new
        num_sum = jnp.einsum('sgqb,sgqbd->sgqd', factor, num_block, precision=highest) + num_new * factor_new[..., None]
        return (num_sum / den_sum[..., None]).astype(jnp.bfloat16).reshape(STEPS, H * HD)
    attention = lax.map(one_request, jnp.arange(REQS, dtype=jnp.int32))
    attn_out = jnp.transpose(attention, (1, 0, 2))
    tail_index = (owner_dev * TAIL + owner_row).reshape(-1).astype(jnp.int32)
    tail_kv = jnp.zeros((N_INST * N_SEQ * TAIL, 2 * KVH * HD), jnp.bfloat16).at[tail_index].set(new_kv.reshape(STEPS * REQS, 2 * KVH * HD))
    return (attn_out, tail_kv)
```

```python
import math

import jax
import jax.numpy as jnp
from jax import lax
from jax.experimental import pallas as pl
from jax.experimental.pallas import tpu as pltpu
from jax.sharding import PartitionSpec as P

MESH = pl.DeviceIdType.MESH
F32 = jnp.float32
BF16 = jnp.bfloat16
I32 = jnp.int32

N = 4
CHIPS = 64
SLOTS = 32
REQS = 32
LOW = -1e30
SCALE = 1.0 / math.sqrt(128)
UNROLL = 4
KV_PARTS = SLOTS // UNROLL


def iota(shape, dim):
    return lax.broadcasted_iota(I32, shape, dim)


def halves(first, second, late):
    lane = iota(first.shape, 1)
    if late is True:
        return jnp.where(lane < 64, pltpu.roll(first, 64, 1), second)
    if late is False:
        return jnp.where(lane < 64, first, pltpu.roll(second, 64, 1))
    low = jnp.where(late, pltpu.roll(first, 64, 1), first)
    high = jnp.where(late, second, pltpu.roll(second, 64, 1))
    return jnp.where(lane < 64, low, high)


def kernel(
    kv, q, nk, dev, slot, own_dev, own_row, lens, out, tail,
    kvb, gat, gq, gn, qr, wb, cb, mb, db, fb, mx, dx, mc, mt, dt, s32, r32, sb, rb, ss, rs, meta, smeta, codes,
    kv_sem, sa, ra, sbx, rbx, s_sib, r_sib, m_sems, s_chunk, r_chunk, all_sems, meta_sem,
):
    z = lax.axis_index("inst")
    c = lax.axis_index("seq")
    y, x, core = c // 8, (c // 2) % 4, c % 2
    me = z * 32 + c
    chip = z * 16 + y * 4 + x
    sib = 1 - core
    sibling = (z, y * 8 + x * 2 + sib)

    def place(pz, py, px):
        return (pz, py * 8 + px * 2 + core)

    def kv_copy(part):
        span = pl.ds(part * UNROLL, UNROLL)
        return pltpu.make_async_copy(kv.at[span], kvb.at[span], kv_sem.at[part])

    @pl.loop(0, KV_PARTS)
    def _(part):
        kv_copy(part).start()

    barrier = pltpu.get_barrier_semaphore()

    @pl.loop(1, CHIPS)
    def _(d):
        peer = place((z + d // 16) % 4, (y + (d // 4) % 4) % 4, (x + d % 4) % 4)
        pl.semaphore_signal(barrier, inc=1, device_id=peer, device_id_type=MESH)

    pl.semaphore_signal(barrier, inc=1, device_id=sibling, device_id_type=MESH)

    for s in range(2):
        own = q[s].astype(F32)
        gat[s, core, z, y, x] = jnp.concatenate([own[:, :128], own[:, 128:]], axis=0).astype(BF16)
    fresh = jnp.concatenate([nk[0].astype(F32), nk[1].astype(F32)], axis=1)
    gat[2, core, z, y, x] = jnp.concatenate([fresh, jnp.zeros((8, 128), F32)], axis=0).astype(BF16)

    pl.semaphore_wait(barrier, CHIPS)

    def moved(u, da, db):
        if u == 0:
            return z, (y + da) % 4, (x + db) % 4
        if u == 1:
            return (z + da) % 4, y, (x + db) % 4
        return (z + da) % 4, (y + db) % 4, x

    def plane_copy(u, d, at, to):
        block = gat.at[u, core, at[0], at[1], at[2]]
        return pltpu.make_async_remote_copy(
            src_ref=block, dst_ref=block, send_sem=sa.at[u, d], recv_sem=ra.at[u, d],
            device_id=place(*to), device_id_type=MESH,
        )

    for u in range(3):
        @pl.loop(1, 16)
        def _(d):
            plane_copy(u, d, (z, y, x), moved(u, d // 4, d % 4)).start()

    mine = jnp.where(dev[...] == me, slot[...], -1)
    code = iota((REQS, 128), 0) * 128 + iota((REQS, 128), 1) + 1
    for n in range(SLOTS):
        codes[n : n + 1, :] = jnp.sum(jnp.where(mine == n, code, 0), axis=0, keepdims=True)
    owned = jnp.where(own_dev[...] == me, own_row[...], -1)
    row_code = iota((2, REQS), 0) * REQS + iota((2, REQS), 1) + 1
    for e in range(8):
        hit = jnp.sum(jnp.where(owned == e, row_code, 0), axis=0, keepdims=True)
        codes[SLOTS + e : SLOTS + e + 1, :] = jnp.concatenate([hit, jnp.zeros((1, 96), I32)], axis=1)
    found = jnp.broadcast_to(jnp.sum(codes[...], axis=1, keepdims=True), (40, 128))
    held = found[:SLOTS]
    req_col = jnp.where(held > 0, jnp.minimum((held - 1) >> 7, REQS - 1), -1)
    rows, lanes = iota((SLOTS, 128), 0), iota((SLOTS, 128), 1)
    req_row = jnp.sum(jnp.where(rows == lanes, req_col, 0), axis=0, keepdims=True)
    req_row = jnp.where(lanes < SLOTS, jnp.broadcast_to(req_row, (SLOTS, 128)), -2)
    before = jnp.max(jnp.where((req_row == req_col) & (lanes < rows), lanes, -1), axis=1, keepdims=True)
    last = jnp.max(jnp.where(req_row == rows, lanes, -1), axis=1, keepdims=True)
    meta[:SLOTS] = jnp.where(
        lanes == 0, req_col, jnp.where(lanes == 1, held, jnp.where(lanes == 2, before, last))
    )
    meta[SLOTS:] = found[SLOTS:]
    meta_copy = pltpu.make_async_copy(meta, smeta, meta_sem)
    meta_copy.start()

    def axis_copy(u, k, at):
        if u == 0:
            block, to = gat.at[0, core, at], place((at + k) % 4, y, x)
        elif u == 1:
            block, to = gat.at[1, core, :, at], place(z, (at + k) % 4, x)
        else:
            block, to = gat.at[2, core, :, :, at], place(z, y, (at + k) % 4)
        return pltpu.make_async_remote_copy(
            src_ref=block, dst_ref=block, send_sem=sbx.at[u, k], recv_sem=rbx.at[u, k],
            device_id=to, device_id_type=MESH,
        )

    def sib_copy(u, of):
        block = gat.at[u, of]
        return pltpu.make_async_remote_copy(
            src_ref=block, dst_ref=block, send_sem=s_sib.at[u], recv_sem=r_sib.at[u],
            device_id=sibling, device_id_type=MESH,
        )

    here = (z, y, x)
    for u in range(3):
        @pl.loop(1, 16)
        def _(d):
            plane_copy(u, d, moved(u, 4 - d // 4, 4 - d % 4), here).wait_recv()

        for k in range(1, 4):
            axis_copy(u, k, here[u]).start()
    for u in range(3):
        for k in range(1, 4):
            axis_copy(u, k, (here[u] + 4 - k) % 4).wait_recv()
        sib_copy(u, core).start()
    meta_copy.wait()
    for u in range(3):
        sib_copy(u, sib).wait_recv()

    @pl.loop(0, 8)
    def _(k):
        of, i = k // 4, k % 4
        for j in range(16):
            for s in range(2):
                gq[of, i, pl.ds(j * 32 + s * 16, 16), :] = gat[s, of, i, j // 4, j % 4].astype(F32)
            gn[of, i, pl.ds(j * 8, 8), :] = gat[2, of, i, j // 4, j % 4].astype(F32)[:8]

    @pl.loop(0, REQS)
    def _(r):
        i, rl = r // 8, r % 8
        parts = [gq[of, i, pl.ds(rl, 64, stride=8), :].reshape(8, 8, 128) for of in range(2)]
        qr[r] = jnp.concatenate(parts, axis=1).astype(BF16)

    token = iota((128, 128), 0)
    blank = jnp.zeros((16, 128), BF16)

    @pl.loop(0, KV_PARTS)
    def _(part):
        kv_copy(part).wait()
        for e in range(UNROLL):
            n = part * UNROLL + e
            r = jnp.maximum(smeta[n, 0], 0)
            b = (jnp.maximum(smeta[n, 1], 1) - 1) % 128
            count = jnp.where(smeta[n, 1] > 0, lens[r] - b * 128, 0)
            heads = qr[r]
            score = jnp.zeros((128, 128), F32)
            for kt in range(4):
                rows_of = []
                for g in range(8):
                    if g == 2 * kt:
                        rows_of.append(jnp.concatenate([heads[g], blank], axis=1))
                    elif g == 2 * kt + 1:
                        rows_of.append(jnp.concatenate([blank, heads[g]], axis=1))
                    else:
                        rows_of.append(jnp.concatenate([blank, blank], axis=1))
                score = score + lax.dot_general(
                    kvb[n, :, kt * 256 : kt * 256 + 256], jnp.concatenate(rows_of, axis=0),
                    (((1,), (1,)), ((), ())), preferred_element_type=F32,
                )
            valid = token < count
            score = jnp.where(valid, score * SCALE, LOW)
            peak = jnp.max(score, axis=0, keepdims=True)
            w = jnp.where(valid, jnp.exp(score - peak), 0.0).astype(BF16).astype(F32)
            mb[pl.ds(n, 1), :] = peak
            db[pl.ds(n, 1), :] = jnp.sum(w, axis=0, keepdims=True)
            wb[n] = w.T.astype(BF16)

    rows = iota((REQS, 128), 0)
    top = jnp.full((REQS, 128), LOW, F32)
    for n in range(SLOTS):
        top = jnp.where(rows == smeta[n, 0], jnp.maximum(top, mb[n : n + 1, :]), top)
    mx[0] = top

    def pair_copy(buf, k):
        return pltpu.make_async_remote_copy(
            src_ref=buf.at[0], dst_ref=buf.at[1], send_sem=m_sems.at[2 * k], recv_sem=m_sems.at[2 * k + 1],
            device_id=sibling, device_id_type=MESH,
        )

    pair_copy(mx, 0).start()

    @pl.loop(0, KV_PARTS)
    def _(part):
        for e in range(UNROLL):
            n = part * UNROLL + e
            for kt in range(4):
                both = jnp.dot(
                    wb[n, kt * 32 : kt * 32 + 32, :], kvb[n, :, 1024 + kt * 256 : 1280 + kt * 256],
                    preferred_element_type=F32,
                )
                cb[n, kt * 32 : kt * 32 + 16, :] = both[:16, :128]
                cb[n, kt * 32 + 16 : kt * 32 + 32, :] = both[16:, 128:]

    pair_copy(mx, 0).wait_recv()
    chip_top = jnp.maximum(top, mx[1])
    mc[...] = chip_top
    den = jnp.zeros((REQS, 128), F32)
    fb[...] = jnp.zeros((128, 128), F32)
    for n in range(SLOTS):
        r = smeta[n, 0]
        factor = jnp.exp(mb[n : n + 1, :] - mc[pl.ds(jnp.maximum(r, 0), 1), :])
        fb[n : n + 1, :] = factor
        den = den + jnp.where(rows == r, factor * db[n : n + 1, :], 0.0)
    dx[0] = den
    pair_copy(dx, 1).start()
    fb[...] = fb[...].T

    def chunk_copy(kt):
        return pltpu.make_async_remote_copy(
            src_ref=s32.at[sib, :, pl.ds(pl.multiple_of(kt * 128, 128), 128), :], dst_ref=r32.at[kt],
            send_sem=s_chunk.at[kt], recv_sem=r_chunk.at[kt], device_id=sibling, device_id_type=MESH,
        )

    @pl.loop(0, 4)
    def _(k):
        kt = (y + k) % 4
        span = pl.ds(pl.multiple_of(kt * 32, 32), 32)
        scales = fb[span, :]
        for n in range(SLOTS):
            prev = smeta[n, 2]
            earlier = jnp.where(prev >= 0, cb[jnp.maximum(prev, 0), span, :], 0.0)
            cb[n, span, :] = cb[n, span, :] * scales[:, n : n + 1] + earlier
        for r in range(REQS):
            end = smeta[r, 3]
            sums = jnp.where(end >= 0, cb[jnp.maximum(end, 0), span, :], 0.0)
            for xh in range(2):
                for of in range(2):
                    start = kt * 128 + xh * 64 + r % 8
                    s32[of, r // 8, pl.ds(start, 8, stride=8), :] = sums[xh * 16 + of * 8 : xh * 16 + of * 8 + 8]
        chunk_copy(kt).start()

    pair_copy(dx, 1).wait_recv()
    chip_den = dx[0] + dx[1]
    pad = jnp.zeros((96, 128), F32)
    mt[...] = jnp.concatenate([chip_top, pad], axis=0).T
    dt[...] = jnp.concatenate([chip_den, pad], axis=0).T
    lane8 = iota((8, 128), 1)
    for i in range(4):
        for xl in range(2):
            packed = jnp.zeros((8, 128), F32)
            for t in range(4):
                for w, src in ((0, mt), (1, dt)):
                    got = src[pl.ds(core * 8 + xl * 4 + t, 8, stride=16), :]
                    to = w * 32 + t * 8
                    got = pltpu.roll(got, (to - 8 * i) % 128, 1)
                    packed = jnp.where((lane8 >= to) & (lane8 < to + 8), got, packed)
            for g in range(8):
                ss[i * 16 + g * 2 + xl] = packed[g : g + 1, :]

    def block_copy(to_chip, to):
        return pltpu.make_async_remote_copy(
            src_ref=sb.at[to_chip], dst_ref=rb.at[chip], send_sem=all_sems.at[0], recv_sem=all_sems.at[1],
            device_id=to, device_id_type=MESH,
        )

    def side_copy(to_chip, to):
        return pltpu.make_async_remote_copy(
            src_ref=ss.at[to_chip], dst_ref=rs.at[chip], send_sem=all_sems.at[2], recv_sem=all_sems.at[3],
            device_id=to, device_id_type=MESH,
        )

    rs[chip] = ss[chip]

    @pl.loop(0, 4)
    def _(k):
        kt = (y + k) % 4
        chunk_copy(kt).wait_recv()
        for i in range(4):
            for j in range(4):
                at = pl.ds(pl.multiple_of(kt * 128 + j * 32, 32), 32)
                total = s32[core, i, at, :] + r32[kt, i, j * 32 : j * 32 + 32, :]
                sb[i * 16 + kt * 4 + j] = total.astype(BF16)

        @pl.loop(0, 16)
        def _(d):
            pz, px = (z + d // 4) % 4, (x + d % 4) % 4
            to_chip, to = pz * 16 + kt * 4 + px, place(pz, kt, px)

            @pl.when(k * 16 + d > 0)
            def _():
                block_copy(to_chip, to).start()
                side_copy(to_chip, to).start()

    rb[chip] = sb[chip]

    for e in range(4):
        found_row = smeta[SLOTS + e, 0]
        which = jnp.maximum(found_row - 1, 0)
        late, r = which // 32, which % 32
        pair = [gn[of, r // 8, pl.ds(r % 8, 16, stride=8), :] for of in range(2)]
        tail[e] = jnp.where(found_row > 0, halves(pair[0], pair[1], late > 0), 0.0).astype(BF16)

    head = y * 2 + x // 2
    new_rows = []
    for at in (head, head + 8):
        pair = [gn[of, z, pl.ds(pl.multiple_of(at * 8, 8), 8), :] for of in range(2)]
        new_rows.append([halves(pair[0], pair[1], late) for late in (False, True)])
    new_m, new_den, new_num = [], [], []
    for t in range(4):
        mine_q = q[t // 2].astype(F32)[:, (t % 2) * 128 : (t % 2) * 128 + 128]
        found_scores = [
            jnp.sum(mine_q * new_rows[0][j], axis=1, keepdims=True) * SCALE for j in range(t // 2 + 1)
        ]
        peak = found_scores[0]
        for more in found_scores[1:]:
            peak = jnp.maximum(peak, more)
        ws = [jnp.exp(v - peak).astype(BF16).astype(F32) for v in found_scores]
        new_m.append(peak)
        new_den.append(sum(ws[1:], ws[0]))
        num = ws[0] * new_rows[1][0]
        for j in range(1, len(ws)):
            num = num + ws[j] * new_rows[1][j]
        new_num.append(num)
    new_m = jnp.concatenate(new_m, axis=0)
    new_den = jnp.concatenate(new_den, axis=0)
    new_num = jnp.concatenate(new_num, axis=0)

    most = pl.ds(0, CHIPS - 1)
    all_blocks = pltpu.make_async_remote_copy(
        src_ref=sb.at[most], dst_ref=rb.at[most], send_sem=all_sems.at[0], recv_sem=all_sems.at[1],
        device_id=sibling, device_id_type=MESH,
    )
    all_sides = pltpu.make_async_remote_copy(
        src_ref=ss.at[most], dst_ref=rs.at[most], send_sem=all_sems.at[2], recv_sem=all_sems.at[3],
        device_id=sibling, device_id_type=MESH,
    )
    all_sides.wait_recv()
    side = rs[...].reshape(CHIPS, 128)
    side = jnp.concatenate([side, jnp.zeros((128 - CHIPS, 128), F32)], axis=0).T
    side_m, side_den = side[0:32, :CHIPS], side[32:64, :CHIPS]
    final_m = jnp.maximum(jnp.max(side_m, axis=1, keepdims=True), new_m)
    scales = jnp.exp(side_m - final_m)
    new_scale = jnp.exp(new_m - final_m)
    final_den = jnp.sum(scales * side_den, axis=1, keepdims=True) + new_den * new_scale
    total = new_num * new_scale
    all_blocks.wait_recv()
    for k in range(CHIPS):
        total = total + scales[:, k : k + 1] * rb[k].astype(F32)
    result = total / final_den
    for t in range(4):
        out[t // 2, :, (t % 2) * 128 : (t % 2) * 128 + 128] = result[t * 8 : t * 8 + 8].astype(BF16)

    all_blocks.wait_send()
    all_sides.wait_send()
    for u in range(3):
        @pl.loop(1, 16)
        def _(d):
            plane_copy(u, d, here, moved(u, d // 4, d % 4)).wait_send()

        for k in range(1, 4):
            axis_copy(u, k, here[u]).wait_send()
        sib_copy(u, core).wait_send()
    pair_copy(mx, 0).wait_send()
    pair_copy(dx, 1).wait_send()

    @pl.loop(0, 4)
    def _(k):
        chunk_copy(k).wait_send()


def per_device(kv_pool, queries, new_kv, lengths, block_dev, block_slot, owner_dev, owner_row):
    vmem = pl.BlockSpec(memory_space=pltpu.VMEM)
    dma = pltpu.SemaphoreType.DMA
    result, tail = pl.pallas_call(
        kernel,
        out_shape=(
            jax.ShapeDtypeStruct((2, 8, 256), BF16),
            jax.ShapeDtypeStruct((4, 16, 128), BF16),
        ),
        in_specs=[pl.BlockSpec(memory_space=pl.ANY)] + [vmem] * 6 + [pl.BlockSpec(memory_space=pltpu.SMEM)],
        out_specs=(vmem, vmem),
        scratch_shapes=[
            pltpu.VMEM((SLOTS, 128, 2048), BF16),
            pltpu.VMEM((3, 2, 4, 4, 4, 16, 128), BF16),
            pltpu.VMEM((2, 4, 512, 128), F32),
            pltpu.VMEM((2, 4, 128, 128), F32),
            pltpu.VMEM((REQS, 8, 16, 128), BF16),
            pltpu.VMEM((SLOTS, 128, 128), BF16),
            pltpu.VMEM((SLOTS, 128, 128), F32),
            pltpu.VMEM((SLOTS, 128), F32),
            pltpu.VMEM((SLOTS, 128), F32),
            pltpu.VMEM((128, 128), F32),
            pltpu.VMEM((2, REQS, 128), F32),
            pltpu.VMEM((2, REQS, 128), F32),
            pltpu.VMEM((REQS, 128), F32),
            pltpu.VMEM((128, 128), F32),
            pltpu.VMEM((128, 128), F32),
            pltpu.VMEM((2, 4, 512, 128), F32),
            pltpu.VMEM((4, 4, 128, 128), F32),
            pltpu.VMEM((CHIPS, 32, 128), BF16),
            pltpu.VMEM((CHIPS, 32, 128), BF16),
            pltpu.VMEM((CHIPS, 1, 128), F32),
            pltpu.VMEM((CHIPS, 1, 128), F32),
            pltpu.VMEM((40, 128), I32),
            pltpu.SMEM((40, 128), I32),
            pltpu.VMEM((40, 128), I32),
            dma((KV_PARTS,)),
            dma((3, 16)),
            dma((3, 16)),
            dma((3, 4)),
            dma((3, 4)),
            dma((3,)),
            dma((3,)),
            dma((4,)),
            dma((4,)),
            dma((4,)),
            dma((4,)),
            dma,
        ],
        compiler_params=pltpu.CompilerParams(
            collective_id=0, has_side_effects=True, vmem_limit_bytes=56 * 1024 * 1024
        ),
    )(kv_pool, queries, new_kv, block_dev, block_slot, owner_dev, owner_row, lengths)
    return result, tail.reshape(4, 2048)


def solution(mesh):
    placed = (
        P(("inst", "seq"), None, None),
        P(None, "inst", "seq"),
        P(None, "inst", "seq"),
        P(),
        P(),
        P(),
        P(),
        P(),
    )
    return jax.shard_map(
        per_device,
        mesh=mesh,
        in_specs=placed,
        out_specs=(P(None, "inst", "seq"), P(("inst", "seq"), None)),
        check_vma=False,
    )
```

```python
import math

import jax
import jax.numpy as jnp
from jax import lax
from jax.experimental import pallas as pl
from jax.experimental.pallas import tpu as pltpu
from jax.sharding import PartitionSpec as P

MESH = pl.DeviceIdType.MESH
F32 = jnp.float32
BF16 = jnp.bfloat16
I32 = jnp.int32

N = 4
CHIPS = 64
SLOTS = 32
REQS = 32
LOW = -1e30
SCALE = 1.0 / math.sqrt(128)
UNROLL = 4
GROUP = 8
KV_PARTS = SLOTS // UNROLL
FAR_FIRST = (3, 2, 1, 0)


def iota(shape, dim):
    return lax.broadcasted_iota(I32, shape, dim)


def halves(first, second, late):
    lane = iota(first.shape, 1)
    if late is True:
        return jnp.where(lane < 64, pltpu.roll(first, 64, 1), second)
    if late is False:
        return jnp.where(lane < 64, first, pltpu.roll(second, 64, 1))
    low = jnp.where(late, pltpu.roll(first, 64, 1), first)
    high = jnp.where(late, second, pltpu.roll(second, 64, 1))
    return jnp.where(lane < 64, low, high)


def kernel(
    kv, q, nk, dev, slot, own_dev, own_row, lens, out, tail,
    kvb, gat, gnb, gq, gn, wb, cb, mb, db, fb, mx, lift, mc, mt, dt, s32, r32, sb, rb, ss, rs, tl, meta, smeta, codes,
    k_sem, v_sem, sg, rg, s_sib, r_sib, m_sems, s_chunk, r_chunk, all_sems, meta_sem,
):
    z = lax.axis_index("inst")
    c = lax.axis_index("seq")
    y, x, core = c // 8, (c // 2) % 4, c % 2
    me = z * 32 + c
    chip = z * 16 + y * 4 + x
    sib = 1 - core
    sibling = (z, y * 8 + x * 2 + sib)

    def place(pz, py, px):
        return (pz, py * 8 + px * 2 + core)

    def offset(d):
        return (z + d // 16) % 4, (y + (d // 4) % 4) % 4, (x + d % 4) % 4

    barrier = pltpu.get_barrier_semaphore()

    @pl.loop(1, CHIPS)
    def _(d):
        pl.semaphore_signal(barrier, inc=1, device_id=place(*offset(d)), device_id_type=MESH)

    pl.semaphore_signal(barrier, inc=1, device_id=sibling, device_id_type=MESH)

    def key_copy(part):
        span = pl.ds(part * UNROLL, UNROLL)
        cols = pl.ds(0, 1024)
        return pltpu.make_async_copy(kv.at[span, :, cols], kvb.at[span, :, cols], k_sem.at[part])

    def value_copy(part):
        span = pl.ds(part * UNROLL, UNROLL)
        cols = pl.ds(1024, 1024)
        return pltpu.make_async_copy(kv.at[span, :, cols], kvb.at[span, :, cols], v_sem.at[part])

    @pl.loop(0, KV_PARTS)
    def _(part):
        key_copy(part).start()

    spot = y * 4 + x
    own = [q[s].astype(F32) for s in range(2)]
    gat[core, z, spot] = jnp.concatenate(
        [own[0][:, :128], own[0][:, 128:], own[1][:, :128], own[1][:, 128:]], axis=0
    ).astype(BF16)
    fresh = jnp.concatenate([nk[0].astype(F32), nk[1].astype(F32)], axis=1)
    gnb[core, chip] = jnp.concatenate([fresh, jnp.zeros((8, 128), F32)], axis=0).astype(BF16)

    pl.semaphore_wait(barrier, CHIPS)

    def query_copy(d):
        block = gat.at[core, z, spot]
        return pltpu.make_async_remote_copy(
            src_ref=block, dst_ref=block, send_sem=sg.at[d // 16], recv_sem=rg.at[d // 16],
            device_id=place(*offset(d)), device_id_type=MESH,
        )

    def fresh_copy(d):
        block = gnb.at[core, chip]
        return pltpu.make_async_remote_copy(
            src_ref=block, dst_ref=block, send_sem=sg.at[4], recv_sem=rg.at[4],
            device_id=place(*offset(d)), device_id_type=MESH,
        )

    def plane_wait(dz):
        at = (z + 4 - dz) % 4
        block = gat.at[core, at] if dz else gat.at[core, at, pl.ds(0, 15)]
        return pltpu.make_async_remote_copy(
            src_ref=block, dst_ref=block, send_sem=sg.at[dz], recv_sem=rg.at[dz],
            device_id=sibling, device_id_type=MESH,
        )

    def sib_copy(dz, of):
        block = gat.at[of, (z + 4 - dz) % 4]
        return pltpu.make_async_remote_copy(
            src_ref=block, dst_ref=block, send_sem=s_sib.at[dz], recv_sem=r_sib.at[dz],
            device_id=sibling, device_id_type=MESH,
        )

    def sib_fresh(of):
        block = gnb.at[of]
        return pltpu.make_async_remote_copy(
            src_ref=block, dst_ref=block, send_sem=s_sib.at[4], recv_sem=r_sib.at[4],
            device_id=sibling, device_id_type=MESH,
        )

    def fresh_wait():
        block = gnb.at[core, pl.ds(0, CHIPS - 1)]
        return pltpu.make_async_remote_copy(
            src_ref=block, dst_ref=block, send_sem=sg.at[4], recv_sem=rg.at[4],
            device_id=sibling, device_id_type=MESH,
        )

    @pl.loop(0, CHIPS - 1)
    def _(d):
        query_copy(CHIPS - 1 - d).start()

    @pl.loop(0, KV_PARTS)
    def _(part):
        value_copy(part).start()

    @pl.loop(1, CHIPS)
    def _(d):
        fresh_copy(d).start()

    mine = jnp.where(dev[...] == me, slot[...], -1)
    code = iota((REQS, 128), 0) * 128 + iota((REQS, 128), 1) + 1

    @pl.loop(0, SLOTS // 4)
    def _(group):
        for e in range(4):
            n = group * 4 + e
            codes[pl.ds(n, 1), :] = jnp.sum(jnp.where(mine == n, code, 0), axis=0, keepdims=True)

    owned = jnp.where(own_dev[...] == me, own_row[...], -1)
    row_code = iota((2, REQS), 0) * REQS + iota((2, REQS), 1) + 1
    pad_row = jnp.zeros((1, 96), I32)
    for e in range(4):
        hit = jnp.sum(jnp.where(owned == e, row_code, 0), axis=0, keepdims=True)
        codes[SLOTS + e : SLOTS + e + 1, :] = jnp.concatenate([hit, pad_row], axis=1)
    codes[SLOTS + 4 :, :] = jnp.zeros((4, 128), I32)

    found = jnp.broadcast_to(jnp.sum(codes[...], axis=1, keepdims=True), (40, 128))
    held = found[:SLOTS]
    req_col = jnp.where(held > 0, jnp.minimum((held - 1) >> 7, REQS - 1), -1)
    rows, lanes = iota((SLOTS, 128), 0), iota((SLOTS, 128), 1)
    req_row = jnp.sum(jnp.where(rows == lanes, req_col, 0), axis=0, keepdims=True)
    req_row = jnp.where(lanes < SLOTS, jnp.broadcast_to(req_row, (SLOTS, 128)), -2)
    before = jnp.max(jnp.where((req_row == req_col) & (lanes < rows), lanes, -1), axis=1, keepdims=True)
    last = jnp.max(jnp.where(req_row == rows, lanes, -1), axis=1, keepdims=True)
    meta[:SLOTS] = jnp.where(
        lanes == 0, req_col, jnp.where(lanes == 1, held, jnp.where(lanes == 2, before, last))
    )
    meta[SLOTS:] = found[SLOTS:]
    meta_copy = pltpu.make_async_copy(meta, smeta, meta_sem)
    meta_copy.start()

    def widen(of, dz):
        i = (z + 4 - dz) % 4

        @pl.loop(0, 4)
        def _(group):
            for e in range(4):
                j = group * 4 + e
                gq[of, i, pl.ds(j * 32, 32), :] = gat[of, i, j].astype(F32)

    for dz in FAR_FIRST:
        plane_wait(dz).wait_recv()
        sib_copy(dz, core).start()
        widen(core, dz)
    meta_copy.wait()
    for dz in FAR_FIRST:
        sib_copy(dz, sib).wait_recv()
        widen(sib, dz)

    token = iota((128, 128), 0)
    head_of = iota((16, 128), 1) // 16
    pick = [jnp.where(head_of == g, 1.0, 0.0).astype(BF16) for g in range(8)]

    @pl.loop(0, KV_PARTS)
    def _(part):
        key_copy(part).wait()
        for e in range(UNROLL):
            n = part * UNROLL + e
            r = jnp.maximum(smeta[n, 0], 0)
            b = (jnp.maximum(smeta[n, 1], 1) - 1) % 128
            count = jnp.where(smeta[n, 1] > 0, lens[r] - b * 128, 0)
            parts = [gq[of, r // 8, pl.ds(r % 8, 64, stride=8), :].reshape(8, 8, 128) for of in range(2)]
            turned = jnp.concatenate(parts, axis=1).reshape(128, 128).T.astype(BF16).reshape(8, 16, 128)
            score = jnp.zeros((128, 128), F32)
            for kt in range(4):
                pair = [(turned * pick[g]).reshape(128, 128) for g in (2 * kt, 2 * kt + 1)]
                score = score + jnp.dot(
                    kvb[n, :, kt * 256 : kt * 256 + 256], jnp.concatenate(pair, axis=0),
                    preferred_element_type=F32,
                )
            valid = token < count
            score = jnp.where(valid, score * SCALE, LOW)
            peak = jnp.max(score, axis=0, keepdims=True)
            w = jnp.where(valid, jnp.exp(score - peak), 0.0).astype(BF16)
            mb[pl.ds(n, 1), :] = peak
            db[pl.ds(n, 1), :] = jnp.sum(w.astype(F32), axis=0, keepdims=True)
            wb[n] = w.T

    fresh_wait().wait_recv()
    sib_fresh(core).start()

    rows = iota((REQS, 128), 0)
    top = jnp.full((REQS, 128), LOW, F32)

    @pl.loop(0, SLOTS // 4, init_carry=top)
    def top(group, most):
        for e in range(4):
            n = group * 4 + e
            most = jnp.where(rows == smeta[n, 0], jnp.maximum(most, mb[pl.ds(n, 1), :]), most)
        return most

    mc[...] = top
    fb[...] = jnp.zeros((128, 128), F32)

    @pl.loop(0, SLOTS // 4, init_carry=jnp.zeros((REQS, 128), F32))
    def den(group, sums):
        for e in range(4):
            n = group * 4 + e
            r = smeta[n, 0]
            factor = jnp.exp(mb[pl.ds(n, 1), :] - mc[pl.ds(jnp.maximum(r, 0), 1), :])
            fb[pl.ds(n, 1), :] = factor
            sums = sums + jnp.where(rows == r, factor * db[pl.ds(n, 1), :], 0.0)
        return sums

    fb[...] = fb[...].T
    mx[0, 0] = top
    mx[0, 1] = den
    pair_copy = pltpu.make_async_remote_copy(
        src_ref=mx.at[0], dst_ref=mx.at[1], send_sem=m_sems.at[0], recv_sem=m_sems.at[1],
        device_id=sibling, device_id_type=MESH,
    )
    pair_copy.start()

    @pl.loop(0, KV_PARTS)
    def _(part):
        value_copy(part).wait()

    def turn(k):
        return (y + k) % 4

    def product(k, n):
        kt = turn(k)
        both = jnp.dot(
            wb[n, pl.ds(pl.multiple_of(kt * 32, 32), 32), :],
            kvb[n, :, pl.ds(pl.multiple_of(1024 + kt * 256, 256), 256)],
            preferred_element_type=F32,
        )
        return jnp.concatenate([both[:16, :128], both[16:, 128:]], axis=0)

    def chunk_copy(k):
        kt = turn(k)
        return pltpu.make_async_remote_copy(
            src_ref=s32.at[sib, :, pl.ds(pl.multiple_of(kt * 128, 128), 128), :], dst_ref=r32.at[k],
            send_sem=s_chunk.at[k], recv_sem=r_chunk.at[k], device_id=sibling, device_id_type=MESH,
        )

    def block_copy(to_chip, to):
        return pltpu.make_async_remote_copy(
            src_ref=sb.at[to_chip], dst_ref=rb.at[chip], send_sem=all_sems.at[0], recv_sem=all_sems.at[1],
            device_id=to, device_id_type=MESH,
        )

    def side_copy(to_chip, to):
        return pltpu.make_async_remote_copy(
            src_ref=ss.at[to_chip], dst_ref=rs.at[chip], send_sem=all_sems.at[2], recv_sem=all_sems.at[3],
            device_id=to, device_id_type=MESH,
        )

    def merge(k):
        kt = turn(k)
        chunk_copy(k).wait_recv()
        shift = (128 - (kt * 32 + core * 8)) % 128

        @pl.loop(0, 4)
        def _(i):
            mine_f, other_f = [pltpu.roll(lift[f, pl.ds(i * 8, 8), :], shift, 1) for f in range(2)]
            for j in range(4):
                total = []
                for t in range(4):
                    lane = (j // 2) * 16 + (j % 2) * 4 + t
                    at = pl.ds(pl.multiple_of(kt * 128 + j * 32 + t * 8, 8), 8)
                    there = r32[k, i, j * 32 + t * 8 : j * 32 + t * 8 + 8, :]
                    total.append(
                        s32[core, i, at, :] * mine_f[:, lane : lane + 1] + there * other_f[:, lane : lane + 1]
                    )
                sb[i * 16 + kt * 4 + j] = jnp.concatenate(total, axis=0).astype(BF16)

    def meet():
        pair_copy.wait_recv()
        chip_top = jnp.maximum(top, mx[1, 0])
        mine_f, other_f = jnp.exp(top - chip_top), jnp.exp(mx[1, 0] - chip_top)
        chip_den = den * mine_f + mx[1, 1] * other_f
        pad = jnp.zeros((96, 128), F32)
        mt[...] = jnp.concatenate([chip_top, pad], axis=0).T
        dt[...] = jnp.concatenate([chip_den, pad], axis=0).T
        lane8 = iota((8, 128), 1)
        for i in range(4):
            for xl in range(2):
                packed = jnp.zeros((8, 128), F32)
                for t in range(4):
                    for w, src in ((0, mt), (1, dt)):
                        got = src[pl.ds(core * 8 + xl * 4 + t, 8, stride=16), :]
                        to = w * 32 + t * 8
                        got = pltpu.roll(got, (to - 8 * i) % 128, 1)
                        packed = jnp.where((lane8 >= to) & (lane8 < to + 8), got, packed)
                for g in range(8):
                    ss[i * 16 + g * 2 + xl] = packed[g : g + 1, :]
        rs[chip] = ss[chip]
        lift[0] = mine_f
        lift[1] = other_f

    def send(k):
        kt = turn(k)

        @pl.loop(0, 16)
        def _(d):
            pz, px = (z + d // 4) % 4, (x + d % 4) % 4
            to_chip, to = pz * 16 + kt * 4 + px, place(pz, kt, px)

            @pl.when(k * 16 + d > 0)
            def _():
                block_copy(to_chip, to).start()
                side_copy(to_chip, to).start()

    @pl.loop(0, 5)
    def _(k):
        kt = turn(k)

        @pl.when(k < 4)
        def _():
            @pl.loop(0, SLOTS // GROUP)
            def _(group):
                scales = fb[pl.ds(pl.multiple_of(kt * 32, 32), 32), :]
                scales = pltpu.roll(scales, (128 - group * GROUP) % 128, 1)
                for e in range(GROUP):
                    n = group * GROUP + e
                    prev = smeta[n, 2]
                    earlier = jnp.where(prev >= 0, cb[jnp.maximum(prev, 0)], 0.0)
                    cb[n] = product(k, n) * scales[:, e : e + 1] + earlier

            @pl.loop(0, 4)
            def _(i):
                for rl in range(8):
                    end = smeta[i * 8 + rl, 3]
                    sums = jnp.where(end >= 0, cb[jnp.maximum(end, 0)], 0.0)
                    for xh in range(2):
                        for of in range(2):
                            start = kt * 128 + xh * 64 + rl
                            s32[of, i, pl.ds(start, 8, stride=8), :] = sums[xh * 16 + of * 8 : xh * 16 + of * 8 + 8]

            chunk_copy(k).start()

        @pl.when(k == 1)
        def _():
            meet()

        @pl.when(k > 0)
        def _():
            merge(k - 1)
            send(k - 1)

    rb[chip] = sb[chip]

    sib_fresh(sib).wait_recv()
    @pl.loop(0, 8)
    def _(k):
        of, i = k // 4, k % 4
        for j in range(16):
            gn[of, i, j * 8 : j * 8 + 8, :] = gnb[of, i * 16 + j].astype(F32)[:8]

    @pl.loop(0, 4)
    def _(e):
        found_row = smeta[SLOTS + e, 0]
        which = jnp.maximum(found_row - 1, 0)
        late, r = which // 32, which % 32
        pair = [gn[of, r // 8, pl.ds(r % 8, 16, stride=8), :] for of in range(2)]
        tl[pl.ds(pl.multiple_of(e * 16, 16), 16), :] = jnp.where(found_row > 0, halves(pair[0], pair[1], late > 0), 0.0)
    for j in range(16):
        tail[:, j * 128 : j * 128 + 128] = tl[pl.ds(j, 4, stride=16), :].astype(BF16)

    head = y * 2 + x // 2
    new_rows = []
    for at in (head, head + 8):
        pair = [gn[of, z, pl.ds(pl.multiple_of(at * 8, 8), 8), :] for of in range(2)]
        new_rows.append([halves(pair[0], pair[1], late) for late in (False, True)])
    new_m, new_den, new_num = [], [], []
    for t in range(4):
        mine_q = q[t // 2].astype(F32)[:, (t % 2) * 128 : (t % 2) * 128 + 128]
        found_scores = [
            jnp.sum(mine_q * new_rows[0][j], axis=1, keepdims=True) * SCALE for j in range(t // 2 + 1)
        ]
        peak = found_scores[0]
        for more in found_scores[1:]:
            peak = jnp.maximum(peak, more)
        ws = [jnp.exp(v - peak).astype(BF16).astype(F32) for v in found_scores]
        new_m.append(peak)
        new_den.append(sum(ws[1:], ws[0]))
        num = ws[0] * new_rows[1][0]
        for j in range(1, len(ws)):
            num = num + ws[j] * new_rows[1][j]
        new_num.append(num)
    new_m = jnp.concatenate(new_m, axis=0)
    new_den = jnp.concatenate(new_den, axis=0)
    new_num = jnp.concatenate(new_num, axis=0)

    most = pl.ds(0, CHIPS - 1)
    all_blocks = pltpu.make_async_remote_copy(
        src_ref=sb.at[most], dst_ref=rb.at[most], send_sem=all_sems.at[0], recv_sem=all_sems.at[1],
        device_id=sibling, device_id_type=MESH,
    )
    all_sides = pltpu.make_async_remote_copy(
        src_ref=ss.at[most], dst_ref=rs.at[most], send_sem=all_sems.at[2], recv_sem=all_sems.at[3],
        device_id=sibling, device_id_type=MESH,
    )
    all_sides.wait_recv()
    side = rs[...].reshape(CHIPS, 128)
    side = jnp.concatenate([side, jnp.zeros((128 - CHIPS, 128), F32)], axis=0).T
    side_m, side_den = side[0:32, :CHIPS], side[32:64, :CHIPS]
    final_m = jnp.maximum(jnp.max(side_m, axis=1, keepdims=True), new_m)
    scales = jnp.exp(side_m - final_m)
    new_scale = jnp.exp(new_m - final_m)
    final_den = jnp.sum(scales * side_den, axis=1, keepdims=True) + new_den * new_scale
    total = new_num * new_scale
    all_blocks.wait_recv()
    scales = jnp.concatenate([scales, jnp.zeros((32, 128 - CHIPS), F32)], axis=1)

    @pl.loop(0, CHIPS // 8, init_carry=(total, scales))
    def total_and_scales(group, carry):
        total, scales = carry
        for e in range(8):
            total = total + scales[:, e : e + 1] * rb[group * 8 + e].astype(F32)
        return total, pltpu.roll(scales, 120, 1)

    total = total_and_scales[0]
    result = total / final_den
    for t in range(4):
        out[t // 2, :, (t % 2) * 128 : (t % 2) * 128 + 128] = result[t * 8 : t * 8 + 8].astype(BF16)

    all_blocks.wait_send()
    all_sides.wait_send()
    for dz in FAR_FIRST:
        plane_wait(dz).wait_send()
        sib_copy(dz, core).wait_send()
    fresh_wait().wait_send()
    sib_fresh(core).wait_send()
    pair_copy.wait_send()
    for k in range(4):
        chunk_copy(k).wait_send()


def hand_over(result, rows, out, tail, sems):
    copies = [
        pltpu.make_async_copy(result, out, sems.at[0]),
        pltpu.make_async_copy(rows, tail, sems.at[1]),
    ]
    for copy in copies:
        copy.start()
    for copy in copies:
        copy.wait()


def per_device(kv_pool, queries, new_kv, lengths, block_dev, block_slot, owner_dev, owner_row):
    vmem = pl.BlockSpec(memory_space=pltpu.VMEM)
    dma = pltpu.SemaphoreType.DMA
    result, tail = pl.pallas_call(
        kernel,
        out_shape=(
            jax.ShapeDtypeStruct((2, 8, 256), BF16),
            jax.ShapeDtypeStruct((4, 2048), BF16),
        ),
        in_specs=[pl.BlockSpec(memory_space=pl.ANY)] + [vmem] * 6 + [pl.BlockSpec(memory_space=pltpu.SMEM)],
        out_specs=(vmem, vmem),
        scratch_shapes=[
            pltpu.VMEM((SLOTS, 128, 2048), BF16),
            pltpu.VMEM((2, 4, 16, 32, 128), BF16),
            pltpu.VMEM((2, CHIPS, 16, 128), BF16),
            pltpu.VMEM((2, 4, 512, 128), F32),
            pltpu.VMEM((2, 4, 128, 128), F32),
            pltpu.VMEM((SLOTS, 128, 128), BF16),
            pltpu.VMEM((SLOTS, 32, 128), F32),
            pltpu.VMEM((SLOTS, 128), F32),
            pltpu.VMEM((SLOTS, 128), F32),
            pltpu.VMEM((128, 128), F32),
            pltpu.VMEM((2, 2, REQS, 128), F32),
            pltpu.VMEM((2, REQS, 128), F32),
            pltpu.VMEM((REQS, 128), F32),
            pltpu.VMEM((128, 128), F32),
            pltpu.VMEM((128, 128), F32),
            pltpu.VMEM((2, 4, 512, 128), F32),
            pltpu.VMEM((4, 4, 128, 128), F32),
            pltpu.VMEM((CHIPS, 32, 128), BF16),
            pltpu.VMEM((CHIPS, 32, 128), BF16),
            pltpu.VMEM((CHIPS, 1, 128), F32),
            pltpu.VMEM((CHIPS, 1, 128), F32),
            pltpu.VMEM((64, 128), F32),
            pltpu.VMEM((40, 128), I32),
            pltpu.SMEM((40, 128), I32),
            pltpu.VMEM((40, 128), I32),
            dma((KV_PARTS,)),
            dma((KV_PARTS,)),
            dma((5,)),
            dma((5,)),
            dma((5,)),
            dma((5,)),
            dma((2,)),
            dma((4,)),
            dma((4,)),
            dma((4,)),
            dma,
        ],
        compiler_params=pltpu.CompilerParams(
            collective_id=0, has_side_effects=True, vmem_limit_bytes=56 * 1024 * 1024
        ),
    )(kv_pool, queries, new_kv, block_dev, block_slot, owner_dev, owner_row, lengths)
    anywhere = pl.BlockSpec(memory_space=pltpu.HBM)
    return pl.pallas_call(
        hand_over,
        out_shape=(
            jax.ShapeDtypeStruct((2, 8, 256), BF16),
            jax.ShapeDtypeStruct((4, 2048), BF16),
        ),
        in_specs=[anywhere] * 2,
        out_specs=(anywhere, anywhere),
        scratch_shapes=[dma((2,))],
    )(result, tail)


def solution(mesh):
    placed = (
        P(("inst", "seq"), None, None),
        P(None, "inst", "seq"),
        P(None, "inst", "seq"),
        P(),
        P(),
        P(),
        P(),
        P(),
    )
    return jax.shard_map(
        per_device,
        mesh=mesh,
        in_specs=placed,
        out_specs=(P(None, "inst", "seq"), P(("inst", "seq"), None)),
        check_vma=False,
    )
```

```python
import math

import jax
import jax.numpy as jnp
from jax import lax
from jax.experimental import pallas as pl
from jax.experimental.pallas import tpu as pltpu
from jax.sharding import PartitionSpec as P

MESH = pl.DeviceIdType.MESH
F32 = jnp.float32
BF16 = jnp.bfloat16
I32 = jnp.int32

N = 4
CHIPS = 64
SLOTS = 32
REQS = 32
LOW = -1e30
SCALE = 1.0 / math.sqrt(128)
UNROLL = 4
GROUP = 16
KV_PARTS = SLOTS // UNROLL
FAR_FIRST = (3, 2, 1, 0)


def iota(shape, dim):
    return lax.broadcasted_iota(I32, shape, dim)


def halves(first, second, late):
    lane = iota(first.shape, 1)
    if late is True:
        return jnp.where(lane < 64, pltpu.roll(first, 64, 1), second)
    if late is False:
        return jnp.where(lane < 64, first, pltpu.roll(second, 64, 1))
    low = jnp.where(late, pltpu.roll(first, 64, 1), first)
    high = jnp.where(late, second, pltpu.roll(second, 64, 1))
    return jnp.where(lane < 64, low, high)


def kernel(
    kv, q_in, nk_in, dev_in, slot_in, own_dev_in, own_row_in, lens_in, out_at, tail_at,
    q, nk, dev, slot, own_dev, own_row, lens, out, tail,
    kvb, gat, gnb, gq, gn, wb, cb, mb, db, fb, mx, lift, mc, mt, dt, s32, r32, sb, rb, ss, rs, tl, meta, smeta, codes,
    k_sem, v_sem, sg, rg, s_sib, r_sib, m_sems, s_chunk, r_chunk, all_sems, meta_sem, io_sem,
):
    z = lax.axis_index("inst")
    c = lax.axis_index("seq")
    y, x, core = c // 8, (c // 2) % 4, c % 2
    me = z * 32 + c
    chip = z * 16 + y * 4 + x
    sib = 1 - core
    sibling = (z, y * 8 + x * 2 + sib)

    def place(pz, py, px):
        return (pz, py * 8 + px * 2 + core)

    loads = [
        pltpu.make_async_copy(src, dst, io_sem.at[k])
        for k, (src, dst) in enumerate([
            (q_in, q), (nk_in, nk), (dev_in, dev), (slot_in, slot),
            (own_dev_in, own_dev), (own_row_in, own_row), (lens_in, lens),
        ])
    ]
    for load in loads:
        load.start()

    def offset(d):
        return (z + d // 16) % 4, (y + (d // 4) % 4) % 4, (x + d % 4) % 4

    barrier = pltpu.get_barrier_semaphore()

    @pl.loop(1, CHIPS)
    def _(d):
        pl.semaphore_signal(barrier, inc=1, device_id=place(*offset(d)), device_id_type=MESH)

    pl.semaphore_signal(barrier, inc=1, device_id=sibling, device_id_type=MESH)

    def key_copy(part):
        span = pl.ds(part * UNROLL, UNROLL)
        cols = pl.ds(0, 1024)
        return pltpu.make_async_copy(kv.at[span, :, cols], kvb.at[span, :, cols], k_sem.at[part])

    def value_copy(part):
        span = pl.ds(part * UNROLL, UNROLL)
        cols = pl.ds(1024, 1024)
        return pltpu.make_async_copy(kv.at[span, :, cols], kvb.at[span, :, cols], v_sem.at[part])

    @pl.loop(0, KV_PARTS)
    def _(part):
        key_copy(part).start()

    spot = y * 4 + x
    for load in loads[:2]:
        load.wait()
    own = [q[s].astype(F32) for s in range(2)]
    gat[core, z, spot] = jnp.concatenate(
        [own[0][:, :128], own[0][:, 128:], own[1][:, :128], own[1][:, 128:]], axis=0
    ).astype(BF16)
    fresh = jnp.concatenate([nk[0].astype(F32), nk[1].astype(F32)], axis=1)
    gnb[core, chip] = jnp.concatenate([fresh, jnp.zeros((8, 128), F32)], axis=0).astype(BF16)

    pl.semaphore_wait(barrier, CHIPS)

    def query_copy(d):
        block = gat.at[core, z, spot]
        return pltpu.make_async_remote_copy(
            src_ref=block, dst_ref=block, send_sem=sg.at[d // 16], recv_sem=rg.at[d // 16],
            device_id=place(*offset(d)), device_id_type=MESH,
        )

    def fresh_copy(d):
        block = gnb.at[core, chip]
        return pltpu.make_async_remote_copy(
            src_ref=block, dst_ref=block, send_sem=sg.at[4], recv_sem=rg.at[4],
            device_id=place(*offset(d)), device_id_type=MESH,
        )

    def plane_wait(dz):
        at = (z + 4 - dz) % 4
        block = gat.at[core, at] if dz else gat.at[core, at, pl.ds(0, 15)]
        return pltpu.make_async_remote_copy(
            src_ref=block, dst_ref=block, send_sem=sg.at[dz], recv_sem=rg.at[dz],
            device_id=sibling, device_id_type=MESH,
        )

    def sib_copy(dz, of):
        block = gat.at[of, (z + 4 - dz) % 4]
        return pltpu.make_async_remote_copy(
            src_ref=block, dst_ref=block, send_sem=s_sib.at[dz], recv_sem=r_sib.at[dz],
            device_id=sibling, device_id_type=MESH,
        )

    def sib_fresh(of):
        block = gnb.at[of]
        return pltpu.make_async_remote_copy(
            src_ref=block, dst_ref=block, send_sem=s_sib.at[4], recv_sem=r_sib.at[4],
            device_id=sibling, device_id_type=MESH,
        )

    def fresh_wait():
        block = gnb.at[core, pl.ds(0, CHIPS - 1)]
        return pltpu.make_async_remote_copy(
            src_ref=block, dst_ref=block, send_sem=sg.at[4], recv_sem=rg.at[4],
            device_id=sibling, device_id_type=MESH,
        )

    @pl.loop(0, CHIPS - 1)
    def _(d):
        query_copy(CHIPS - 1 - d).start()

    @pl.loop(0, KV_PARTS)
    def _(part):
        value_copy(part).start()

    @pl.loop(1, CHIPS)
    def _(d):
        fresh_copy(d).start()

    for load in loads[2:]:
        load.wait()
    mine = jnp.where(dev[...] == me, slot[...], -1)
    code = iota((REQS, 128), 0) * 128 + iota((REQS, 128), 1) + 1

    @pl.loop(0, SLOTS // 4)
    def _(group):
        for e in range(4):
            n = group * 4 + e
            codes[pl.ds(n, 1), :] = jnp.sum(jnp.where(mine == n, code, 0), axis=0, keepdims=True)

    owned = jnp.where(own_dev[...] == me, own_row[...], -1)
    row_code = iota((2, REQS), 0) * REQS + iota((2, REQS), 1) + 1
    pad_row = jnp.zeros((1, 96), I32)
    for e in range(4):
        hit = jnp.sum(jnp.where(owned == e, row_code, 0), axis=0, keepdims=True)
        codes[SLOTS + e : SLOTS + e + 1, :] = jnp.concatenate([hit, pad_row], axis=1)
    codes[SLOTS + 4 :, :] = jnp.zeros((4, 128), I32)

    found = jnp.broadcast_to(jnp.sum(codes[...], axis=1, keepdims=True), (40, 128))
    held = found[:SLOTS]
    req_col = jnp.where(held > 0, jnp.minimum((held - 1) >> 7, REQS - 1), -1)
    rows, lanes = iota((SLOTS, 128), 0), iota((SLOTS, 128), 1)
    req_row = jnp.sum(jnp.where(rows == lanes, req_col, 0), axis=0, keepdims=True)
    req_row = jnp.where(lanes < SLOTS, jnp.broadcast_to(req_row, (SLOTS, 128)), -2)
    before = jnp.max(jnp.where((req_row == req_col) & (lanes < rows), lanes, -1), axis=1, keepdims=True)
    last = jnp.max(jnp.where(req_row == rows, lanes, -1), axis=1, keepdims=True)
    meta[:SLOTS] = jnp.where(
        lanes == 0, req_col, jnp.where(lanes == 1, held, jnp.where(lanes == 2, before, last))
    )
    meta[SLOTS:] = found[SLOTS:]
    meta_copy = pltpu.make_async_copy(meta, smeta, meta_sem)
    meta_copy.start()

    def widen(of, dz):
        i = (z + 4 - dz) % 4

        @pl.loop(0, 4)
        def _(group):
            for e in range(4):
                j = group * 4 + e
                gq[of, i, pl.ds(j * 32, 32), :] = gat[of, i, j].astype(F32)

    for dz in FAR_FIRST:
        plane_wait(dz).wait_recv()
        sib_copy(dz, core).start()
        widen(core, dz)
    meta_copy.wait()
    for dz in FAR_FIRST:
        sib_copy(dz, sib).wait_recv()
        widen(sib, dz)

    lane128 = iota((128, 128), 1)
    blank = jnp.zeros((16, 128), BF16)
    mt[...] = jnp.zeros((128, 128), F32)
    dt[...] = jnp.zeros((128, 128), F32)

    @pl.loop(0, KV_PARTS)
    def _(part):
        key_copy(part).wait()
        peaks = mt[...]
        sums = dt[...]
        for e in range(UNROLL):
            n = part * UNROLL + e
            r = jnp.maximum(smeta[n, 0], 0)
            b = (jnp.maximum(smeta[n, 1], 1) - 1) % 128
            count = jnp.where(smeta[n, 1] > 0, lens[r] - b * 128, 0)
            parts = [gq[of, r // 8, pl.ds(r % 8, 64, stride=8), :].reshape(8, 8, 128) for of in range(2)]
            heads = jnp.concatenate(parts, axis=1).astype(BF16)
            score = []
            for kt in range(4):
                first = jnp.concatenate([heads[2 * kt], blank], axis=1)
                second = jnp.concatenate([blank, heads[2 * kt + 1]], axis=1)
                score.append(lax.dot_general(
                    jnp.concatenate([first, second], axis=0), kvb[n, :, kt * 256 : kt * 256 + 256],
                    (((1,), (1,)), ((), ())), preferred_element_type=F32,
                ))
            valid = lane128 < count
            score = jnp.where(valid, jnp.concatenate(score, axis=0) * SCALE, LOW)
            peak = jnp.max(score, axis=1, keepdims=True)
            w = jnp.where(valid, jnp.exp(score - peak), 0.0).astype(BF16)
            wb[n] = w
            peaks = jnp.where(lane128 == n, peak, peaks)
            sums = jnp.where(lane128 == n, jnp.sum(w.astype(F32), axis=1, keepdims=True), sums)
        mt[...] = peaks
        dt[...] = sums

    mb[...] = mt[...].T[:SLOTS]
    db[...] = dt[...].T[:SLOTS]

    fresh_wait().wait_recv()
    sib_fresh(core).start()

    rows = iota((REQS, 128), 0)
    top = jnp.full((REQS, 128), LOW, F32)

    @pl.loop(0, SLOTS // 4, init_carry=top)
    def top(group, most):
        for e in range(4):
            n = group * 4 + e
            most = jnp.where(rows == smeta[n, 0], jnp.maximum(most, mb[pl.ds(n, 1), :]), most)
        return most

    mc[...] = top
    fb[...] = jnp.zeros((128, 128), F32)

    @pl.loop(0, SLOTS // 4, init_carry=jnp.zeros((REQS, 128), F32))
    def den(group, sums):
        for e in range(4):
            n = group * 4 + e
            r = smeta[n, 0]
            factor = jnp.exp(mb[pl.ds(n, 1), :] - mc[pl.ds(jnp.maximum(r, 0), 1), :])
            fb[pl.ds(n, 1), :] = factor
            sums = sums + jnp.where(rows == r, factor * db[pl.ds(n, 1), :], 0.0)
        return sums

    fb[...] = fb[...].T
    mx[0, 0] = top
    mx[0, 1] = den
    pair_copy = pltpu.make_async_remote_copy(
        src_ref=mx.at[0], dst_ref=mx.at[1], send_sem=m_sems.at[0], recv_sem=m_sems.at[1],
        device_id=sibling, device_id_type=MESH,
    )
    pair_copy.start()

    @pl.loop(0, KV_PARTS)
    def _(part):
        value_copy(part).wait()

    def turn(k):
        return (y + k) % 4

    def product(k, n):
        kt = turn(k)
        both = jnp.dot(
            wb[n, pl.ds(pl.multiple_of(kt * 32, 32), 32), :],
            kvb[n, :, pl.ds(pl.multiple_of(1024 + kt * 256, 256), 256)],
            preferred_element_type=F32,
        )
        return jnp.concatenate([both[:16, :128], both[16:, 128:]], axis=0)

    def chunk_copy(k):
        kt = turn(k)
        return pltpu.make_async_remote_copy(
            src_ref=s32.at[sib, :, pl.ds(pl.multiple_of(kt * 128, 128), 128), :], dst_ref=r32.at[k],
            send_sem=s_chunk.at[k], recv_sem=r_chunk.at[k], device_id=sibling, device_id_type=MESH,
        )

    def block_copy(to_chip, to):
        return pltpu.make_async_remote_copy(
            src_ref=sb.at[to_chip], dst_ref=rb.at[chip], send_sem=all_sems.at[0], recv_sem=all_sems.at[1],
            device_id=to, device_id_type=MESH,
        )

    def side_copy(to_chip, to):
        return pltpu.make_async_remote_copy(
            src_ref=ss.at[to_chip], dst_ref=rs.at[chip], send_sem=all_sems.at[2], recv_sem=all_sems.at[3],
            device_id=to, device_id_type=MESH,
        )

    def merge(k):
        kt = turn(k)
        chunk_copy(k).wait_recv()
        shift = (128 - (kt * 32 + core * 8)) % 128

        @pl.loop(0, 4)
        def _(i):
            mine_f, other_f = [pltpu.roll(lift[f, pl.ds(i * 8, 8), :], shift, 1) for f in range(2)]
            for j in range(4):
                total = []
                for t in range(4):
                    lane = (j // 2) * 16 + (j % 2) * 4 + t
                    at = pl.ds(pl.multiple_of(kt * 128 + j * 32 + t * 8, 8), 8)
                    there = r32[k, i, j * 32 + t * 8 : j * 32 + t * 8 + 8, :]
                    total.append(
                        s32[core, i, at, :] * mine_f[:, lane : lane + 1] + there * other_f[:, lane : lane + 1]
                    )
                sb[i * 16 + kt * 4 + j] = jnp.concatenate(total, axis=0).astype(BF16)

    def meet():
        pair_copy.wait_recv()
        chip_top = jnp.maximum(top, mx[1, 0])
        mine_f, other_f = jnp.exp(top - chip_top), jnp.exp(mx[1, 0] - chip_top)
        chip_den = den * mine_f + mx[1, 1] * other_f
        pad = jnp.zeros((96, 128), F32)
        mt[...] = jnp.concatenate([chip_top, pad], axis=0).T
        dt[...] = jnp.concatenate([chip_den, pad], axis=0).T
        lane8 = iota((8, 128), 1)
        for i in range(4):
            for xl in range(2):
                packed = jnp.zeros((8, 128), F32)
                for t in range(4):
                    for w, src in ((0, mt), (1, dt)):
                        got = src[pl.ds(core * 8 + xl * 4 + t, 8, stride=16), :]
                        to = w * 32 + t * 8
                        got = pltpu.roll(got, (to - 8 * i) % 128, 1)
                        packed = jnp.where((lane8 >= to) & (lane8 < to + 8), got, packed)
                for g in range(8):
                    ss[i * 16 + g * 2 + xl] = packed[g : g + 1, :]
        rs[chip] = ss[chip]
        lift[0] = mine_f
        lift[1] = other_f

    def send(k):
        kt = turn(k)

        @pl.loop(0, 16)
        def _(d):
            pz, px = (z + d // 4) % 4, (x + d % 4) % 4
            to_chip, to = pz * 16 + kt * 4 + px, place(pz, kt, px)

            @pl.when(k * 16 + d > 0)
            def _():
                block_copy(to_chip, to).start()
                side_copy(to_chip, to).start()

    @pl.loop(0, 5)
    def _(k):
        kt = turn(k)

        @pl.when(k < 4)
        def _():
            @pl.loop(0, SLOTS // GROUP)
            def _(group):
                scales = fb[pl.ds(pl.multiple_of(kt * 32, 32), 32), :]
                scales = pltpu.roll(scales, (128 - group * GROUP) % 128, 1)
                for e in range(GROUP):
                    n = group * GROUP + e
                    prev = smeta[n, 2]
                    earlier = jnp.where(prev >= 0, cb[jnp.maximum(prev, 0)], 0.0)
                    cb[n] = product(k, n) * scales[:, e : e + 1] + earlier

            @pl.loop(0, 4)
            def _(i):
                for rl in range(8):
                    end = smeta[i * 8 + rl, 3]
                    sums = jnp.where(end >= 0, cb[jnp.maximum(end, 0)], 0.0)
                    for xh in range(2):
                        for of in range(2):
                            start = kt * 128 + xh * 64 + rl
                            s32[of, i, pl.ds(start, 8, stride=8), :] = sums[xh * 16 + of * 8 : xh * 16 + of * 8 + 8]

            chunk_copy(k).start()

        @pl.when(k == 1)
        def _():
            meet()

        @pl.when(k > 0)
        def _():
            merge(k - 1)
            send(k - 1)

    rb[chip] = sb[chip]

    sib_fresh(sib).wait_recv()
    @pl.loop(0, 8)
    def _(k):
        of, i = k // 4, k % 4
        for j in range(16):
            gn[of, i, j * 8 : j * 8 + 8, :] = gnb[of, i * 16 + j].astype(F32)[:8]

    @pl.loop(0, 4)
    def _(e):
        found_row = smeta[SLOTS + e, 0]
        which = jnp.maximum(found_row - 1, 0)
        late, r = which // 32, which % 32
        pair = [gn[of, r // 8, pl.ds(r % 8, 16, stride=8), :] for of in range(2)]
        tl[pl.ds(pl.multiple_of(e * 16, 16), 16), :] = jnp.where(found_row > 0, halves(pair[0], pair[1], late > 0), 0.0)
    for j in range(16):
        tail[:, j * 128 : j * 128 + 128] = tl[pl.ds(j, 4, stride=16), :].astype(BF16)

    head = y * 2 + x // 2
    new_rows = []
    for at in (head, head + 8):
        pair = [gn[of, z, pl.ds(pl.multiple_of(at * 8, 8), 8), :] for of in range(2)]
        new_rows.append([halves(pair[0], pair[1], late) for late in (False, True)])
    new_m, new_den, new_num = [], [], []
    for t in range(4):
        mine_q = q[t // 2].astype(F32)[:, (t % 2) * 128 : (t % 2) * 128 + 128]
        found_scores = [
            jnp.sum(mine_q * new_rows[0][j], axis=1, keepdims=True) * SCALE for j in range(t // 2 + 1)
        ]
        peak = found_scores[0]
        for more in found_scores[1:]:
            peak = jnp.maximum(peak, more)
        ws = [jnp.exp(v - peak).astype(BF16).astype(F32) for v in found_scores]
        new_m.append(peak)
        new_den.append(sum(ws[1:], ws[0]))
        num = ws[0] * new_rows[1][0]
        for j in range(1, len(ws)):
            num = num + ws[j] * new_rows[1][j]
        new_num.append(num)
    new_m = jnp.concatenate(new_m, axis=0)
    new_den = jnp.concatenate(new_den, axis=0)
    new_num = jnp.concatenate(new_num, axis=0)

    most = pl.ds(0, CHIPS - 1)
    all_blocks = pltpu.make_async_remote_copy(
        src_ref=sb.at[most], dst_ref=rb.at[most], send_sem=all_sems.at[0], recv_sem=all_sems.at[1],
        device_id=sibling, device_id_type=MESH,
    )
    all_sides = pltpu.make_async_remote_copy(
        src_ref=ss.at[most], dst_ref=rs.at[most], send_sem=all_sems.at[2], recv_sem=all_sems.at[3],
        device_id=sibling, device_id_type=MESH,
    )
    all_sides.wait_recv()
    side = rs[...].reshape(CHIPS, 128)
    side = jnp.concatenate([side, jnp.zeros((128 - CHIPS, 128), F32)], axis=0).T
    side_m, side_den = side[0:32, :CHIPS], side[32:64, :CHIPS]
    final_m = jnp.maximum(jnp.max(side_m, axis=1, keepdims=True), new_m)
    scales = jnp.exp(side_m - final_m)
    new_scale = jnp.exp(new_m - final_m)
    final_den = jnp.sum(scales * side_den, axis=1, keepdims=True) + new_den * new_scale
    total = new_num * new_scale
    all_blocks.wait_recv()
    scales = jnp.concatenate([scales, jnp.zeros((32, 128 - CHIPS), F32)], axis=1)

    @pl.loop(0, CHIPS // 8, init_carry=(total, scales))
    def total_and_scales(group, carry):
        total, scales = carry
        for e in range(8):
            total = total + scales[:, e : e + 1] * rb[group * 8 + e].astype(F32)
        return total, pltpu.roll(scales, 120, 1)

    total = total_and_scales[0]
    result = total / final_den
    for t in range(4):
        out[t // 2, :, (t % 2) * 128 : (t % 2) * 128 + 128] = result[t * 8 : t * 8 + 8].astype(BF16)

    stores = [
        pltpu.make_async_copy(src, dst, io_sem.at[k])
        for k, (src, dst) in enumerate([(out, out_at), (tail, tail_at)])
    ]
    for store in stores:
        store.start()

    all_blocks.wait_send()
    all_sides.wait_send()
    for dz in FAR_FIRST:
        plane_wait(dz).wait_send()
        sib_copy(dz, core).wait_send()
    fresh_wait().wait_send()
    sib_fresh(core).wait_send()
    pair_copy.wait_send()
    for k in range(4):
        chunk_copy(k).wait_send()
    for store in stores:
        store.wait()


def hand_over(result, rows, out, tail, sems):
    copies = [
        pltpu.make_async_copy(result, out, sems.at[0]),
        pltpu.make_async_copy(rows, tail, sems.at[1]),
    ]
    for copy in copies:
        copy.start()
    for copy in copies:
        copy.wait()


def per_device(kv_pool, queries, new_kv, lengths, block_dev, block_slot, owner_dev, owner_row):
    anywhere = pl.BlockSpec(memory_space=pltpu.HBM)
    dma = pltpu.SemaphoreType.DMA
    result, tail = pl.pallas_call(
        kernel,
        out_shape=(
            jax.ShapeDtypeStruct((2, 8, 256), BF16),
            jax.ShapeDtypeStruct((4, 2048), BF16),
        ),
        in_specs=[anywhere] * 8,
        out_specs=(anywhere, anywhere),
        scratch_shapes=[
            pltpu.VMEM((2, 8, 256), BF16),
            pltpu.VMEM((2, 8, 64), BF16),
            pltpu.VMEM((REQS, 128), I32),
            pltpu.VMEM((REQS, 128), I32),
            pltpu.VMEM((2, REQS), I32),
            pltpu.VMEM((2, REQS), I32),
            pltpu.SMEM((REQS,), I32),
            pltpu.VMEM((2, 8, 256), BF16),
            pltpu.VMEM((4, 2048), BF16),
            pltpu.VMEM((SLOTS, 128, 2048), BF16),
            pltpu.VMEM((2, 4, 16, 32, 128), BF16),
            pltpu.VMEM((2, CHIPS, 16, 128), BF16),
            pltpu.VMEM((2, 4, 512, 128), F32),
            pltpu.VMEM((2, 4, 128, 128), F32),
            pltpu.VMEM((SLOTS, 128, 128), BF16),
            pltpu.VMEM((SLOTS, 32, 128), F32),
            pltpu.VMEM((SLOTS, 128), F32),
            pltpu.VMEM((SLOTS, 128), F32),
            pltpu.VMEM((128, 128), F32),
            pltpu.VMEM((2, 2, REQS, 128), F32),
            pltpu.VMEM((2, REQS, 128), F32),
            pltpu.VMEM((REQS, 128), F32),
            pltpu.VMEM((128, 128), F32),
            pltpu.VMEM((128, 128), F32),
            pltpu.VMEM((2, 4, 512, 128), F32),
            pltpu.VMEM((4, 4, 128, 128), F32),
            pltpu.VMEM((CHIPS, 32, 128), BF16),
            pltpu.VMEM((CHIPS, 32, 128), BF16),
            pltpu.VMEM((CHIPS, 1, 128), F32),
            pltpu.VMEM((CHIPS, 1, 128), F32),
            pltpu.VMEM((64, 128), F32),
            pltpu.VMEM((40, 128), I32),
            pltpu.SMEM((40, 128), I32),
            pltpu.VMEM((40, 128), I32),
            dma((KV_PARTS,)),
            dma((KV_PARTS,)),
            dma((5,)),
            dma((5,)),
            dma((5,)),
            dma((5,)),
            dma((2,)),
            dma((4,)),
            dma((4,)),
            dma((4,)),
            dma,
            dma((7,)),
        ],
        compiler_params=pltpu.CompilerParams(
            collective_id=0, has_side_effects=True, vmem_limit_bytes=56 * 1024 * 1024
        ),
    )(kv_pool, queries, new_kv, block_dev, block_slot, owner_dev, owner_row, lengths)
    return pl.pallas_call(
        hand_over,
        out_shape=(
            jax.ShapeDtypeStruct((2, 8, 256), BF16),
            jax.ShapeDtypeStruct((4, 2048), BF16),
        ),
        in_specs=[anywhere] * 2,
        out_specs=(anywhere, anywhere),
        scratch_shapes=[dma((2,))],
    )(result, tail)


def solution(mesh):
    placed = (
        P(("inst", "seq"), None, None),
        P(None, "inst", "seq"),
        P(None, "inst", "seq"),
        P(),
        P(),
        P(),
        P(),
        P(),
    )
    return jax.shard_map(
        per_device,
        mesh=mesh,
        in_specs=placed,
        out_specs=(P(None, "inst", "seq"), P(("inst", "seq"), None)),
        check_vma=False,
    )
```

```python
import math

import jax
import jax.numpy as jnp
from jax import lax
from jax.experimental import pallas as pl
from jax.experimental.pallas import tpu as pltpu
from jax.sharding import PartitionSpec as P

MESH = pl.DeviceIdType.MESH
F32 = jnp.float32
BF16 = jnp.bfloat16
I32 = jnp.int32

N = 4
CHIPS = 64
SLOTS = 32
REQS = 32
LOW = -1e30
SCALE = 1.0 / math.sqrt(128)
UNROLL = 4
GROUP = 16
KV_PARTS = SLOTS // UNROLL


def iota(shape, dim):
    return lax.broadcasted_iota(I32, shape, dim)


def halves(first, second, late):
    lane = iota(first.shape, 1)
    if late is True:
        return jnp.where(lane < 64, pltpu.roll(first, 64, 1), second)
    if late is False:
        return jnp.where(lane < 64, first, pltpu.roll(second, 64, 1))
    low = jnp.where(late, pltpu.roll(first, 64, 1), first)
    high = jnp.where(late, second, pltpu.roll(second, 64, 1))
    return jnp.where(lane < 64, low, high)


def kernel(
    kv, q_in, nk_in, dev_in, slot_in, own_dev_in, own_row_in, lens_in, out_at, tail_at,
    q, nk, dev, slot, own_dev, own_row, lens, out, tail,
    kvb, gat, nx, tile, gnt, gq, gn, wb, pk, dn, cb, mx, mxr, mt, uw, s32, r32, sb, rb, ss, rs, tl, meta, smeta, codes,
    k_sem, v_sem, sg, rg, s_sib, r_sib, n_sems, s_m, r_m, s_chunk, r_chunk, all_sems, meta_sem, io_sem,
):
    z = lax.axis_index("inst")
    c = lax.axis_index("seq")
    y, x, core = c // 8, (c // 2) % 4, c % 2
    me = z * 32 + c
    chip = z * 16 + y * 4 + x
    sib = 1 - core
    sibling = (z, y * 8 + x * 2 + sib)

    def place(pz, py, px):
        return (pz, py * 8 + px * 2 + core)

    loads = [
        pltpu.make_async_copy(src, dst, io_sem.at[k])
        for k, (src, dst) in enumerate([
            (q_in, q), (nk_in, nk), (dev_in, dev), (slot_in, slot),
            (own_dev_in, own_dev), (own_row_in, own_row), (lens_in, lens),
        ])
    ]
    for load in loads:
        load.start()

    def offset(d):
        return (z + d // 16) % 4, (y + (d // 4) % 4) % 4, (x + d % 4) % 4

    barrier = pltpu.get_barrier_semaphore()

    @pl.loop(1, CHIPS)
    def _(d):
        pl.semaphore_signal(barrier, inc=1, device_id=place(*offset(d)), device_id_type=MESH)

    pl.semaphore_signal(barrier, inc=1, device_id=sibling, device_id_type=MESH)

    def key_copy(part):
        span = pl.ds(part * UNROLL, UNROLL)
        cols = pl.ds(0, 1024)
        return pltpu.make_async_copy(kv.at[span, :, cols], kvb.at[span, :, cols], k_sem.at[part])

    def value_copy(part):
        span = pl.ds(part * UNROLL, UNROLL)
        cols = pl.ds(1024, 1024)
        return pltpu.make_async_copy(kv.at[span, :, cols], kvb.at[span, :, cols], v_sem.at[part])

    @pl.loop(0, KV_PARTS)
    def _(part):
        key_copy(part).start()

    spot = z * 4 + x
    for load in loads[:2]:
        load.wait()
    own = [q[s].astype(F32) for s in range(2)]
    gat[core, y, spot] = jnp.concatenate(
        [own[0][:, :128], own[0][:, 128:], own[1][:, :128], own[1][:, 128:]], axis=0
    ).astype(BF16)
    nx[0] = jnp.concatenate([nk[0].astype(F32), nk[1].astype(F32)], axis=1)

    pl.semaphore_wait(barrier, CHIPS)

    def turn(k):
        return (y + k) % 4

    def beside(e, py):
        return (z + e // 4) % 4, py, (x + e % 4) % 4

    def query_copy(k, e):
        block = gat.at[core, y, spot]
        return pltpu.make_async_remote_copy(
            src_ref=block, dst_ref=block, send_sem=sg.at[k], recv_sem=rg.at[k],
            device_id=place(*beside(e, (y + 4 - k) % 4)), device_id_type=MESH,
        )

    def plane_wait(k, blocks=16):
        block = gat.at[core, turn(k), pl.ds(0, blocks)]
        return pltpu.make_async_remote_copy(
            src_ref=block, dst_ref=block, send_sem=sg.at[k], recv_sem=rg.at[k],
            device_id=sibling, device_id_type=MESH,
        )

    def sib_copy(k, of):
        block = gat.at[of, turn(k)]
        return pltpu.make_async_remote_copy(
            src_ref=block, dst_ref=block, send_sem=s_sib.at[k], recv_sem=r_sib.at[k],
            device_id=sibling, device_id_type=MESH,
        )

    @pl.loop(1, CHIPS)
    def _(d):
        query_copy(d // 16, d % 16).start()

    pair_rows = pltpu.make_async_remote_copy(
        src_ref=nx.at[0], dst_ref=nx.at[1], send_sem=n_sems.at[0], recv_sem=n_sems.at[1],
        device_id=sibling, device_id_type=MESH,
    )
    pair_rows.start()
    shelf = z * 8 + y * 2 + x // 2

    def fresh_copy(d):
        return pltpu.make_async_remote_copy(
            src_ref=tile, dst_ref=gnt.at[x % 2, shelf], send_sem=n_sems.at[2], recv_sem=n_sems.at[3],
            device_id=place(*offset(d)), device_id_type=MESH,
        )

    def fresh_wait(blocks):
        block = gnt.at[0, pl.ds(0, blocks)]
        return pltpu.make_async_remote_copy(
            src_ref=block, dst_ref=block, send_sem=n_sems.at[2], recv_sem=n_sems.at[3],
            device_id=sibling, device_id_type=MESH,
        )

    def sib_fresh(of):
        block = gnt.at[(x + of) % 2]
        return pltpu.make_async_remote_copy(
            src_ref=block, dst_ref=block, send_sem=n_sems.at[4], recv_sem=n_sems.at[5],
            device_id=sibling, device_id_type=MESH,
        )

    @pl.loop(0, KV_PARTS)
    def _(part):
        value_copy(part).start()

    for load in loads[2:]:
        load.wait()
    mine = jnp.where(dev[...] == me, slot[...], -1)
    code = iota((REQS, 128), 0) * 128 + iota((REQS, 128), 1) + 1

    @pl.loop(0, SLOTS // 4)
    def _(group):
        for e in range(4):
            n = group * 4 + e
            codes[pl.ds(n, 1), :] = jnp.sum(jnp.where(mine == n, code, 0), axis=0, keepdims=True)

    owned = jnp.where(own_dev[...] == me, own_row[...], -1)
    row_code = iota((2, REQS), 0) * REQS + iota((2, REQS), 1) + 1
    pad_row = jnp.zeros((1, 96), I32)
    for e in range(4):
        hit = jnp.sum(jnp.where(owned == e, row_code, 0), axis=0, keepdims=True)
        codes[SLOTS + e : SLOTS + e + 1, :] = jnp.concatenate([hit, pad_row], axis=1)
    codes[SLOTS + 4 :, :] = jnp.zeros((4, 128), I32)

    found = jnp.broadcast_to(jnp.sum(codes[...], axis=1, keepdims=True), (40, 128))
    held = found[:SLOTS]
    req_col = jnp.where(held > 0, jnp.minimum((held - 1) >> 7, REQS - 1), -1)
    rows, lanes = iota((SLOTS, 128), 0), iota((SLOTS, 128), 1)
    req_row = jnp.sum(jnp.where(rows == lanes, req_col, 0), axis=0, keepdims=True)
    req_row = jnp.where(lanes < SLOTS, jnp.broadcast_to(req_row, (SLOTS, 128)), -2)
    before = jnp.max(jnp.where((req_row == req_col) & (lanes < rows), lanes, -1), axis=1, keepdims=True)
    last = jnp.max(jnp.where(req_row == rows, lanes, -1), axis=1, keepdims=True)
    meta[:SLOTS] = jnp.where(
        lanes == 0, req_col, jnp.where(lanes == 1, held, jnp.where(lanes == 2, before, last))
    )
    meta[SLOTS:] = found[SLOTS:]
    meta_copy = pltpu.make_async_copy(meta, smeta, meta_sem)
    meta_copy.start()

    pair_rows.wait_recv()
    both_rows = [jnp.where(core == of, nx[0], nx[1]) for of in range(2)]
    tile[...] = jnp.concatenate(both_rows, axis=0).astype(BF16)

    @pl.when(core == 0)
    def _():
        gnt[x % 2, shelf] = tile[...]

    @pl.loop(0, 32)
    def _(half):
        @pl.when(2 * half + core > 0)
        def _():
            fresh_copy(2 * half + core).start()

    plane_wait(0, 15).wait_recv()
    sib_copy(0, core).start()
    meta_copy.wait()

    @pl.loop(0, KV_PARTS)
    def _(part):
        key_copy(part).wait()

    lanes = iota((32, 128), 1)
    blank = jnp.zeros((16, 128), BF16)

    def chunk_copy(k):
        return pltpu.make_async_remote_copy(
            src_ref=s32.at[k, sib], dst_ref=r32.at[k],
            send_sem=s_chunk.at[k], recv_sem=r_chunk.at[k], device_id=sibling, device_id_type=MESH,
        )

    def peak_copy(k):
        return pltpu.make_async_remote_copy(
            src_ref=mx.at[k], dst_ref=mxr.at[k], send_sem=s_m.at[k], recv_sem=r_m.at[k],
            device_id=sibling, device_id_type=MESH,
        )

    def block_copy(to_chip, to):
        return pltpu.make_async_remote_copy(
            src_ref=sb.at[to_chip], dst_ref=rb.at[chip], send_sem=all_sems.at[0], recv_sem=all_sems.at[1],
            device_id=to, device_id_type=MESH,
        )

    def side_copy(to_chip, to):
        return pltpu.make_async_remote_copy(
            src_ref=ss.at[to_chip], dst_ref=rs.at[chip], send_sem=all_sems.at[2], recv_sem=all_sems.at[3],
            device_id=to, device_id_type=MESH,
        )

    def scores(k):
        cols = pl.ds(pl.multiple_of(turn(k) * 256, 256), 256)

        @pl.loop(0, SLOTS // GROUP, init_carry=jnp.full((32, 128), LOW, F32))
        def most(group, most):
            for e in range(GROUP):
                n = group * GROUP + e
                r = jnp.maximum(smeta[n, 0], 0)
                b = (jnp.maximum(smeta[n, 1], 1) - 1) % 128
                count = jnp.where(smeta[n, 1] > 0, lens[r] - b * 128, 0)
                parts = [gq[of, r // 8, pl.ds(r % 8, 16, stride=8), :].reshape(2, 8, 128) for of in range(2)]
                heads = jnp.concatenate(parts, axis=1).astype(BF16)
                first = jnp.concatenate([heads[0], blank], axis=1)
                second = jnp.concatenate([blank, heads[1]], axis=1)
                score = lax.dot_general(
                    jnp.concatenate([first, second], axis=0), kvb[n, :, cols],
                    (((1,), (1,)), ((), ())), preferred_element_type=F32,
                )
                valid = lanes < count
                score = jnp.where(valid, score * SCALE, LOW)
                peak = jnp.max(score, axis=1, keepdims=True)
                w = jnp.where(valid, jnp.exp(score - peak), 0.0).astype(BF16)
                wb[n] = w
                pk[n] = jnp.broadcast_to(peak, (32, 128))
                dn[n] = jnp.broadcast_to(jnp.sum(w.astype(F32), axis=1, keepdims=True), (32, 128))
                most = jnp.where(lanes == smeta[n, 0], jnp.maximum(most, peak), most)
            return most

        return most

    def values(k, most):
        cols = pl.ds(pl.multiple_of(1024 + turn(k) * 256, 256), 256)

        @pl.loop(0, SLOTS // GROUP, init_carry=jnp.zeros((32, 128), F32))
        def den(group, den):
            for e in range(GROUP):
                n = group * GROUP + e
                r = smeta[n, 0]
                best = jnp.max(jnp.where(lanes == r, most, LOW), axis=1, keepdims=True)
                factor = jnp.exp(pk[n] - best)
                both = jnp.dot(wb[n], kvb[n, :, cols], preferred_element_type=F32)
                num = jnp.concatenate([both[:16, :128], both[16:, 128:]], axis=0)
                prev = smeta[n, 2]
                earlier = jnp.where(prev >= 0, cb[jnp.maximum(prev, 0)], 0.0)
                cb[n] = num * factor + earlier
                den = den + jnp.where(lanes == r, factor * dn[n], 0.0)
            return den

        mx[k, 0] = most
        mx[k, 1] = den
        peak_copy(k).start()

    def hand_on(k):
        @pl.loop(0, 4)
        def _(i):
            for rl in range(8):
                end = smeta[i * 8 + rl, 3]
                sums = jnp.where(end >= 0, cb[jnp.maximum(end, 0)], 0.0)
                for xh in range(2):
                    for of in range(2):
                        at = pl.ds(xh * 64 + rl, 8, stride=8)
                        s32[k, of, i, at, :] = sums[xh * 16 + of * 8 : xh * 16 + of * 8 + 8]

        chunk_copy(k).start()

    def merge(k):
        kt = turn(k)
        peak_copy(k).wait_recv()
        top, other = mx[k, 0], mxr[k, 0]
        chip_top = jnp.maximum(top, other)
        mine_f, other_f = jnp.exp(top - chip_top), jnp.exp(other - chip_top)
        chip_den = mx[k, 1] * mine_f + mxr[k, 1] * other_f
        mt[...] = jnp.concatenate([mine_f, other_f, chip_top, chip_den], axis=0)
        for w in range(2):
            for xh in range(2):
                row = pl.multiple_of(64 + w * 32 + xh * 16 + core * 8, 8)
                uw[w * 16 + xh * 8 : w * 16 + xh * 8 + 8, :] = mt[pl.ds(row, 8), :]
        lane4 = iota((4, 128), 1)
        packed = [jnp.zeros((4, 128), F32) for _ in range(4)]
        for w in range(2):
            for t in range(4):
                got = uw[pl.ds(w * 16 + t, 4, stride=4), :]
                to = w * 32 + t * 8
                for i in range(4):
                    there = pltpu.roll(got, (to - 8 * i) % 128, 1)
                    packed[i] = jnp.where((lane4 >= to) & (lane4 < to + 8), there, packed[i])
        for i in range(4):
            for j in range(4):
                ss[i * 16 + kt * 4 + j] = packed[i][j : j + 1, :]
        mt[...] = pltpu.roll(mt[...].T, (128 - core * 8) % 128, 1)
        chunk_copy(k).wait_recv()

        @pl.loop(0, 4)
        def _(i):
            factors = mt[pl.ds(pl.multiple_of(i * 8, 8), 8), :]
            for j in range(4):
                total = []
                for t in range(4):
                    lane = (j // 2) * 16 + (j % 2) * 4 + t
                    at = slice(j * 32 + t * 8, j * 32 + t * 8 + 8)
                    total.append(
                        s32[k, core, i, at, :] * factors[:, lane : lane + 1]
                        + r32[k, i, at, :] * factors[:, 32 + lane : 33 + lane]
                    )
                sb[i * 16 + kt * 4 + j] = jnp.concatenate(total, axis=0).astype(BF16)

    def send(k):
        kt = turn(k)

        @pl.loop(0, 16)
        def _(e):
            pz, _, px = beside(e, kt)
            to_chip, to = pz * 16 + kt * 4 + px, place(pz, kt, px)

            @pl.when(k * 16 + e > 0)
            def _():
                block_copy(to_chip, to).start()
                side_copy(to_chip, to).start()

    @pl.loop(0, 5)
    def _(k):
        @pl.when(k < 4)
        def _():
            sib_copy(k, sib).wait_recv()

            @pl.loop(0, 8)
            def _(part):
                of, i = part // 4, part % 4
                for j in range(4):
                    gq[of, i, j * 32 : j * 32 + 32, :] = gat[of, turn(k), i * 4 + j].astype(F32)

            most = scores(k)

            @pl.when(k < 3)
            def _():
                plane_wait(k + 1).wait_recv()
                sib_copy(k + 1, core).start()

            @pl.when(k == 0)
            def _():
                @pl.loop(0, KV_PARTS)
                def _(part):
                    value_copy(part).wait()

            values(k, most)

        @pl.when(k > 0)
        def _():
            merge(k - 1)
            send(k - 1)

        @pl.when(k < 4)
        def _():
            hand_on(k)

    rb[chip] = sb[chip]
    rs[chip] = ss[chip]

    @pl.when(core == 0)
    def _():
        fresh_wait(31).wait_recv()

    @pl.when(core == 1)
    def _():
        fresh_wait(32).wait_recv()

    sib_fresh(core).start()
    sib_fresh(sib).wait_recv()

    @pl.loop(0, 4)
    def _(i):
        for j in range(16):
            fresh = gnt[j % 2, i * 8 + j // 2].astype(F32)
            for of in range(2):
                gn[of, i, j * 8 : j * 8 + 8, :] = fresh[of * 8 : of * 8 + 8]

    @pl.loop(0, 4)
    def _(e):
        found_row = smeta[SLOTS + e, 0]
        which = jnp.maximum(found_row - 1, 0)
        late, r = which // 32, which % 32
        pair = [gn[of, r // 8, pl.ds(r % 8, 16, stride=8), :] for of in range(2)]
        tl[pl.ds(pl.multiple_of(e * 16, 16), 16), :] = jnp.where(found_row > 0, halves(pair[0], pair[1], late > 0), 0.0)
    for j in range(16):
        tail[:, j * 128 : j * 128 + 128] = tl[pl.ds(j, 4, stride=16), :].astype(BF16)

    head = y * 2 + x // 2
    new_rows = []
    for at in (head, head + 8):
        pair = [gn[of, z, pl.ds(pl.multiple_of(at * 8, 8), 8), :] for of in range(2)]
        new_rows.append([halves(pair[0], pair[1], late) for late in (False, True)])
    new_m, new_den, new_num = [], [], []
    for t in range(4):
        mine_q = q[t // 2].astype(F32)[:, (t % 2) * 128 : (t % 2) * 128 + 128]
        found_scores = [
            jnp.sum(mine_q * new_rows[0][j], axis=1, keepdims=True) * SCALE for j in range(t // 2 + 1)
        ]
        peak = found_scores[0]
        for more in found_scores[1:]:
            peak = jnp.maximum(peak, more)
        ws = [jnp.exp(v - peak).astype(BF16).astype(F32) for v in found_scores]
        new_m.append(peak)
        new_den.append(sum(ws[1:], ws[0]))
        num = ws[0] * new_rows[1][0]
        for j in range(1, len(ws)):
            num = num + ws[j] * new_rows[1][j]
        new_num.append(num)
    new_m = jnp.concatenate(new_m, axis=0)
    new_den = jnp.concatenate(new_den, axis=0)
    new_num = jnp.concatenate(new_num, axis=0)

    most = pl.ds(0, CHIPS - 1)
    all_blocks = pltpu.make_async_remote_copy(
        src_ref=sb.at[most], dst_ref=rb.at[most], send_sem=all_sems.at[0], recv_sem=all_sems.at[1],
        device_id=sibling, device_id_type=MESH,
    )
    all_sides = pltpu.make_async_remote_copy(
        src_ref=ss.at[most], dst_ref=rs.at[most], send_sem=all_sems.at[2], recv_sem=all_sems.at[3],
        device_id=sibling, device_id_type=MESH,
    )
    all_sides.wait_recv()
    side = rs[...].reshape(CHIPS, 128)
    side = jnp.concatenate([side, jnp.zeros((128 - CHIPS, 128), F32)], axis=0).T
    side_m, side_den = side[0:32, :CHIPS], side[32:64, :CHIPS]
    final_m = jnp.maximum(jnp.max(side_m, axis=1, keepdims=True), new_m)
    scales = jnp.exp(side_m - final_m)
    new_scale = jnp.exp(new_m - final_m)
    final_den = jnp.sum(scales * side_den, axis=1, keepdims=True) + new_den * new_scale
    total = new_num * new_scale
    all_blocks.wait_recv()
    scales = jnp.concatenate([scales, jnp.zeros((32, 128 - CHIPS), F32)], axis=1)

    @pl.loop(0, CHIPS // 8, init_carry=(total, scales))
    def total_and_scales(group, carry):
        total, scales = carry
        for e in range(8):
            total = total + scales[:, e : e + 1] * rb[group * 8 + e].astype(F32)
        return total, pltpu.roll(scales, 120, 1)

    total = total_and_scales[0]
    result = total / final_den
    for t in range(4):
        out[t // 2, :, (t % 2) * 128 : (t % 2) * 128 + 128] = result[t * 8 : t * 8 + 8].astype(BF16)

    stores = [
        pltpu.make_async_copy(src, dst, io_sem.at[k])
        for k, (src, dst) in enumerate([(out, out_at), (tail, tail_at)])
    ]
    for store in stores:
        store.start()

    all_blocks.wait_send()
    all_sides.wait_send()
    plane_wait(0, 15).wait_send()
    for k in range(1, 4):
        plane_wait(k).wait_send()
    for k in range(4):
        sib_copy(k, core).wait_send()
        peak_copy(k).wait_send()
        chunk_copy(k).wait_send()
    pair_rows.wait_send()

    @pl.when(core == 0)
    def _():
        fresh_wait(31).wait_send()

    @pl.when(core == 1)
    def _():
        fresh_wait(32).wait_send()

    sib_fresh(core).wait_send()
    for store in stores:
        store.wait()


def hand_over(result, rows, out, tail, sems):
    copies = [
        pltpu.make_async_copy(result, out, sems.at[0]),
        pltpu.make_async_copy(rows, tail, sems.at[1]),
    ]
    for copy in copies:
        copy.start()
    for copy in copies:
        copy.wait()


def per_device(kv_pool, queries, new_kv, lengths, block_dev, block_slot, owner_dev, owner_row):
    anywhere = pl.BlockSpec(memory_space=pltpu.HBM)
    dma = pltpu.SemaphoreType.DMA
    result, tail = pl.pallas_call(
        kernel,
        out_shape=(
            jax.ShapeDtypeStruct((2, 8, 256), BF16),
            jax.ShapeDtypeStruct((4, 2048), BF16),
        ),
        in_specs=[anywhere] * 8,
        out_specs=(anywhere, anywhere),
        scratch_shapes=[
            pltpu.VMEM((2, 8, 256), BF16),
            pltpu.VMEM((2, 8, 64), BF16),
            pltpu.VMEM((REQS, 128), I32),
            pltpu.VMEM((REQS, 128), I32),
            pltpu.VMEM((2, REQS), I32),
            pltpu.VMEM((2, REQS), I32),
            pltpu.SMEM((REQS,), I32),
            pltpu.VMEM((2, 8, 256), BF16),
            pltpu.VMEM((4, 2048), BF16),
            pltpu.VMEM((SLOTS, 128, 2048), BF16),
            pltpu.VMEM((2, 4, 16, 32, 128), BF16),
            pltpu.VMEM((2, 8, 128), F32),
            pltpu.VMEM((16, 128), BF16),
            pltpu.VMEM((2, 32, 16, 128), BF16),
            pltpu.VMEM((2, 4, 128, 128), F32),
            pltpu.VMEM((2, 4, 128, 128), F32),
            pltpu.VMEM((SLOTS, 32, 128), BF16),
            pltpu.VMEM((SLOTS, 32, 128), F32),
            pltpu.VMEM((SLOTS, 32, 128), F32),
            pltpu.VMEM((SLOTS, 32, 128), F32),
            pltpu.VMEM((4, 2, 32, 128), F32),
            pltpu.VMEM((4, 2, 32, 128), F32),
            pltpu.VMEM((128, 128), F32),
            pltpu.VMEM((32, 128), F32),
            pltpu.VMEM((4, 2, 4, 128, 128), F32),
            pltpu.VMEM((4, 4, 128, 128), F32),
            pltpu.VMEM((CHIPS, 32, 128), BF16),
            pltpu.VMEM((CHIPS, 32, 128), BF16),
            pltpu.VMEM((CHIPS, 1, 128), F32),
            pltpu.VMEM((CHIPS, 1, 128), F32),
            pltpu.VMEM((64, 128), F32),
            pltpu.VMEM((40, 128), I32),
            pltpu.SMEM((40, 128), I32),
            pltpu.VMEM((40, 128), I32),
            dma((KV_PARTS,)),
            dma((KV_PARTS,)),
            dma((4,)),
            dma((4,)),
            dma((4,)),
            dma((4,)),
            dma((6,)),
            dma((4,)),
            dma((4,)),
            dma((4,)),
            dma((4,)),
            dma((4,)),
            dma,
            dma((7,)),
        ],
        compiler_params=pltpu.CompilerParams(
            collective_id=0, has_side_effects=True, vmem_limit_bytes=56 * 1024 * 1024
        ),
    )(kv_pool, queries, new_kv, block_dev, block_slot, owner_dev, owner_row, lengths)
    return pl.pallas_call(
        hand_over,
        out_shape=(
            jax.ShapeDtypeStruct((2, 8, 256), BF16),
            jax.ShapeDtypeStruct((4, 2048), BF16),
        ),
        in_specs=[anywhere] * 2,
        out_specs=(anywhere, anywhere),
        scratch_shapes=[dma((2,))],
    )(result, tail)


def solution(mesh):
    placed = (
        P(("inst", "seq"), None, None),
        P(None, "inst", "seq"),
        P(None, "inst", "seq"),
        P(),
        P(),
        P(),
        P(),
        P(),
    )
    return jax.shard_map(
        per_device,
        mesh=mesh,
        in_specs=placed,
        out_specs=(P(None, "inst", "seq"), P(("inst", "seq"), None)),
        check_vma=False,
    )
```

```python
import math

import jax
import jax.numpy as jnp
from jax import lax
from jax.experimental import pallas as pl
from jax.experimental.pallas import tpu as pltpu
from jax.sharding import PartitionSpec as P

MESH = pl.DeviceIdType.MESH
F32 = jnp.float32
BF16 = jnp.bfloat16
I32 = jnp.int32

N = 4
CHIPS = 64
SLOTS = 32
REQS = 32
LOW = -1e30
SCALE = 1.0 / math.sqrt(128)
UNROLL = 4
GROUP = 32
SHIFT = (0, 2, 1, 3)
KV_PARTS = SLOTS // UNROLL


def iota(shape, dim):
    return lax.broadcasted_iota(I32, shape, dim)


def halves(first, second, late):
    lane = iota(first.shape, 1)
    if late is True:
        return jnp.where(lane < 64, pltpu.roll(first, 64, 1), second)
    if late is False:
        return jnp.where(lane < 64, first, pltpu.roll(second, 64, 1))
    low = jnp.where(late, pltpu.roll(first, 64, 1), first)
    high = jnp.where(late, second, pltpu.roll(second, 64, 1))
    return jnp.where(lane < 64, low, high)


def kernel(
    kv, q_in, nk_in, dev_in, slot_in, own_dev_in, own_row_in, lens_in, out_at, tail_at,
    q, nk, dev, slot, own_dev, own_row, lens, out, tail,
    kvb, gat, nx, tile, gnt, gq, gn, wb, pk, dn, cb, mx, mxr, mt, uw, s32, r32, sb, rb, ss, rs, tl, meta, smeta, codes,
    k_sem, v_sem, sg, rg, s_sib, r_sib, n_sems, s_m, r_m, s_chunk, r_chunk, b_sems, e_sems, meta_sem, io_sem,
):
    z = lax.axis_index("inst")
    c = lax.axis_index("seq")
    y, x, core = c // 8, (c // 2) % 4, c % 2
    me = z * 32 + c
    chip = z * 16 + y * 4 + x
    sib = 1 - core
    sibling = (z, y * 8 + x * 2 + sib)

    def place(pz, py, px):
        return (pz, py * 8 + px * 2 + core)

    loads = [
        pltpu.make_async_copy(src, dst, io_sem.at[k])
        for k, (src, dst) in enumerate([
            (q_in, q), (nk_in, nk), (dev_in, dev), (slot_in, slot),
            (own_dev_in, own_dev), (own_row_in, own_row), (lens_in, lens),
        ])
    ]
    for load in loads:
        load.start()

    def offset(d):
        return (z + d // 16) % 4, (y + (d // 4) % 4) % 4, (x + d % 4) % 4

    def beside(e, py):
        return (z + e // 4) % 4, py, (x + e % 4) % 4

    barrier = pltpu.get_barrier_semaphore()

    @pl.loop(1, 16)
    def _(e):
        pl.semaphore_signal(barrier, inc=1, device_id=place(*beside(e, y)), device_id_type=MESH)

    for m in range(1, 4):
        pl.semaphore_signal(barrier, inc=1, device_id=place(z, (y + m) % 4, x), device_id_type=MESH)
    pl.semaphore_signal(barrier, inc=1, device_id=sibling, device_id_type=MESH)

    def key_copy(part):
        span = pl.ds(part * UNROLL, UNROLL)
        cols = pl.ds(0, 1024)
        return pltpu.make_async_copy(kv.at[span, :, cols], kvb.at[span, :, cols], k_sem.at[part])

    def value_copy(part):
        span = pl.ds(part * UNROLL, UNROLL)
        cols = pl.ds(1024, 1024)
        return pltpu.make_async_copy(kv.at[span, :, cols], kvb.at[span, :, cols], v_sem.at[part])

    @pl.loop(0, KV_PARTS)
    def _(part):
        key_copy(part).start()

    spot = z * 4 + x
    for load in loads[:2]:
        load.wait()
    own = [q[s].astype(F32) for s in range(2)]
    gat[core, y, spot] = jnp.concatenate(
        [own[0][:, :128], own[0][:, 128:], own[1][:, :128], own[1][:, 128:]], axis=0
    ).astype(BF16)
    nx[0] = jnp.concatenate([nk[0].astype(F32), nk[1].astype(F32)], axis=1)

    pl.semaphore_wait(barrier, 19)

    def shift(k):
        return jnp.where(k == 1, 2, jnp.where(k == 2, 1, k))

    def turn(k):
        return (y + shift(k)) % 4

    def push(block, k, to):
        return pltpu.make_async_remote_copy(
            src_ref=block, dst_ref=block, send_sem=sg.at[k], recv_sem=rg.at[k],
            device_id=to, device_id_type=MESH,
        )

    def plane_copy(e):
        return push(gat.at[core, y, spot], 0, place(*beside(e, y)))

    def across_copy():
        return push(gat.at[core, y, spot], 4, place(z, (y + 2) % 4, x))

    def relay_copy(e):
        return push(gat.at[core, (y + 2) % 4, spot], 1, place(*beside(e, y)))

    def next_copy(m):
        return push(gat.at[core, y], 2 if m == 3 else 3, place(z, (y + m) % 4, x))

    def arrived(k, plane, blocks):
        return push(gat.at[core, plane, pl.ds(0, blocks)], k, sibling)

    def sib_copy(k, of):
        block = gat.at[of, turn(k)]
        return pltpu.make_async_remote_copy(
            src_ref=block, dst_ref=block, send_sem=s_sib.at[k], recv_sem=r_sib.at[k],
            device_id=sibling, device_id_type=MESH,
        )

    across_copy().start()

    @pl.loop(1, 16)
    def _(e):
        plane_copy(e).start()

    pair_rows = pltpu.make_async_remote_copy(
        src_ref=nx.at[0], dst_ref=nx.at[1], send_sem=n_sems.at[0], recv_sem=n_sems.at[1],
        device_id=sibling, device_id_type=MESH,
    )
    pair_rows.start()
    shelf = z * 8 + y * 2 + x // 2

    def fresh_copy(d):
        return pltpu.make_async_remote_copy(
            src_ref=tile, dst_ref=gnt.at[x % 2, shelf], send_sem=n_sems.at[2], recv_sem=n_sems.at[3],
            device_id=place(*offset(d)), device_id_type=MESH,
        )

    def fresh_wait(blocks):
        block = gnt.at[0, pl.ds(0, blocks)]
        return pltpu.make_async_remote_copy(
            src_ref=block, dst_ref=block, send_sem=n_sems.at[2], recv_sem=n_sems.at[3],
            device_id=sibling, device_id_type=MESH,
        )

    def sib_fresh(of):
        block = gnt.at[(x + of) % 2]
        return pltpu.make_async_remote_copy(
            src_ref=block, dst_ref=block, send_sem=n_sems.at[4], recv_sem=n_sems.at[5],
            device_id=sibling, device_id_type=MESH,
        )

    @pl.loop(0, KV_PARTS)
    def _(part):
        value_copy(part).start()

    for load in loads[2:]:
        load.wait()
    mine = jnp.where(dev[...] == me, slot[...], -1)
    code = iota((REQS, 128), 0) * 128 + iota((REQS, 128), 1) + 1

    @pl.loop(0, SLOTS // 4)
    def _(group):
        for e in range(4):
            n = group * 4 + e
            codes[pl.ds(n, 1), :] = jnp.sum(jnp.where(mine == n, code, 0), axis=0, keepdims=True)

    owned = jnp.where(own_dev[...] == me, own_row[...], -1)
    row_code = iota((2, REQS), 0) * REQS + iota((2, REQS), 1) + 1
    pad_row = jnp.zeros((1, 96), I32)
    for e in range(4):
        hit = jnp.sum(jnp.where(owned == e, row_code, 0), axis=0, keepdims=True)
        codes[SLOTS + e : SLOTS + e + 1, :] = jnp.concatenate([hit, pad_row], axis=1)
    codes[SLOTS + 4 :, :] = jnp.zeros((4, 128), I32)

    found = jnp.broadcast_to(jnp.sum(codes[...], axis=1, keepdims=True), (40, 128))
    held = found[:SLOTS]
    req_col = jnp.where(held > 0, jnp.minimum((held - 1) >> 7, REQS - 1), -1)
    rows, lanes = iota((SLOTS, 128), 0), iota((SLOTS, 128), 1)
    req_row = jnp.sum(jnp.where(rows == lanes, req_col, 0), axis=0, keepdims=True)
    req_row = jnp.where(lanes < SLOTS, jnp.broadcast_to(req_row, (SLOTS, 128)), -2)
    before = jnp.max(jnp.where((req_row == req_col) & (lanes < rows), lanes, -1), axis=1, keepdims=True)
    last = jnp.max(jnp.where(req_row == rows, lanes, -1), axis=1, keepdims=True)
    meta[:SLOTS] = jnp.where(
        lanes == 0, req_col, jnp.where(lanes == 1, held, jnp.where(lanes == 2, before, last))
    )
    meta[SLOTS:] = found[SLOTS:]
    meta_copy = pltpu.make_async_copy(meta, smeta, meta_sem)
    meta_copy.start()

    pair_rows.wait_recv()
    both_rows = [jnp.where(core == of, nx[0], nx[1]) for of in range(2)]
    tile[...] = jnp.concatenate(both_rows, axis=0).astype(BF16)

    @pl.when(core == 0)
    def _():
        gnt[x % 2, shelf] = tile[...]

    push(gat.at[core, (y + 2) % 4, spot], 4, sibling).wait_recv()

    @pl.loop(1, 16)
    def _(e):
        relay_copy(e).start()

    arrived(0, y, 15).wait_recv()
    sib_copy(0, core).start()
    for m in (3, 1):
        next_copy(m).start()

    @pl.loop(0, 32)
    def _(half):
        @pl.when(2 * half + core > 0)
        def _():
            fresh_copy(2 * half + core).start()

    meta_copy.wait()

    @pl.loop(0, KV_PARTS)
    def _(part):
        key_copy(part).wait()

    lanes = iota((32, 128), 1)
    blank = jnp.zeros((16, 128), BF16)

    def chunk_copy(k):
        return pltpu.make_async_remote_copy(
            src_ref=s32.at[k, sib], dst_ref=r32.at[k],
            send_sem=s_chunk.at[k], recv_sem=r_chunk.at[k], device_id=sibling, device_id_type=MESH,
        )

    def peak_copy(k):
        return pltpu.make_async_remote_copy(
            src_ref=mx.at[k], dst_ref=mxr.at[k], send_sem=s_m.at[k], recv_sem=r_m.at[k],
            device_id=sibling, device_id_type=MESH,
        )

    def block_copy(k, at, to):
        return pltpu.make_async_remote_copy(
            src_ref=sb.at[turn(k), at], dst_ref=rb.at[y, spot], send_sem=b_sems.at[0, k], recv_sem=b_sems.at[1, k],
            device_id=to, device_id_type=MESH,
        )

    def side_copy(k, at, to):
        return pltpu.make_async_remote_copy(
            src_ref=ss.at[turn(k), at], dst_ref=rs.at[y, spot], send_sem=e_sems.at[0, k], recv_sem=e_sems.at[1, k],
            device_id=to, device_id_type=MESH,
        )

    def all_copy(buf, sems, k):
        block = buf.at[(y + 4 - SHIFT[k]) % 4, pl.ds(0, 16 if k else 15)]
        return pltpu.make_async_remote_copy(
            src_ref=block, dst_ref=block, send_sem=sems.at[0, k], recv_sem=sems.at[1, k],
            device_id=sibling, device_id_type=MESH,
        )

    def scores(k):
        cols = pl.ds(pl.multiple_of(turn(k) * 256, 256), 256)

        @pl.loop(0, SLOTS // GROUP, init_carry=jnp.full((32, 128), LOW, F32))
        def most(group, most):
            for e in range(GROUP):
                n = group * GROUP + e
                r = jnp.maximum(smeta[n, 0], 0)
                b = (jnp.maximum(smeta[n, 1], 1) - 1) % 128
                count = jnp.where(smeta[n, 1] > 0, lens[r] - b * 128, 0)
                parts = [gq[of, r // 8, pl.ds(r % 8, 16, stride=8), :].reshape(2, 8, 128) for of in range(2)]
                heads = jnp.concatenate(parts, axis=1).astype(BF16)
                first = jnp.concatenate([heads[0], blank], axis=1)
                second = jnp.concatenate([blank, heads[1]], axis=1)
                score = lax.dot_general(
                    jnp.concatenate([first, second], axis=0), kvb[n, :, cols],
                    (((1,), (1,)), ((), ())), preferred_element_type=F32,
                )
                valid = lanes < count
                score = jnp.where(valid, score * SCALE, LOW)
                peak = jnp.max(score, axis=1, keepdims=True)
                w = jnp.where(valid, jnp.exp(score - peak), 0.0).astype(BF16)
                wb[n] = w
                pk[n] = jnp.broadcast_to(peak, (32, 128))
                dn[n] = jnp.broadcast_to(jnp.sum(w.astype(F32), axis=1, keepdims=True), (32, 128))
                most = jnp.where(lanes == smeta[n, 0], jnp.maximum(most, peak), most)
            return most

        return most

    def values(k, most):
        cols = pl.ds(pl.multiple_of(1024 + turn(k) * 256, 256), 256)

        @pl.loop(0, SLOTS // GROUP, init_carry=jnp.zeros((32, 128), F32))
        def den(group, den):
            for e in range(GROUP):
                n = group * GROUP + e
                r = smeta[n, 0]
                best = jnp.max(jnp.where(lanes == r, most, LOW), axis=1, keepdims=True)
                factor = jnp.exp(pk[n] - best)
                both = jnp.dot(wb[n], kvb[n, :, cols], preferred_element_type=F32)
                num = jnp.concatenate([both[:16, :128], both[16:, 128:]], axis=0)
                prev = smeta[n, 2]
                earlier = jnp.where(prev >= 0, cb[jnp.maximum(prev, 0)], 0.0)
                cb[n] = num * factor + earlier
                den = den + jnp.where(lanes == r, factor * dn[n], 0.0)
            return den

        mx[k, 0] = most
        mx[k, 1] = den
        peak_copy(k).start()

    def hand_on(k):
        @pl.loop(0, 4)
        def _(i):
            for rl in range(8):
                end = smeta[i * 8 + rl, 3]
                sums = jnp.where(end >= 0, cb[jnp.maximum(end, 0)], 0.0)
                for xh in range(2):
                    for of in range(2):
                        at = pl.ds(xh * 64 + rl, 8, stride=8)
                        s32[k, of, i, at, :] = sums[xh * 16 + of * 8 : xh * 16 + of * 8 + 8]

        chunk_copy(k).start()

    def merge(k):
        kt = turn(k)
        peak_copy(k).wait_recv()
        top, other = mx[k, 0], mxr[k, 0]
        chip_top = jnp.maximum(top, other)
        mine_f, other_f = jnp.exp(top - chip_top), jnp.exp(other - chip_top)
        chip_den = mx[k, 1] * mine_f + mxr[k, 1] * other_f
        mt[...] = jnp.concatenate([mine_f, other_f, chip_top, chip_den], axis=0)
        for w in range(2):
            for xh in range(2):
                row = pl.multiple_of(64 + w * 32 + xh * 16 + core * 8, 8)
                uw[w * 16 + xh * 8 : w * 16 + xh * 8 + 8, :] = mt[pl.ds(row, 8), :]
        lane4 = iota((4, 128), 1)
        packed = [jnp.zeros((4, 128), F32) for _ in range(4)]
        for w in range(2):
            for t in range(4):
                got = uw[pl.ds(w * 16 + t, 4, stride=4), :]
                to = w * 32 + t * 8
                for i in range(4):
                    there = pltpu.roll(got, (to - 8 * i) % 128, 1)
                    packed[i] = jnp.where((lane4 >= to) & (lane4 < to + 8), there, packed[i])
        for i in range(4):
            for j in range(4):
                ss[kt, i * 4 + j] = packed[i][j : j + 1, :]
        mt[...] = pltpu.roll(mt[...].T, (128 - core * 8) % 128, 1)
        chunk_copy(k).wait_recv()

        @pl.loop(0, 4)
        def _(i):
            factors = mt[pl.ds(pl.multiple_of(i * 8, 8), 8), :]
            for j in range(4):
                total = []
                for t in range(4):
                    lane = (j // 2) * 16 + (j % 2) * 4 + t
                    at = slice(j * 32 + t * 8, j * 32 + t * 8 + 8)
                    total.append(
                        s32[k, core, i, at, :] * factors[:, lane : lane + 1]
                        + r32[k, i, at, :] * factors[:, 32 + lane : 33 + lane]
                    )
                sb[kt, i * 4 + j] = jnp.concatenate(total, axis=0).astype(BF16)

    def send(k):
        kt = turn(k)

        @pl.loop(0, 16)
        def _(e):
            pz, _, px = beside(e, kt)
            at, to = pz * 4 + px, place(pz, kt, px)

            @pl.when(k * 16 + e > 0)
            def _():
                block_copy(k, at, to).start()
                side_copy(k, at, to).start()

    def pass_fresh():
        @pl.when(core == 0)
        def _():
            fresh_wait(31).wait_recv()

        @pl.when(core == 1)
        def _():
            fresh_wait(32).wait_recv()

        sib_fresh(core).start()

    @pl.loop(0, 5)
    def _(k):
        @pl.when(k < 4)
        def _():
            sib_copy(k, sib).wait_recv()

            @pl.loop(0, 8)
            def _(part):
                of, i = part // 4, part % 4
                for j in range(4):
                    gq[of, i, j * 32 : j * 32 + 32, :] = gat[of, turn(k), i * 4 + j].astype(F32)

            most = scores(k)

            for after, off, blocks in ((0, 2, 15), (1, 1, 16), (2, 3, 16)):
                @pl.when(k == after)
                def _():
                    arrived(after + 1, (y + off) % 4, blocks).wait_recv()
                    sib_copy(after + 1, core).start()

            @pl.when(k == 0)
            def _():
                @pl.loop(0, KV_PARTS)
                def _(part):
                    value_copy(part).wait()

            values(k, most)
            hand_on(k)

        @pl.when(k > 0)
        def _():
            merge(k - 1)
            send(k - 1)

        @pl.when(k == 3)
        def _():
            pass_fresh()

    rb[y, spot] = sb[y, spot]
    rs[y, spot] = ss[y, spot]

    sib_fresh(sib).wait_recv()

    @pl.loop(0, 4)
    def _(i):
        for j in range(16):
            fresh = gnt[j % 2, i * 8 + j // 2].astype(F32)
            for of in range(2):
                gn[of, i, j * 8 : j * 8 + 8, :] = fresh[of * 8 : of * 8 + 8]

    @pl.loop(0, 4)
    def _(e):
        found_row = smeta[SLOTS + e, 0]
        which = jnp.maximum(found_row - 1, 0)
        late, r = which // 32, which % 32
        pair = [gn[of, r // 8, pl.ds(r % 8, 16, stride=8), :] for of in range(2)]
        tl[pl.ds(pl.multiple_of(e * 16, 16), 16), :] = jnp.where(found_row > 0, halves(pair[0], pair[1], late > 0), 0.0)
    for j in range(16):
        tail[:, j * 128 : j * 128 + 128] = tl[pl.ds(j, 4, stride=16), :].astype(BF16)

    head = y * 2 + x // 2
    new_rows = []
    for at in (head, head + 8):
        pair = [gn[of, z, pl.ds(pl.multiple_of(at * 8, 8), 8), :] for of in range(2)]
        new_rows.append([halves(pair[0], pair[1], late) for late in (False, True)])
    new_m, new_den, new_num = [], [], []
    for t in range(4):
        mine_q = q[t // 2].astype(F32)[:, (t % 2) * 128 : (t % 2) * 128 + 128]
        found_scores = [
            jnp.sum(mine_q * new_rows[0][j], axis=1, keepdims=True) * SCALE for j in range(t // 2 + 1)
        ]
        peak = found_scores[0]
        for more in found_scores[1:]:
            peak = jnp.maximum(peak, more)
        ws = [jnp.exp(v - peak).astype(BF16).astype(F32) for v in found_scores]
        new_m.append(peak)
        new_den.append(sum(ws[1:], ws[0]))
        num = ws[0] * new_rows[1][0]
        for j in range(1, len(ws)):
            num = num + ws[j] * new_rows[1][j]
        new_num.append(num)
    new_m = jnp.concatenate(new_m, axis=0)
    new_den = jnp.concatenate(new_den, axis=0)
    new_num = jnp.concatenate(new_num, axis=0)

    def take_in(phases, top, den, total):
        planes = [(y + 4 - SHIFT[k]) % 4 for k in phases]
        count = 16 * len(phases)
        for k in phases:
            all_copy(rs, e_sems, k).wait_recv()
        side = [rs[plane].reshape(16, 128) for plane in planes]
        side = jnp.concatenate(side + [jnp.zeros((128 - count, 128), F32)], axis=0).T
        side_m, side_den = side[0:32, :count], side[32:64, :count]
        new_top = jnp.maximum(jnp.max(side_m, axis=1, keepdims=True), top)
        scales = jnp.exp(side_m - new_top)
        old_scale = jnp.exp(top - new_top)
        den = jnp.sum(scales * side_den, axis=1, keepdims=True) + den * old_scale
        total = total * old_scale
        for k, plane in enumerate(planes):
            all_copy(rb, b_sems, phases[k]).wait_recv()
            for e in range(16):
                total = total + scales[:, k * 16 + e : k * 16 + e + 1] * rb[plane, e].astype(F32)
        return new_top, den, total

    state = take_in((0, 1, 2), new_m, new_den, new_num)
    _, final_den, total = take_in((3,), *state)
    result = total / final_den
    for t in range(4):
        out[t // 2, :, (t % 2) * 128 : (t % 2) * 128 + 128] = result[t * 8 : t * 8 + 8].astype(BF16)

    stores = [
        pltpu.make_async_copy(src, dst, io_sem.at[k])
        for k, (src, dst) in enumerate([(out, out_at), (tail, tail_at)])
    ]
    for store in stores:
        store.start()

    for k in range(4):
        all_copy(sb, b_sems, k).wait_send()
        all_copy(ss, e_sems, k).wait_send()
    across_copy().wait_send()
    arrived(0, y, 15).wait_send()
    arrived(1, y, 15).wait_send()
    for m in (3, 1):
        next_copy(m).wait_send()
    for k in range(4):
        sib_copy(k, core).wait_send()
        peak_copy(k).wait_send()
        chunk_copy(k).wait_send()
    pair_rows.wait_send()

    @pl.when(core == 0)
    def _():
        fresh_wait(31).wait_send()

    @pl.when(core == 1)
    def _():
        fresh_wait(32).wait_send()

    sib_fresh(core).wait_send()
    for store in stores:
        store.wait()


def hand_over(result, rows, out, tail, sems):
    copies = [
        pltpu.make_async_copy(result, out, sems.at[0]),
        pltpu.make_async_copy(rows, tail, sems.at[1]),
    ]
    for copy in copies:
        copy.start()
    for copy in copies:
        copy.wait()


def per_device(kv_pool, queries, new_kv, lengths, block_dev, block_slot, owner_dev, owner_row):
    anywhere = pl.BlockSpec(memory_space=pltpu.HBM)
    dma = pltpu.SemaphoreType.DMA
    result, tail = pl.pallas_call(
        kernel,
        out_shape=(
            jax.ShapeDtypeStruct((2, 8, 256), BF16),
            jax.ShapeDtypeStruct((4, 2048), BF16),
        ),
        in_specs=[anywhere] * 8,
        out_specs=(anywhere, anywhere),
        scratch_shapes=[
            pltpu.VMEM((2, 8, 256), BF16),
            pltpu.VMEM((2, 8, 64), BF16),
            pltpu.VMEM((REQS, 128), I32),
            pltpu.VMEM((REQS, 128), I32),
            pltpu.VMEM((2, REQS), I32),
            pltpu.VMEM((2, REQS), I32),
            pltpu.SMEM((REQS,), I32),
            pltpu.VMEM((2, 8, 256), BF16),
            pltpu.VMEM((4, 2048), BF16),
            pltpu.VMEM((SLOTS, 128, 2048), BF16),
            pltpu.VMEM((2, 4, 16, 32, 128), BF16),
            pltpu.VMEM((2, 8, 128), F32),
            pltpu.VMEM((16, 128), BF16),
            pltpu.VMEM((2, 32, 16, 128), BF16),
            pltpu.VMEM((2, 4, 128, 128), F32),
            pltpu.VMEM((2, 4, 128, 128), F32),
            pltpu.VMEM((SLOTS, 32, 128), BF16),
            pltpu.VMEM((SLOTS, 32, 128), F32),
            pltpu.VMEM((SLOTS, 32, 128), F32),
            pltpu.VMEM((SLOTS, 32, 128), F32),
            pltpu.VMEM((4, 2, 32, 128), F32),
            pltpu.VMEM((4, 2, 32, 128), F32),
            pltpu.VMEM((128, 128), F32),
            pltpu.VMEM((32, 128), F32),
            pltpu.VMEM((4, 2, 4, 128, 128), F32),
            pltpu.VMEM((4, 4, 128, 128), F32),
            pltpu.VMEM((4, 16, 32, 128), BF16),
            pltpu.VMEM((4, 16, 32, 128), BF16),
            pltpu.VMEM((4, 16, 1, 128), F32),
            pltpu.VMEM((4, 16, 1, 128), F32),
            pltpu.VMEM((64, 128), F32),
            pltpu.VMEM((40, 128), I32),
            pltpu.SMEM((40, 128), I32),
            pltpu.VMEM((40, 128), I32),
            dma((KV_PARTS,)),
            dma((KV_PARTS,)),
            dma((5,)),
            dma((5,)),
            dma((4,)),
            dma((4,)),
            dma((6,)),
            dma((4,)),
            dma((4,)),
            dma((4,)),
            dma((4,)),
            dma((2, 4)),
            dma((2, 4)),
            dma,
            dma((7,)),
        ],
        compiler_params=pltpu.CompilerParams(
            collective_id=0, has_side_effects=True, vmem_limit_bytes=56 * 1024 * 1024
        ),
    )(kv_pool, queries, new_kv, block_dev, block_slot, owner_dev, owner_row, lengths)
    return pl.pallas_call(
        hand_over,
        out_shape=(
            jax.ShapeDtypeStruct((2, 8, 256), BF16),
            jax.ShapeDtypeStruct((4, 2048), BF16),
        ),
        in_specs=[anywhere] * 2,
        out_specs=(anywhere, anywhere),
        scratch_shapes=[dma((2,))],
    )(result, tail)


def solution(mesh):
    placed = (
        P(("inst", "seq"), None, None),
        P(None, "inst", "seq"),
        P(None, "inst", "seq"),
        P(),
        P(),
        P(),
        P(),
        P(),
    )
    return jax.shard_map(
        per_device,
        mesh=mesh,
        in_specs=placed,
        out_specs=(P(None, "inst", "seq"), P(("inst", "seq"), None)),
        check_vma=False,
    )
```

```python
import math

import jax
import jax.numpy as jnp
from jax import lax
from jax.experimental import pallas as pl
from jax.experimental.pallas import tpu as pltpu
from jax.sharding import PartitionSpec as P

MESH = pl.DeviceIdType.MESH
F32 = jnp.float32
BF16 = jnp.bfloat16
I32 = jnp.int32

N = 4
CHIPS = 64
SLOTS = 32
REQS = 32
LOW = -1e30
SCALE = 1.0 / math.sqrt(128)
UNROLL = 4
GROUP = 32
SHIFT = (0, 2, 1, 3)
KV_PARTS = SLOTS // UNROLL


def iota(shape, dim):
    return lax.broadcasted_iota(I32, shape, dim)


def halves(first, second, late):
    lane = iota(first.shape, 1)
    if late is True:
        return jnp.where(lane < 64, pltpu.roll(first, 64, 1), second)
    if late is False:
        return jnp.where(lane < 64, first, pltpu.roll(second, 64, 1))
    low = jnp.where(late, pltpu.roll(first, 64, 1), first)
    high = jnp.where(late, second, pltpu.roll(second, 64, 1))
    return jnp.where(lane < 64, low, high)


def kernel(
    kv, q_in, nk_in, dev_in, slot_in, own_dev_in, own_row_in, lens_in, out_at, tail_at,
    q, nk, dev, slot, own_dev, own_row, lens, out, tail,
    info, kvb, gat, nx, tile, gnt, gq, gn, wb, pk, dn, cb, mx, mxr, mt, lift, uw, s32, r32, sb, rb, ss, rs, tl, meta, smeta, codes,
    k_sem, v_sem, sg, rg, s_sib, r_sib, n_sems, s_m, r_m, s_chunk, r_chunk, b_sems, e_sems, meta_sem, io_sem,
):
    z = lax.axis_index("inst")
    c = lax.axis_index("seq")
    y, x, core = c >> 3, (c >> 1) & 3, c & 1
    zs, ys, xs = [[(v + d) & 3 for d in range(4)] for v in (z, y, x)]
    me = z * 32 + c
    chip = z * 16 + y * 4 + x
    sib = 1 - core
    sibling = (z, y * 8 + x * 2 + sib)

    def place(pz, py, px):
        return (pz, py * 8 + px * 2 + core)

    loads = [
        pltpu.make_async_copy(src, dst, io_sem.at[k])
        for k, (src, dst) in enumerate([
            (q_in, q), (nk_in, nk), (dev_in, dev), (slot_in, slot),
            (own_dev_in, own_dev), (own_row_in, own_row), (lens_in, lens),
        ])
    ]
    for load in loads[:2]:
        load.start()

    def beside(e, py):
        return zs[e // 4], py, xs[e % 4]

    barrier = pltpu.get_barrier_semaphore()

    for e in range(1, 16):
        pl.semaphore_signal(barrier, inc=1, device_id=place(*beside(e, y)), device_id_type=MESH)
    for m in range(1, 4):
        pl.semaphore_signal(barrier, inc=1, device_id=place(z, ys[m], x), device_id_type=MESH)
    pl.semaphore_signal(barrier, inc=1, device_id=sibling, device_id_type=MESH)
    for load in loads[2:]:
        load.start()

    def key_copy(part):
        span = pl.ds(part * UNROLL, UNROLL)
        cols = pl.ds(0, 1024)
        return pltpu.make_async_copy(kv.at[span, :, cols], kvb.at[span, :, cols], k_sem.at[part])

    def value_copy(part):
        span = pl.ds(part * UNROLL, UNROLL)
        cols = pl.ds(1024, 1024)
        return pltpu.make_async_copy(kv.at[span, :, cols], kvb.at[span, :, cols], v_sem.at[part])

    @pl.loop(0, KV_PARTS)
    def _(part):
        key_copy(part).start()

    spot = z * 4 + x
    for load in loads[:2]:
        load.wait()
    own = [q[s].astype(F32) for s in range(2)]
    gat[core, y, spot] = jnp.concatenate(
        [own[0][:, :128], own[0][:, 128:], own[1][:, :128], own[1][:, 128:]], axis=0
    ).astype(BF16)
    nx[0] = jnp.concatenate([nk[0].astype(F32), nk[1].astype(F32)], axis=1)

    pl.semaphore_wait(barrier, 19)

    def turn(k):
        return (y + ((k & 1) << 1) + (k >> 1)) & 3

    def push(block, k, to):
        return pltpu.make_async_remote_copy(
            src_ref=block, dst_ref=block, send_sem=sg.at[k], recv_sem=rg.at[k],
            device_id=to, device_id_type=MESH,
        )

    def plane_copy(e):
        return push(gat.at[core, y, spot], 0, place(*beside(e, y)))

    def across_copy():
        return push(gat.at[core, y, spot], 4, place(z, ys[2], x))

    def relay_copy(e):
        return push(gat.at[core, ys[2], spot], 1, place(*beside(e, y)))

    def next_copy(m):
        return push(gat.at[core, y], 2 if m == 3 else 3, place(z, ys[m], x))

    def arrived(k, plane, blocks):
        return push(gat.at[core, plane, pl.ds(0, blocks)], k, sibling)

    def sib_copy(k, of):
        block = gat.at[of, turn(k)]
        return pltpu.make_async_remote_copy(
            src_ref=block, dst_ref=block, send_sem=s_sib.at[k], recv_sem=r_sib.at[k],
            device_id=sibling, device_id_type=MESH,
        )

    across_copy().start()

    for e in range(1, 16):
        plane_copy(e).start()

    pair_rows = pltpu.make_async_remote_copy(
        src_ref=nx.at[0], dst_ref=nx.at[1], send_sem=n_sems.at[0], recv_sem=n_sems.at[1],
        device_id=sibling, device_id_type=MESH,
    )
    pair_rows.start()
    shelf = z * 2 + (x >> 1)
    side_of = (x + core) & 1

    def fresh_copy(e):
        return pltpu.make_async_remote_copy(
            src_ref=tile, dst_ref=gnt.at[y, x & 1, shelf], send_sem=n_sems.at[2], recv_sem=n_sems.at[3],
            device_id=place(*beside(e, y)), device_id_type=MESH,
        )

    def fresh_wait(tiles):
        block = gnt.at[y, side_of, pl.ds(0, tiles)]
        return pltpu.make_async_remote_copy(
            src_ref=block, dst_ref=block, send_sem=n_sems.at[2], recv_sem=n_sems.at[3],
            device_id=sibling, device_id_type=MESH,
        )

    def fresh_plane(m):
        block = gnt.at[y, side_of]
        return pltpu.make_async_remote_copy(
            src_ref=block, dst_ref=block, send_sem=n_sems.at[4], recv_sem=n_sems.at[5],
            device_id=place(z, ys[m], x), device_id_type=MESH,
        )

    def fresh_planes():
        block = gnt.at[pl.ds(0, 3), side_of]
        return pltpu.make_async_remote_copy(
            src_ref=block, dst_ref=block, send_sem=n_sems.at[4], recv_sem=n_sems.at[5],
            device_id=sibling, device_id_type=MESH,
        )

    def sib_fresh(of):
        block = gnt.at[:, (x + of) & 1]
        return pltpu.make_async_remote_copy(
            src_ref=block, dst_ref=block, send_sem=n_sems.at[6], recv_sem=n_sems.at[7],
            device_id=sibling, device_id_type=MESH,
        )

    @pl.loop(0, KV_PARTS)
    def _(part):
        value_copy(part).start()

    for load in loads[2:]:
        load.wait()
    mine = jnp.where(dev[...] == me, slot[...], -1)
    code = iota((REQS, 128), 0) * 128 + iota((REQS, 128), 1) + 1

    @pl.loop(0, SLOTS // 4)
    def _(group):
        for e in range(4):
            n = group * 4 + e
            codes[pl.ds(n, 1), :] = jnp.sum(jnp.where(mine == n, code, 0), axis=0, keepdims=True)

    owned = jnp.where(own_dev[...] == me, own_row[...], -1)
    row_code = iota((2, REQS), 0) * REQS + iota((2, REQS), 1) + 1
    pad_row = jnp.zeros((1, 96), I32)
    for e in range(4):
        hit = jnp.sum(jnp.where(owned == e, row_code, 0), axis=0, keepdims=True)
        codes[SLOTS + e : SLOTS + e + 1, :] = jnp.concatenate([hit, pad_row], axis=1)
    codes[SLOTS + 4 :, :] = jnp.zeros((4, 128), I32)

    found = jnp.broadcast_to(jnp.sum(codes[...], axis=1, keepdims=True), (40, 128))
    held = found[:SLOTS]
    req_col = jnp.where(held > 0, jnp.minimum((held - 1) >> 7, REQS - 1), -1)
    rows, lanes = iota((SLOTS, 128), 0), iota((SLOTS, 128), 1)
    req_row = jnp.sum(jnp.where(rows == lanes, req_col, 0), axis=0, keepdims=True)
    req_row = jnp.where(lanes < SLOTS, jnp.broadcast_to(req_row, (SLOTS, 128)), -2)
    before = jnp.max(jnp.where((req_row == req_col) & (lanes < rows), lanes, -1), axis=1, keepdims=True)
    last = jnp.max(jnp.where(req_row == rows, lanes, -1), axis=1, keepdims=True)
    meta[:SLOTS] = jnp.where(
        lanes == 0, req_col, jnp.where(lanes == 1, held, jnp.where(lanes == 2, before, last))
    )
    meta[SLOTS:] = found[SLOTS:]
    meta_copy = pltpu.make_async_copy(meta, smeta, meta_sem)
    meta_copy.start()

    pair_rows.wait_recv()
    both_rows = [jnp.where(core == of, nx[0], nx[1]) for of in range(2)]
    tile[...] = jnp.concatenate(both_rows, axis=0).astype(BF16)

    @pl.when(core == 0)
    def _():
        gnt[y, x & 1, shelf] = tile[...]

    push(gat.at[core, ys[2], spot], 4, sibling).wait_recv()

    for e in range(1, 16):
        relay_copy(e).start()

    arrived(0, y, 15).wait_recv()
    sib_copy(0, core).start()
    for m in (3, 1):
        next_copy(m).start()

    for of in range(2):
        @pl.when(core == of)
        def _():
            for e in range(2 - of, 16, 2):
                fresh_copy(e).start()

    meta_copy.wait()

    @pl.loop(0, SLOTS)
    def _(n):
        req, held, prev, end = smeta[n, 0], smeta[n, 1], smeta[n, 2], smeta[n, 3]
        r = jnp.maximum(req, 0)
        b = (jnp.maximum(held, 1) - 1) & 127
        info[0, n] = req
        info[1, n] = r >> 3
        info[2, n] = r & 7
        info[3, n] = jnp.where(held > 0, lens[r] - b * 128, 0)
        info[4, n] = prev
        info[5, n] = jnp.maximum(prev, 0)
        info[6, n] = end
        info[7, n] = jnp.maximum(end, 0)


    @pl.loop(0, KV_PARTS)
    def _(part):
        key_copy(part).wait()

    lanes = iota((32, 128), 1)
    blank = jnp.zeros((16, 128), BF16)

    def chunk_copy(k):
        return pltpu.make_async_remote_copy(
            src_ref=s32.at[k, sib], dst_ref=r32.at[k],
            send_sem=s_chunk.at[k], recv_sem=r_chunk.at[k], device_id=sibling, device_id_type=MESH,
        )

    def peak_copy(k):
        return pltpu.make_async_remote_copy(
            src_ref=mx.at[k], dst_ref=mxr.at[k], send_sem=s_m.at[k], recv_sem=r_m.at[k],
            device_id=sibling, device_id_type=MESH,
        )

    def block_copy(k, at, to):
        return pltpu.make_async_remote_copy(
            src_ref=sb.at[turn(k), at], dst_ref=rb.at[y, spot], send_sem=b_sems.at[0, k], recv_sem=b_sems.at[1, k],
            device_id=to, device_id_type=MESH,
        )

    def side_copy(k, at, to):
        return pltpu.make_async_remote_copy(
            src_ref=ss.at[turn(k), at], dst_ref=rs.at[y, spot], send_sem=e_sems.at[0, k], recv_sem=e_sems.at[1, k],
            device_id=to, device_id_type=MESH,
        )

    def all_copy(buf, sems, k):
        block = buf.at[ys[(4 - SHIFT[k]) % 4], pl.ds(0, 16 if k else 15)]
        return pltpu.make_async_remote_copy(
            src_ref=block, dst_ref=block, send_sem=sems.at[0, k], recv_sem=sems.at[1, k],
            device_id=sibling, device_id_type=MESH,
        )

    def scores(k):
        cols = pl.ds(pl.multiple_of(turn(k) * 256, 256), 256)

        @pl.loop(0, SLOTS // GROUP, init_carry=jnp.full((32, 128), LOW, F32))
        def most(group, most):
            for e in range(GROUP):
                n = group * GROUP + e
                i, rl, count = info[1, n], info[2, n], info[3, n]
                parts = [gq[of, i, pl.ds(rl, 16, stride=8), :].reshape(2, 8, 128) for of in range(2)]
                heads = jnp.concatenate(parts, axis=1).astype(BF16)
                first = jnp.concatenate([heads[0], blank], axis=1)
                second = jnp.concatenate([blank, heads[1]], axis=1)
                score = lax.dot_general(
                    jnp.concatenate([first, second], axis=0), kvb[n, :, cols],
                    (((1,), (1,)), ((), ())), preferred_element_type=F32,
                )
                score = jnp.where(lanes < count, score * SCALE, LOW)
                peak = jnp.max(score, axis=1, keepdims=True)
                wb[n] = jnp.exp(score - peak).astype(BF16)
                pk[n] = jnp.broadcast_to(peak, (32, 128))
                most = jnp.where(lanes == info[0, n], jnp.maximum(most, peak), most)
            return most

        return most

    def values(k, most):
        cols = pl.ds(pl.multiple_of(1024 + turn(k) * 256, 256), 256)
        dn[...] = jnp.dot(
            wb[...].reshape(SLOTS * 32, 128), jnp.ones((128, 128), BF16), preferred_element_type=F32
        ).reshape(SLOTS, 32, 128)

        @pl.loop(0, SLOTS // GROUP, init_carry=jnp.zeros((32, 128), F32))
        def den(group, den):
            for e in range(GROUP):
                n = group * GROUP + e
                r = info[0, n]
                best = jnp.max(jnp.where(lanes == r, most, LOW), axis=1, keepdims=True)
                factor = jnp.exp(pk[n] - best)
                both = jnp.dot(wb[n], kvb[n, :, cols], preferred_element_type=F32)
                num = jnp.concatenate([both[:16, :128], both[16:, 128:]], axis=0)
                earlier = jnp.where(info[4, n] >= 0, cb[info[5, n]], 0.0)
                cb[n] = num * factor + earlier
                den = den + jnp.where(lanes == r, factor * dn[n], 0.0)
            return den

        mx[k, 0] = most
        mx[k, 1] = den
        peak_copy(k).start()

    def hand_on(k):
        @pl.loop(0, 4)
        def _(i):
            for rl in range(8):
                sums = jnp.where(info[6, i * 8 + rl] >= 0, cb[info[7, i * 8 + rl]], 0.0)
                for xh in range(2):
                    for of in range(2):
                        at = pl.ds(xh * 64 + rl, 8, stride=8)
                        s32[k, of, i, at, :] = sums[xh * 16 + of * 8 : xh * 16 + of * 8 + 8]

        chunk_copy(k).start()

    def merge(k):
        kt = turn(k)
        peak_copy(k).wait_recv()
        top, other = mx[k, 0], mxr[k, 0]
        chip_top = jnp.maximum(top, other)
        mine_f, other_f = jnp.exp(top - chip_top), jnp.exp(other - chip_top)
        chip_den = mx[k, 1] * mine_f + mxr[k, 1] * other_f
        mt[0:32, :] = chip_top
        mt[32:64, :] = chip_den
        for w in range(2):
            for xh in range(2):
                row = pl.multiple_of(w * 32 + xh * 16 + core * 8, 8)
                uw[w * 16 + xh * 8 : w * 16 + xh * 8 + 8, :] = mt[pl.ds(row, 8), :]
        lane4 = iota((4, 128), 1)
        packed = [jnp.zeros((4, 128), F32) for _ in range(4)]
        for w in range(2):
            for t in range(4):
                got = uw[pl.ds(w * 16 + t, 4, stride=4), :]
                to = w * 32 + t * 8
                for i in range(4):
                    there = pltpu.roll(got, (to - 8 * i) % 128, 1)
                    packed[i] = jnp.where((lane4 >= to) & (lane4 < to + 8), there, packed[i])
        for i in range(4):
            for j in range(4):
                ss[kt, i * 4 + j] = packed[i][j : j + 1, :]
        both_f = jnp.concatenate([mine_f, other_f, jnp.zeros((64, 128), F32)], axis=0).T
        lift[...] = pltpu.roll(both_f[0:32], (128 - core * 8) % 128, 1)
        chunk_copy(k).wait_recv()

        @pl.loop(0, 4)
        def _(i):
            factors = lift[pl.ds(pl.multiple_of(i * 8, 8), 8), :]
            for j in range(4):
                total = []
                for t in range(4):
                    lane = (j // 2) * 16 + (j % 2) * 4 + t
                    at = slice(j * 32 + t * 8, j * 32 + t * 8 + 8)
                    total.append(
                        s32[k, core, i, at, :] * factors[:, lane : lane + 1]
                        + r32[k, i, at, :] * factors[:, 32 + lane : 33 + lane]
                    )
                sb[kt, i * 4 + j] = jnp.concatenate(total, axis=0).astype(BF16)

    def send(k):
        kt = turn(k)

        def one(e):
            pz, _, px = beside(e, kt)
            at, to = pz * 4 + px, place(pz, kt, px)
            block_copy(k, at, to).start()
            side_copy(k, at, to).start()

        @pl.when(k > 0)
        def _():
            one(0)

        for e in range(1, 16):
            one(e)

    def spread_fresh():
        @pl.when(core == 0)
        def _():
            fresh_wait(7).wait_recv()

        @pl.when(core == 1)
        def _():
            fresh_wait(8).wait_recv()

        for m in range(1, 4):
            fresh_plane(m).start()

    def pass_fresh():
        fresh_planes().wait_recv()
        sib_fresh(core).start()

    @pl.loop(0, 5)
    def _(k):
        @pl.when(k < 4)
        def _():
            sib_copy(k, sib).wait_recv()

            @pl.loop(0, 8)
            def _(part):
                of, i = part >> 2, part & 3
                for j in range(4):
                    gq[of, i, j * 32 : j * 32 + 32, :] = gat[of, turn(k), i * 4 + j].astype(F32)

            most = scores(k)

            for after, off, blocks in ((0, 2, 15), (1, 1, 16), (2, 3, 16)):
                @pl.when(k == after)
                def _():
                    arrived(after + 1, ys[off], blocks).wait_recv()
                    sib_copy(after + 1, core).start()

            @pl.when(k == 0)
            def _():
                @pl.loop(0, KV_PARTS)
                def _(part):
                    value_copy(part).wait()

            values(k, most)
            hand_on(k)

        @pl.when(k > 0)
        def _():
            merge(k - 1)
            send(k - 1)

        @pl.when(k == 1)
        def _():
            spread_fresh()

        @pl.when(k == 3)
        def _():
            pass_fresh()

    rb[y, spot] = sb[y, spot]
    rs[y, spot] = ss[y, spot]

    sib_fresh(sib).wait_recv()

    @pl.loop(0, 4)
    def _(i):
        for j in range(16):
            fresh = gnt[j // 4, j % 2, i * 2 + (j % 4) // 2].astype(F32)
            for of in range(2):
                gn[of, i, j * 8 : j * 8 + 8, :] = fresh[of * 8 : of * 8 + 8]

    @pl.loop(0, 4)
    def _(e):
        found_row = smeta[SLOTS + e, 0]
        which = jnp.maximum(found_row - 1, 0)
        late, r = which >> 5, which & 31
        pair = [gn[of, r >> 3, pl.ds(r & 7, 16, stride=8), :] for of in range(2)]
        tl[pl.ds(pl.multiple_of(e * 16, 16), 16), :] = jnp.where(found_row > 0, halves(pair[0], pair[1], late > 0), 0.0)
    for j in range(16):
        tail[:, j * 128 : j * 128 + 128] = tl[pl.ds(j, 4, stride=16), :].astype(BF16)

    head = y * 2 + x // 2
    new_rows = []
    for at in (head, head + 8):
        pair = [gn[of, z, pl.ds(pl.multiple_of(at * 8, 8), 8), :] for of in range(2)]
        new_rows.append([halves(pair[0], pair[1], late) for late in (False, True)])
    new_m, new_den, new_num = [], [], []
    for t in range(4):
        mine_q = q[t // 2].astype(F32)[:, (t % 2) * 128 : (t % 2) * 128 + 128]
        found_scores = [
            jnp.sum(mine_q * new_rows[0][j], axis=1, keepdims=True) * SCALE for j in range(t // 2 + 1)
        ]
        peak = found_scores[0]
        for more in found_scores[1:]:
            peak = jnp.maximum(peak, more)
        ws = [jnp.exp(v - peak).astype(BF16).astype(F32) for v in found_scores]
        new_m.append(peak)
        new_den.append(sum(ws[1:], ws[0]))
        num = ws[0] * new_rows[1][0]
        for j in range(1, len(ws)):
            num = num + ws[j] * new_rows[1][j]
        new_num.append(num)
    new_m = jnp.concatenate(new_m, axis=0)
    new_den = jnp.concatenate(new_den, axis=0)
    new_num = jnp.concatenate(new_num, axis=0)

    def take_in(phases, top, den, total):
        planes = [ys[(4 - SHIFT[k]) % 4] for k in phases]
        count = 16 * len(phases)
        for k in phases:
            all_copy(rs, e_sems, k).wait_recv()
        side = [rs[plane].reshape(16, 128) for plane in planes]
        side = jnp.concatenate(side + [jnp.zeros((128 - count, 128), F32)], axis=0).T
        side_m, side_den = side[0:32, :count], side[32:64, :count]
        new_top = jnp.maximum(jnp.max(side_m, axis=1, keepdims=True), top)
        scales = jnp.exp(side_m - new_top)
        old_scale = jnp.exp(top - new_top)
        den = jnp.sum(scales * side_den, axis=1, keepdims=True) + den * old_scale
        total = total * old_scale
        for k, plane in enumerate(planes):
            all_copy(rb, b_sems, phases[k]).wait_recv()
            for e in range(16):
                total = total + scales[:, k * 16 + e : k * 16 + e + 1] * rb[plane, e].astype(F32)
        return new_top, den, total

    state = take_in((0, 1, 2), new_m, new_den, new_num)
    _, final_den, total = take_in((3,), *state)
    result = total / final_den
    for t in range(4):
        out[t // 2, :, (t % 2) * 128 : (t % 2) * 128 + 128] = result[t * 8 : t * 8 + 8].astype(BF16)

    stores = [
        pltpu.make_async_copy(src, dst, io_sem.at[k])
        for k, (src, dst) in enumerate([(out, out_at), (tail, tail_at)])
    ]
    for store in stores:
        store.start()

    for k in range(4):
        all_copy(sb, b_sems, k).wait_send()
        all_copy(ss, e_sems, k).wait_send()
    across_copy().wait_send()
    arrived(0, y, 15).wait_send()
    arrived(1, y, 15).wait_send()
    for m in (3, 1):
        next_copy(m).wait_send()
    for k in range(4):
        sib_copy(k, core).wait_send()
        peak_copy(k).wait_send()
        chunk_copy(k).wait_send()
    pair_rows.wait_send()

    @pl.when(core == 0)
    def _():
        fresh_wait(7).wait_send()

    @pl.when(core == 1)
    def _():
        fresh_wait(8).wait_send()

    fresh_planes().wait_send()
    sib_fresh(core).wait_send()
    for store in stores:
        store.wait()


def hand_over(result, rows, out, tail, sems):
    copies = [
        pltpu.make_async_copy(result, out, sems.at[0]),
        pltpu.make_async_copy(rows, tail, sems.at[1]),
    ]
    for copy in copies:
        copy.start()
    for copy in copies:
        copy.wait()


def per_device(kv_pool, queries, new_kv, lengths, block_dev, block_slot, owner_dev, owner_row):
    anywhere = pl.BlockSpec(memory_space=pltpu.HBM)
    dma = pltpu.SemaphoreType.DMA
    result, tail = pl.pallas_call(
        kernel,
        out_shape=(
            jax.ShapeDtypeStruct((2, 8, 256), BF16),
            jax.ShapeDtypeStruct((4, 2048), BF16),
        ),
        in_specs=[anywhere] * 8,
        out_specs=(anywhere, anywhere),
        scratch_shapes=[
            pltpu.VMEM((2, 8, 256), BF16),
            pltpu.VMEM((2, 8, 64), BF16),
            pltpu.VMEM((REQS, 128), I32),
            pltpu.VMEM((REQS, 128), I32),
            pltpu.VMEM((2, REQS), I32),
            pltpu.VMEM((2, REQS), I32),
            pltpu.SMEM((REQS,), I32),
            pltpu.VMEM((2, 8, 256), BF16),
            pltpu.VMEM((4, 2048), BF16),
            pltpu.SMEM((8, SLOTS), I32),
            pltpu.VMEM((SLOTS, 128, 2048), BF16),
            pltpu.VMEM((2, 4, 16, 32, 128), BF16),
            pltpu.VMEM((2, 8, 128), F32),
            pltpu.VMEM((16, 128), BF16),
            pltpu.VMEM((4, 2, 8, 16, 128), BF16),
            pltpu.VMEM((2, 4, 128, 128), F32),
            pltpu.VMEM((2, 4, 128, 128), F32),
            pltpu.VMEM((SLOTS, 32, 128), BF16),
            pltpu.VMEM((SLOTS, 32, 128), F32),
            pltpu.VMEM((SLOTS, 32, 128), F32),
            pltpu.VMEM((SLOTS, 32, 128), F32),
            pltpu.VMEM((4, 2, 32, 128), F32),
            pltpu.VMEM((4, 2, 32, 128), F32),
            pltpu.VMEM((64, 128), F32),
            pltpu.VMEM((32, 128), F32),
            pltpu.VMEM((32, 128), F32),
            pltpu.VMEM((4, 2, 4, 128, 128), F32),
            pltpu.VMEM((4, 4, 128, 128), F32),
            pltpu.VMEM((4, 16, 32, 128), BF16),
            pltpu.VMEM((4, 16, 32, 128), BF16),
            pltpu.VMEM((4, 16, 1, 128), F32),
            pltpu.VMEM((4, 16, 1, 128), F32),
            pltpu.VMEM((64, 128), F32),
            pltpu.VMEM((40, 128), I32),
            pltpu.SMEM((40, 128), I32),
            pltpu.VMEM((40, 128), I32),
            dma((KV_PARTS,)),
            dma((KV_PARTS,)),
            dma((5,)),
            dma((5,)),
            dma((4,)),
            dma((4,)),
            dma((8,)),
            dma((4,)),
            dma((4,)),
            dma((4,)),
            dma((4,)),
            dma((2, 4)),
            dma((2, 4)),
            dma,
            dma((7,)),
        ],
        compiler_params=pltpu.CompilerParams(
            collective_id=0, has_side_effects=True, vmem_limit_bytes=56 * 1024 * 1024
        ),
    )(kv_pool, queries, new_kv, block_dev, block_slot, owner_dev, owner_row, lengths)
    return pl.pallas_call(
        hand_over,
        out_shape=(
            jax.ShapeDtypeStruct((2, 8, 256), BF16),
            jax.ShapeDtypeStruct((4, 2048), BF16),
        ),
        in_specs=[anywhere] * 2,
        out_specs=(anywhere, anywhere),
        scratch_shapes=[dma((2,))],
    )(result, tail)


def solution(mesh):
    placed = (
        P(("inst", "seq"), None, None),
        P(None, "inst", "seq"),
        P(None, "inst", "seq"),
        P(),
        P(),
        P(),
        P(),
        P(),
    )
    return jax.shard_map(
        per_device,
        mesh=mesh,
        in_specs=placed,
        out_specs=(P(None, "inst", "seq"), P(("inst", "seq"), None)),
        check_vma=False,
    )
```

```python
import math

import jax
import jax.numpy as jnp
from jax import lax
from jax.experimental import pallas as pl
from jax.experimental.pallas import tpu as pltpu
from jax.sharding import PartitionSpec as P

MESH = pl.DeviceIdType.MESH
F32 = jnp.float32
BF16 = jnp.bfloat16
I32 = jnp.int32

N = 4
CHIPS = 64
SLOTS = 32
REQS = 32
LOW = -1e30
SCALE = 1.0 / math.sqrt(128)
UNROLL = 4
GROUP = 16
SHIFT = (0, 2, 1, 3)
KV_PARTS = SLOTS // UNROLL


def iota(shape, dim):
    return lax.broadcasted_iota(I32, shape, dim)


def halves(first, second, late):
    lane = iota(first.shape, 1)
    if late is True:
        return jnp.where(lane < 64, pltpu.roll(first, 64, 1), second)
    if late is False:
        return jnp.where(lane < 64, first, pltpu.roll(second, 64, 1))
    low = jnp.where(late, pltpu.roll(first, 64, 1), first)
    high = jnp.where(late, second, pltpu.roll(second, 64, 1))
    return jnp.where(lane < 64, low, high)


def kernel(
    kv, q_in, nk_in, dev_in, slot_in, own_dev_in, own_row_in, lens_in, out_at, tail_at,
    q, nk, dev, slot, own_dev, own_row, lens, out, tail,
    info, kvb, gat, nx, tile, gnt, gq, gn, wb, pk, dn, cb, mx, mxr, mt, lift, uw, s32, r32, sb, rb, ss, rs, tl, meta, smeta, codes,
    k_sem, v_sem, sg, rg, s_sib, r_sib, n_sems, s_m, r_m, s_chunk, r_chunk, b_sems, e_sems, meta_sem, io_sem,
):
    z = lax.axis_index("inst")
    c = lax.axis_index("seq")
    y, x, core = c >> 3, (c >> 1) & 3, c & 1
    zs, ys, xs = [[(v + d) & 3 for d in range(4)] for v in (z, y, x)]
    me = z * 32 + c
    chip = z * 16 + y * 4 + x
    sib = 1 - core
    sibling = (z, y * 8 + x * 2 + sib)

    def place(pz, py, px):
        return (pz, py * 8 + px * 2 + core)

    loads = [
        pltpu.make_async_copy(src, dst, io_sem.at[k])
        for k, (src, dst) in enumerate([
            (q_in, q), (nk_in, nk), (dev_in, dev), (slot_in, slot),
            (own_dev_in, own_dev), (own_row_in, own_row), (lens_in, lens),
        ])
    ]
    for load in loads[:2]:
        load.start()

    def beside(e, py):
        return zs[e // 4], py, xs[e % 4]

    barrier = pltpu.get_barrier_semaphore()

    for e in range(1, 16):
        pl.semaphore_signal(barrier, inc=1, device_id=place(*beside(e, y)), device_id_type=MESH)
    for m in range(1, 4):
        pl.semaphore_signal(barrier, inc=1, device_id=place(z, ys[m], x), device_id_type=MESH)
    pl.semaphore_signal(barrier, inc=1, device_id=sibling, device_id_type=MESH)
    for load in loads[2:]:
        load.start()

    def key_copy(part):
        span = pl.ds(part * UNROLL, UNROLL)
        cols = pl.ds(0, 1024)
        return pltpu.make_async_copy(kv.at[span, :, cols], kvb.at[span, :, cols], k_sem.at[part])

    def value_copy(part):
        span = pl.ds(part * UNROLL, UNROLL)
        cols = pl.ds(1024, 1024)
        return pltpu.make_async_copy(kv.at[span, :, cols], kvb.at[span, :, cols], v_sem.at[part])

    @pl.loop(0, KV_PARTS)
    def _(part):
        key_copy(part).start()

    spot = z * 4 + x
    for load in loads[:2]:
        load.wait()
    own = [q[s].astype(F32) for s in range(2)]
    gat[core, y, spot] = jnp.concatenate(
        [own[0][:, :128], own[0][:, 128:], own[1][:, :128], own[1][:, 128:]], axis=0
    ).astype(BF16)
    nx[0] = jnp.concatenate([nk[0].astype(F32), nk[1].astype(F32)], axis=1)

    pl.semaphore_wait(barrier, 19)

    def turn(k):
        return (y + ((k & 1) << 1) + (k >> 1)) & 3

    def push(block, k, to):
        return pltpu.make_async_remote_copy(
            src_ref=block, dst_ref=block, send_sem=sg.at[k], recv_sem=rg.at[k],
            device_id=to, device_id_type=MESH,
        )

    def plane_copy(e):
        return push(gat.at[core, y, spot], 0, place(*beside(e, y)))

    def across_copy():
        return push(gat.at[core, y, spot], 4, place(z, ys[2], x))

    def relay_copy(e):
        return push(gat.at[core, ys[2], spot], 1, place(*beside(e, y)))

    def next_copy(m):
        return push(gat.at[core, y], 2 if m == 3 else 3, place(z, ys[m], x))

    def arrived(k, plane, blocks):
        return push(gat.at[core, plane, pl.ds(0, blocks)], k, sibling)

    def sib_copy(k, of):
        block = gat.at[of, turn(k)]
        return pltpu.make_async_remote_copy(
            src_ref=block, dst_ref=block, send_sem=s_sib.at[k], recv_sem=r_sib.at[k],
            device_id=sibling, device_id_type=MESH,
        )

    across_copy().start()

    for e in range(1, 16):
        plane_copy(e).start()

    pair_rows = pltpu.make_async_remote_copy(
        src_ref=nx.at[0], dst_ref=nx.at[1], send_sem=n_sems.at[0], recv_sem=n_sems.at[1],
        device_id=sibling, device_id_type=MESH,
    )
    pair_rows.start()
    shelf = z * 2 + (x >> 1)
    side_of = (x + core) & 1

    def fresh_copy(e):
        return pltpu.make_async_remote_copy(
            src_ref=tile, dst_ref=gnt.at[y, x & 1, shelf], send_sem=n_sems.at[2], recv_sem=n_sems.at[3],
            device_id=place(*beside(e, y)), device_id_type=MESH,
        )

    def fresh_wait(tiles):
        block = gnt.at[y, side_of, pl.ds(0, tiles)]
        return pltpu.make_async_remote_copy(
            src_ref=block, dst_ref=block, send_sem=n_sems.at[2], recv_sem=n_sems.at[3],
            device_id=sibling, device_id_type=MESH,
        )

    def fresh_plane(m):
        block = gnt.at[y, side_of]
        return pltpu.make_async_remote_copy(
            src_ref=block, dst_ref=block, send_sem=n_sems.at[4], recv_sem=n_sems.at[5],
            device_id=place(z, ys[m], x), device_id_type=MESH,
        )

    def fresh_planes():
        block = gnt.at[pl.ds(0, 3), side_of]
        return pltpu.make_async_remote_copy(
            src_ref=block, dst_ref=block, send_sem=n_sems.at[4], recv_sem=n_sems.at[5],
            device_id=sibling, device_id_type=MESH,
        )

    def sib_fresh(of):
        block = gnt.at[:, (x + of) & 1]
        return pltpu.make_async_remote_copy(
            src_ref=block, dst_ref=block, send_sem=n_sems.at[6], recv_sem=n_sems.at[7],
            device_id=sibling, device_id_type=MESH,
        )

    @pl.loop(0, KV_PARTS)
    def _(part):
        value_copy(part).start()

    for load in loads[2:]:
        load.wait()
    mine = jnp.where(dev[...] == me, slot[...], -1)
    code = iota((REQS, 128), 0) * 128 + iota((REQS, 128), 1) + 1

    @pl.loop(0, SLOTS // 4)
    def _(group):
        for e in range(4):
            n = group * 4 + e
            codes[pl.ds(n, 1), :] = jnp.sum(jnp.where(mine == n, code, 0), axis=0, keepdims=True)

    owned = jnp.where(own_dev[...] == me, own_row[...], -1)
    row_code = iota((2, REQS), 0) * REQS + iota((2, REQS), 1) + 1
    pad_row = jnp.zeros((1, 96), I32)
    for e in range(4):
        hit = jnp.sum(jnp.where(owned == e, row_code, 0), axis=0, keepdims=True)
        codes[SLOTS + e : SLOTS + e + 1, :] = jnp.concatenate([hit, pad_row], axis=1)
    codes[SLOTS + 4 :, :] = jnp.zeros((4, 128), I32)

    found = jnp.broadcast_to(jnp.sum(codes[...], axis=1, keepdims=True), (40, 128))
    held = found[:SLOTS]
    req_col = jnp.where(held > 0, jnp.minimum((held - 1) >> 7, REQS - 1), -1)
    rows, lanes = iota((SLOTS, 128), 0), iota((SLOTS, 128), 1)
    req_row = jnp.sum(jnp.where(rows == lanes, req_col, 0), axis=0, keepdims=True)
    req_row = jnp.where(lanes < SLOTS, jnp.broadcast_to(req_row, (SLOTS, 128)), -2)
    before = jnp.max(jnp.where((req_row == req_col) & (lanes < rows), lanes, -1), axis=1, keepdims=True)
    last = jnp.max(jnp.where(req_row == rows, lanes, -1), axis=1, keepdims=True)
    meta[:SLOTS] = jnp.where(
        lanes == 0, req_col, jnp.where(lanes == 1, held, jnp.where(lanes == 2, before, last))
    )
    meta[SLOTS:] = found[SLOTS:]
    meta_copy = pltpu.make_async_copy(meta, smeta, meta_sem)
    meta_copy.start()

    pair_rows.wait_recv()
    both_rows = [jnp.where(core == of, nx[0], nx[1]) for of in range(2)]
    tile[...] = jnp.concatenate(both_rows, axis=0).astype(BF16)

    @pl.when(core == 0)
    def _():
        gnt[y, x & 1, shelf] = tile[...]

    push(gat.at[core, ys[2], spot], 4, sibling).wait_recv()

    for e in range(1, 16):
        relay_copy(e).start()

    arrived(0, y, 15).wait_recv()
    sib_copy(0, core).start()
    for m in (3, 1):
        next_copy(m).start()

    for of in range(2):
        @pl.when(core == of)
        def _():
            for e in range(2 - of, 16, 2):
                fresh_copy(e).start()

    meta_copy.wait()

    @pl.loop(0, SLOTS)
    def _(n):
        req, held, prev, end = smeta[n, 0], smeta[n, 1], smeta[n, 2], smeta[n, 3]
        r = jnp.maximum(req, 0)
        b = (jnp.maximum(held, 1) - 1) & 127
        info[0, n] = req
        info[1, n] = r >> 3
        info[2, n] = r & 7
        info[3, n] = jnp.where(held > 0, lens[r] - b * 128, 0)
        info[4, n] = prev
        info[5, n] = jnp.maximum(prev, 0)
        info[6, n] = end
        info[7, n] = jnp.maximum(end, 0)


    @pl.loop(0, KV_PARTS)
    def _(part):
        key_copy(part).wait()

    lanes = iota((32, 128), 1)
    blank = jnp.zeros((16, 128), BF16)

    def chunk_copy(k):
        return pltpu.make_async_remote_copy(
            src_ref=s32.at[k, sib], dst_ref=r32.at[k],
            send_sem=s_chunk.at[k], recv_sem=r_chunk.at[k], device_id=sibling, device_id_type=MESH,
        )

    def peak_copy(k):
        return pltpu.make_async_remote_copy(
            src_ref=mx.at[k], dst_ref=mxr.at[k], send_sem=s_m.at[k], recv_sem=r_m.at[k],
            device_id=sibling, device_id_type=MESH,
        )

    def block_copy(k, at, to):
        return pltpu.make_async_remote_copy(
            src_ref=sb.at[turn(k), at], dst_ref=rb.at[y, spot], send_sem=b_sems.at[0, k], recv_sem=b_sems.at[1, k],
            device_id=to, device_id_type=MESH,
        )

    def side_copy(k, at, to):
        return pltpu.make_async_remote_copy(
            src_ref=ss.at[turn(k), at], dst_ref=rs.at[y, spot], send_sem=e_sems.at[0, k], recv_sem=e_sems.at[1, k],
            device_id=to, device_id_type=MESH,
        )

    def all_copy(buf, sems, k):
        block = buf.at[ys[(4 - SHIFT[k]) % 4], pl.ds(0, 16 if k else 15)]
        return pltpu.make_async_remote_copy(
            src_ref=block, dst_ref=block, send_sem=sems.at[0, k], recv_sem=sems.at[1, k],
            device_id=sibling, device_id_type=MESH,
        )

    def scores(k):
        cols = pl.ds(pl.multiple_of(turn(k) * 256, 256), 256)

        @pl.loop(0, SLOTS // GROUP, init_carry=jnp.full((32, 128), LOW, F32))
        def most(group, most):
            for e in range(GROUP):
                n = group * GROUP + e
                i, rl, count = info[1, n], info[2, n], info[3, n]
                parts = [gq[of, i, pl.ds(rl, 16, stride=8), :].reshape(2, 8, 128) for of in range(2)]
                heads = jnp.concatenate(parts, axis=1).astype(BF16)
                first = jnp.concatenate([heads[0], blank], axis=1)
                second = jnp.concatenate([blank, heads[1]], axis=1)
                score = lax.dot_general(
                    jnp.concatenate([first, second], axis=0), kvb[n, :, cols],
                    (((1,), (1,)), ((), ())), preferred_element_type=F32,
                )
                score = jnp.where(lanes < count, score * SCALE, LOW)
                peak = jnp.max(score, axis=1, keepdims=True)
                wb[n] = jnp.exp(score - peak).astype(BF16)
                pk[n] = jnp.broadcast_to(peak, (32, 128))
                most = jnp.where(lanes == info[0, n], jnp.maximum(most, peak), most)
            return most

        return most

    def values(k, most):
        cols = pl.ds(pl.multiple_of(1024 + turn(k) * 256, 256), 256)
        dn[...] = jnp.dot(
            wb[...].reshape(SLOTS * 32, 128), jnp.ones((128, 128), BF16), preferred_element_type=F32
        ).reshape(SLOTS, 32, 128)

        @pl.loop(0, SLOTS // GROUP, init_carry=jnp.zeros((32, 128), F32))
        def den(group, den):
            for e in range(GROUP):
                n = group * GROUP + e
                r = info[0, n]
                best = jnp.max(jnp.where(lanes == r, most, LOW), axis=1, keepdims=True)
                factor = jnp.exp(pk[n] - best)
                both = jnp.dot(wb[n], kvb[n, :, cols], preferred_element_type=F32)
                num = jnp.concatenate([both[:16, :128], both[16:, 128:]], axis=0)
                earlier = jnp.where(info[4, n] >= 0, cb[info[5, n]], 0.0)
                cb[n] = num * factor + earlier
                den = den + jnp.where(lanes == r, factor * dn[n], 0.0)
            return den

        mx[k, 0] = most
        mx[k, 1] = den
        peak_copy(k).start()

    def hand_on(k):
        @pl.loop(0, 4)
        def _(i):
            for rl in range(8):
                sums = jnp.where(info[6, i * 8 + rl] >= 0, cb[info[7, i * 8 + rl]], 0.0)
                for xh in range(2):
                    for of in range(2):
                        at = pl.ds(xh * 64 + rl, 8, stride=8)
                        s32[k, of, i, at, :] = sums[xh * 16 + of * 8 : xh * 16 + of * 8 + 8]

        chunk_copy(k).start()

    def merge(k):
        kt = turn(k)
        peak_copy(k).wait_recv()
        top, other = mx[k, 0], mxr[k, 0]
        chip_top = jnp.maximum(top, other)
        mine_f, other_f = jnp.exp(top - chip_top), jnp.exp(other - chip_top)
        chip_den = mx[k, 1] * mine_f + mxr[k, 1] * other_f
        mt[0:32, :] = chip_top
        mt[32:64, :] = chip_den
        for w in range(2):
            for xh in range(2):
                row = pl.multiple_of(w * 32 + xh * 16 + core * 8, 8)
                uw[w * 16 + xh * 8 : w * 16 + xh * 8 + 8, :] = mt[pl.ds(row, 8), :]
        lane4 = iota((4, 128), 1)
        packed = [jnp.zeros((4, 128), F32) for _ in range(4)]
        for w in range(2):
            for t in range(4):
                got = uw[pl.ds(w * 16 + t, 4, stride=4), :]
                to = w * 32 + t * 8
                for i in range(4):
                    there = pltpu.roll(got, (to - 8 * i) % 128, 1)
                    packed[i] = jnp.where((lane4 >= to) & (lane4 < to + 8), there, packed[i])
        for i in range(4):
            for j in range(4):
                ss[kt, i * 4 + j] = packed[i][j : j + 1, :]
        both_f = jnp.concatenate([mine_f, other_f, jnp.zeros((64, 128), F32)], axis=0).T
        lift[...] = pltpu.roll(both_f[0:32], (128 - core * 8) % 128, 1)
        chunk_copy(k).wait_recv()

        @pl.loop(0, 4)
        def _(i):
            factors = lift[pl.ds(pl.multiple_of(i * 8, 8), 8), :]
            for j in range(4):
                total = []
                for t in range(4):
                    lane = (j // 2) * 16 + (j % 2) * 4 + t
                    at = slice(j * 32 + t * 8, j * 32 + t * 8 + 8)
                    total.append(
                        s32[k, core, i, at, :] * factors[:, lane : lane + 1]
                        + r32[k, i, at, :] * factors[:, 32 + lane : 33 + lane]
                    )
                sb[kt, i * 4 + j] = jnp.concatenate(total, axis=0).astype(BF16)

    def send(k):
        kt = turn(k)

        def one(e):
            pz, _, px = beside(e, kt)
            at, to = pz * 4 + px, place(pz, kt, px)
            block_copy(k, at, to).start()
            side_copy(k, at, to).start()

        @pl.when(k > 0)
        def _():
            one(0)

        for e in range(1, 16):
            one(e)

    def spread_fresh():
        @pl.when(core == 0)
        def _():
            fresh_wait(7).wait_recv()

        @pl.when(core == 1)
        def _():
            fresh_wait(8).wait_recv()

        for m in range(1, 4):
            fresh_plane(m).start()

    def pass_fresh():
        fresh_planes().wait_recv()
        sib_fresh(core).start()

    @pl.loop(0, 5)
    def _(k):
        @pl.when(k < 4)
        def _():
            sib_copy(k, sib).wait_recv()

            @pl.loop(0, 8)
            def _(part):
                of, i = part >> 2, part & 3
                for j in range(4):
                    gq[of, i, j * 32 : j * 32 + 32, :] = gat[of, turn(k), i * 4 + j].astype(F32)

            most = scores(k)

            for after, off, blocks in ((0, 2, 15), (1, 1, 16), (2, 3, 16)):
                @pl.when(k == after)
                def _():
                    arrived(after + 1, ys[off], blocks).wait_recv()
                    sib_copy(after + 1, core).start()

            @pl.when(k == 0)
            def _():
                @pl.loop(0, KV_PARTS)
                def _(part):
                    value_copy(part).wait()

            values(k, most)
            hand_on(k)

        @pl.when(k > 0)
        def _():
            merge(k - 1)
            send(k - 1)

        @pl.when(k == 1)
        def _():
            spread_fresh()

        @pl.when(k == 3)
        def _():
            pass_fresh()

    rb[y, spot] = sb[y, spot]
    rs[y, spot] = ss[y, spot]

    sib_fresh(sib).wait_recv()

    @pl.loop(0, 4)
    def _(i):
        for j in range(16):
            fresh = gnt[j // 4, j % 2, i * 2 + (j % 4) // 2].astype(F32)
            for of in range(2):
                gn[of, i, j * 8 : j * 8 + 8, :] = fresh[of * 8 : of * 8 + 8]

    @pl.loop(0, 4)
    def _(e):
        found_row = smeta[SLOTS + e, 0]
        which = jnp.maximum(found_row - 1, 0)
        late, r = which >> 5, which & 31
        pair = [gn[of, r >> 3, pl.ds(r & 7, 16, stride=8), :] for of in range(2)]
        tl[pl.ds(pl.multiple_of(e * 16, 16), 16), :] = jnp.where(found_row > 0, halves(pair[0], pair[1], late > 0), 0.0)
    for j in range(16):
        tail[:, j * 128 : j * 128 + 128] = tl[pl.ds(j, 4, stride=16), :].astype(BF16)

    head = y * 2 + x // 2
    new_rows = []
    for at in (head, head + 8):
        pair = [gn[of, z, pl.ds(pl.multiple_of(at * 8, 8), 8), :] for of in range(2)]
        new_rows.append([halves(pair[0], pair[1], late) for late in (False, True)])
    new_m, new_den, new_num = [], [], []
    for t in range(4):
        mine_q = q[t // 2].astype(F32)[:, (t % 2) * 128 : (t % 2) * 128 + 128]
        found_scores = [
            jnp.sum(mine_q * new_rows[0][j], axis=1, keepdims=True) * SCALE for j in range(t // 2 + 1)
        ]
        peak = found_scores[0]
        for more in found_scores[1:]:
            peak = jnp.maximum(peak, more)
        ws = [jnp.exp(v - peak).astype(BF16).astype(F32) for v in found_scores]
        new_m.append(peak)
        new_den.append(sum(ws[1:], ws[0]))
        num = ws[0] * new_rows[1][0]
        for j in range(1, len(ws)):
            num = num + ws[j] * new_rows[1][j]
        new_num.append(num)
    new_m = jnp.concatenate(new_m, axis=0)
    new_den = jnp.concatenate(new_den, axis=0)
    new_num = jnp.concatenate(new_num, axis=0)

    def take_in(phases, top, den, total):
        planes = [ys[(4 - SHIFT[k]) % 4] for k in phases]
        count = 16 * len(phases)
        for k in phases:
            all_copy(rs, e_sems, k).wait_recv()
        side = [rs[plane].reshape(16, 128) for plane in planes]
        side = jnp.concatenate(side + [jnp.zeros((128 - count, 128), F32)], axis=0).T
        side_m, side_den = side[0:32, :count], side[32:64, :count]
        new_top = jnp.maximum(jnp.max(side_m, axis=1, keepdims=True), top)
        scales = jnp.exp(side_m - new_top)
        old_scale = jnp.exp(top - new_top)
        den = jnp.sum(scales * side_den, axis=1, keepdims=True) + den * old_scale
        total = total * old_scale
        for k, plane in enumerate(planes):
            all_copy(rb, b_sems, phases[k]).wait_recv()
            for e in range(16):
                total = total + scales[:, k * 16 + e : k * 16 + e + 1] * rb[plane, e].astype(F32)
        return new_top, den, total

    state = take_in((0, 1, 2), new_m, new_den, new_num)
    _, final_den, total = take_in((3,), *state)
    result = total / final_den
    for t in range(4):
        out[t // 2, :, (t % 2) * 128 : (t % 2) * 128 + 128] = result[t * 8 : t * 8 + 8].astype(BF16)

    stores = [
        pltpu.make_async_copy(src, dst, io_sem.at[k])
        for k, (src, dst) in enumerate([(out, out_at), (tail, tail_at)])
    ]
    for store in stores:
        store.start()

    for k in range(4):
        all_copy(sb, b_sems, k).wait_send()
        all_copy(ss, e_sems, k).wait_send()
    across_copy().wait_send()
    arrived(0, y, 15).wait_send()
    arrived(1, y, 15).wait_send()
    for m in (3, 1):
        next_copy(m).wait_send()
    for k in range(4):
        sib_copy(k, core).wait_send()
        peak_copy(k).wait_send()
        chunk_copy(k).wait_send()
    pair_rows.wait_send()

    @pl.when(core == 0)
    def _():
        fresh_wait(7).wait_send()

    @pl.when(core == 1)
    def _():
        fresh_wait(8).wait_send()

    fresh_planes().wait_send()
    sib_fresh(core).wait_send()
    for store in stores:
        store.wait()


def hand_over(result, rows, out, tail, sems):
    copies = [
        pltpu.make_async_copy(result, out, sems.at[0]),
        pltpu.make_async_copy(rows, tail, sems.at[1]),
    ]
    for copy in copies:
        copy.start()
    for copy in copies:
        copy.wait()


def per_device(kv_pool, queries, new_kv, lengths, block_dev, block_slot, owner_dev, owner_row):
    anywhere = pl.BlockSpec(memory_space=pltpu.HBM)
    dma = pltpu.SemaphoreType.DMA
    result, tail = pl.pallas_call(
        kernel,
        out_shape=(
            jax.ShapeDtypeStruct((2, 8, 256), BF16),
            jax.ShapeDtypeStruct((4, 2048), BF16),
        ),
        in_specs=[anywhere] * 8,
        out_specs=(anywhere, anywhere),
        scratch_shapes=[
            pltpu.VMEM((2, 8, 256), BF16),
            pltpu.VMEM((2, 8, 64), BF16),
            pltpu.VMEM((REQS, 128), I32),
            pltpu.VMEM((REQS, 128), I32),
            pltpu.VMEM((2, REQS), I32),
            pltpu.VMEM((2, REQS), I32),
            pltpu.SMEM((REQS,), I32),
            pltpu.VMEM((2, 8, 256), BF16),
            pltpu.VMEM((4, 2048), BF16),
            pltpu.SMEM((8, SLOTS), I32),
            pltpu.VMEM((SLOTS, 128, 2048), BF16),
            pltpu.VMEM((2, 4, 16, 32, 128), BF16),
            pltpu.VMEM((2, 8, 128), F32),
            pltpu.VMEM((16, 128), BF16),
            pltpu.VMEM((4, 2, 8, 16, 128), BF16),
            pltpu.VMEM((2, 4, 128, 128), F32),
            pltpu.VMEM((2, 4, 128, 128), F32),
            pltpu.VMEM((SLOTS, 32, 128), BF16),
            pltpu.VMEM((SLOTS, 32, 128), F32),
            pltpu.VMEM((SLOTS, 32, 128), F32),
            pltpu.VMEM((SLOTS, 32, 128), F32),
            pltpu.VMEM((4, 2, 32, 128), F32),
            pltpu.VMEM((4, 2, 32, 128), F32),
            pltpu.VMEM((64, 128), F32),
            pltpu.VMEM((32, 128), F32),
            pltpu.VMEM((32, 128), F32),
            pltpu.VMEM((4, 2, 4, 128, 128), F32),
            pltpu.VMEM((4, 4, 128, 128), F32),
            pltpu.VMEM((4, 16, 32, 128), BF16),
            pltpu.VMEM((4, 16, 32, 128), BF16),
            pltpu.VMEM((4, 16, 1, 128), F32),
            pltpu.VMEM((4, 16, 1, 128), F32),
            pltpu.VMEM((64, 128), F32),
            pltpu.VMEM((40, 128), I32),
            pltpu.SMEM((40, 128), I32),
            pltpu.VMEM((40, 128), I32),
            dma((KV_PARTS,)),
            dma((KV_PARTS,)),
            dma((5,)),
            dma((5,)),
            dma((4,)),
            dma((4,)),
            dma((8,)),
            dma((4,)),
            dma((4,)),
            dma((4,)),
            dma((4,)),
            dma((2, 4)),
            dma((2, 4)),
            dma,
            dma((7,)),
        ],
        compiler_params=pltpu.CompilerParams(
            collective_id=0, has_side_effects=True, vmem_limit_bytes=56 * 1024 * 1024
        ),
    )(kv_pool, queries, new_kv, block_dev, block_slot, owner_dev, owner_row, lengths)
    return pl.pallas_call(
        hand_over,
        out_shape=(
            jax.ShapeDtypeStruct((2, 8, 256), BF16),
            jax.ShapeDtypeStruct((4, 2048), BF16),
        ),
        in_specs=[anywhere] * 2,
        out_specs=(anywhere, anywhere),
        scratch_shapes=[dma((2,))],
    )(result, tail)


def solution(mesh):
    placed = (
        P(("inst", "seq"), None, None),
        P(None, "inst", "seq"),
        P(None, "inst", "seq"),
        P(),
        P(),
        P(),
        P(),
        P(),
    )
    return jax.shard_map(
        per_device,
        mesh=mesh,
        in_specs=placed,
        out_specs=(P(None, "inst", "seq"), P(("inst", "seq"), None)),
        check_vma=False,
    )
```

```python
import math

import jax
import jax.numpy as jnp
from jax import lax
from jax.experimental import pallas as pl
from jax.experimental.pallas import tpu as pltpu
from jax.sharding import PartitionSpec as P

MESH = pl.DeviceIdType.MESH
F32 = jnp.float32
BF16 = jnp.bfloat16
I32 = jnp.int32

N = 4
CHIPS = 64
SLOTS = 32
REQS = 32
LOW = -1e30
SCALE = 1.0 / math.sqrt(128)
UNROLL = 4
GROUP = 32
SHIFT = (0, 2, 1, 3)
PLACES = (10, 9, 11, 6, 14, 2, 8, 5, 7, 13, 15, 1, 3, 4, 12)
KV_PARTS = SLOTS // UNROLL


def iota(shape, dim):
    return lax.broadcasted_iota(I32, shape, dim)


def halves(first, second, late):
    lane = iota(first.shape, 1)
    if late is True:
        return jnp.where(lane < 64, pltpu.roll(first, 64, 1), second)
    if late is False:
        return jnp.where(lane < 64, first, pltpu.roll(second, 64, 1))
    low = jnp.where(late, pltpu.roll(first, 64, 1), first)
    high = jnp.where(late, second, pltpu.roll(second, 64, 1))
    return jnp.where(lane < 64, low, high)


def kernel(
    kv, q_in, nk_in, dev_in, slot_in, own_dev_in, own_row_in, lens_in, out_at, tail_at,
    q, nk, dev, slot, own_dev, own_row, lens, out, tail,
    info, kvb, gat, nx, tile, gnt, gq, gn, wb, pk, dn, cb, mx, mxr, mt, lift, uw, s32, r32, sb, rb, ss, rs, tl, meta, smeta, codes,
    k_sem, v_sem, sg, rg, s_sib, r_sib, n_sems, s_m, r_m, s_chunk, r_chunk, b_sems, e_sems, meta_sem, io_sem,
):
    z = lax.axis_index("inst")
    c = lax.axis_index("seq")
    y, x, core = c >> 3, (c >> 1) & 3, c & 1
    zs, ys, xs = [[(v + d) & 3 for d in range(4)] for v in (z, y, x)]
    me = z * 32 + c
    chip = z * 16 + y * 4 + x
    sib = 1 - core
    sibling = (z, y * 8 + x * 2 + sib)

    def place(pz, py, px):
        return (pz, py * 8 + px * 2 + core)

    loads = [
        pltpu.make_async_copy(src, dst, io_sem.at[k])
        for k, (src, dst) in enumerate([
            (q_in, q), (nk_in, nk), (dev_in, dev), (slot_in, slot),
            (own_dev_in, own_dev), (own_row_in, own_row), (lens_in, lens),
        ])
    ]
    for load in loads[:2]:
        load.start()

    def beside(e, py):
        return zs[e // 4], py, xs[e % 4]

    barrier = pltpu.get_barrier_semaphore()

    for e in PLACES:
        pl.semaphore_signal(barrier, inc=1, device_id=place(*beside(e, y)), device_id_type=MESH)
    for m in range(1, 4):
        pl.semaphore_signal(barrier, inc=1, device_id=place(z, ys[m], x), device_id_type=MESH)
    pl.semaphore_signal(barrier, inc=1, device_id=sibling, device_id_type=MESH)
    for load in loads[2:]:
        load.start()

    def key_copy(part):
        span = pl.ds(part * UNROLL, UNROLL)
        cols = pl.ds(0, 1024)
        return pltpu.make_async_copy(kv.at[span, :, cols], kvb.at[span, :, cols], k_sem.at[part])

    def value_copy(part):
        span = pl.ds(part * UNROLL, UNROLL)
        cols = pl.ds(1024, 1024)
        return pltpu.make_async_copy(kv.at[span, :, cols], kvb.at[span, :, cols], v_sem.at[part])

    spot = z * 4 + x
    for load in loads[:2]:
        load.wait()
    own = [q[s].astype(F32) for s in range(2)]
    gat[core, y, spot] = jnp.concatenate(
        [own[0][:, :128], own[0][:, 128:], own[1][:, :128], own[1][:, 128:]], axis=0
    ).astype(BF16)
    nx[0] = jnp.concatenate([nk[0].astype(F32), nk[1].astype(F32)], axis=1)

    pl.semaphore_wait(barrier, 19)

    def turn(k):
        return (y + ((k & 1) << 1) + (k >> 1)) & 3

    def push(block, k, to):
        return pltpu.make_async_remote_copy(
            src_ref=block, dst_ref=block, send_sem=sg.at[k], recv_sem=rg.at[k],
            device_id=to, device_id_type=MESH,
        )

    def plane_copy(e):
        return push(gat.at[core, y, spot], 0, place(*beside(e, y)))

    def across_copy():
        return push(gat.at[core, y, spot], 4, place(z, ys[2], x))

    def relay_copy(e):
        return push(gat.at[core, ys[2], spot], 1, place(*beside(e, y)))

    def next_copy(m):
        return push(gat.at[core, y], 2 if m == 3 else 3, place(z, ys[m], x))

    def arrived(k, plane, blocks):
        return push(gat.at[core, plane, pl.ds(0, blocks)], k, sibling)

    def sib_copy(k, of):
        block = gat.at[of, turn(k)]
        return pltpu.make_async_remote_copy(
            src_ref=block, dst_ref=block, send_sem=s_sib.at[k], recv_sem=r_sib.at[k],
            device_id=sibling, device_id_type=MESH,
        )

    across_copy().start()

    for e in PLACES:
        plane_copy(e).start()

    @pl.loop(0, KV_PARTS)
    def _(part):
        key_copy(part).start()

    pair_rows = pltpu.make_async_remote_copy(
        src_ref=nx.at[0], dst_ref=nx.at[1], send_sem=n_sems.at[0], recv_sem=n_sems.at[1],
        device_id=sibling, device_id_type=MESH,
    )
    pair_rows.start()
    shelf = z * 2 + (x >> 1)
    side_of = (x + core) & 1

    def fresh_copy(e):
        return pltpu.make_async_remote_copy(
            src_ref=tile, dst_ref=gnt.at[y, x & 1, shelf], send_sem=n_sems.at[2], recv_sem=n_sems.at[3],
            device_id=place(*beside(e, y)), device_id_type=MESH,
        )

    def fresh_wait(tiles):
        block = gnt.at[y, side_of, pl.ds(0, tiles)]
        return pltpu.make_async_remote_copy(
            src_ref=block, dst_ref=block, send_sem=n_sems.at[2], recv_sem=n_sems.at[3],
            device_id=sibling, device_id_type=MESH,
        )

    def fresh_plane(m):
        block = gnt.at[y, side_of]
        return pltpu.make_async_remote_copy(
            src_ref=block, dst_ref=block, send_sem=n_sems.at[4], recv_sem=n_sems.at[5],
            device_id=place(z, ys[m], x), device_id_type=MESH,
        )

    def fresh_planes():
        block = gnt.at[pl.ds(0, 3), side_of]
        return pltpu.make_async_remote_copy(
            src_ref=block, dst_ref=block, send_sem=n_sems.at[4], recv_sem=n_sems.at[5],
            device_id=sibling, device_id_type=MESH,
        )

    def sib_fresh(of):
        block = gnt.at[:, (x + of) & 1]
        return pltpu.make_async_remote_copy(
            src_ref=block, dst_ref=block, send_sem=n_sems.at[6], recv_sem=n_sems.at[7],
            device_id=sibling, device_id_type=MESH,
        )

    @pl.loop(0, KV_PARTS)
    def _(part):
        value_copy(part).start()

    for load in loads[2:]:
        load.wait()
    mine = jnp.where(dev[...] == me, slot[...], -1)
    code = iota((REQS, 128), 0) * 128 + iota((REQS, 128), 1) + 1

    @pl.loop(0, SLOTS // 4)
    def _(group):
        for e in range(4):
            n = group * 4 + e
            codes[pl.ds(n, 1), :] = jnp.sum(jnp.where(mine == n, code, 0), axis=0, keepdims=True)

    owned = jnp.where(own_dev[...] == me, own_row[...], -1)
    row_code = iota((2, REQS), 0) * REQS + iota((2, REQS), 1) + 1
    pad_row = jnp.zeros((1, 96), I32)
    for e in range(4):
        hit = jnp.sum(jnp.where(owned == e, row_code, 0), axis=0, keepdims=True)
        codes[SLOTS + e : SLOTS + e + 1, :] = jnp.concatenate([hit, pad_row], axis=1)
    codes[SLOTS + 4 :, :] = jnp.zeros((4, 128), I32)

    found = jnp.broadcast_to(jnp.sum(codes[...], axis=1, keepdims=True), (40, 128))
    held = found[:SLOTS]
    req_col = jnp.where(held > 0, jnp.minimum((held - 1) >> 7, REQS - 1), -1)
    rows, lanes = iota((SLOTS, 128), 0), iota((SLOTS, 128), 1)
    req_row = jnp.sum(jnp.where(rows == lanes, req_col, 0), axis=0, keepdims=True)
    req_row = jnp.where(lanes < SLOTS, jnp.broadcast_to(req_row, (SLOTS, 128)), -2)
    before = jnp.max(jnp.where((req_row == req_col) & (lanes < rows), lanes, -1), axis=1, keepdims=True)
    last = jnp.max(jnp.where(req_row == rows, lanes, -1), axis=1, keepdims=True)
    meta[:SLOTS] = jnp.where(
        lanes == 0, req_col, jnp.where(lanes == 1, held, jnp.where(lanes == 2, before, last))
    )
    meta[SLOTS:] = found[SLOTS:]
    meta_copy = pltpu.make_async_copy(meta, smeta, meta_sem)
    meta_copy.start()

    pair_rows.wait_recv()
    both_rows = [jnp.where(core == of, nx[0], nx[1]) for of in range(2)]
    tile[...] = jnp.concatenate(both_rows, axis=0).astype(BF16)

    @pl.when(core == 0)
    def _():
        gnt[y, x & 1, shelf] = tile[...]

    push(gat.at[core, ys[2], spot], 4, sibling).wait_recv()

    for e in PLACES:
        relay_copy(e).start()

    arrived(0, y, 15).wait_recv()
    sib_copy(0, core).start()
    for m in (3, 1):
        next_copy(m).start()

    for of in range(2):
        @pl.when(core == of)
        def _():
            for e in range(2 - of, 16, 2):
                fresh_copy(e).start()

    meta_copy.wait()

    @pl.loop(0, SLOTS)
    def _(n):
        req, held, prev, end = smeta[n, 0], smeta[n, 1], smeta[n, 2], smeta[n, 3]
        r = jnp.maximum(req, 0)
        b = (jnp.maximum(held, 1) - 1) & 127
        info[0, n] = req
        info[1, n] = r >> 3
        info[2, n] = r & 7
        info[3, n] = jnp.where(held > 0, lens[r] - b * 128, 0)
        info[4, n] = prev
        info[5, n] = jnp.maximum(prev, 0)
        info[6, n] = end
        info[7, n] = jnp.maximum(end, 0)


    @pl.loop(0, KV_PARTS)
    def _(part):
        key_copy(part).wait()

    lanes = iota((32, 128), 1)
    blank = jnp.zeros((16, 128), BF16)

    def chunk_copy(k):
        return pltpu.make_async_remote_copy(
            src_ref=s32.at[k, sib], dst_ref=r32.at[k],
            send_sem=s_chunk.at[k], recv_sem=r_chunk.at[k], device_id=sibling, device_id_type=MESH,
        )

    def peak_copy(k):
        return pltpu.make_async_remote_copy(
            src_ref=mx.at[k], dst_ref=mxr.at[k], send_sem=s_m.at[k], recv_sem=r_m.at[k],
            device_id=sibling, device_id_type=MESH,
        )

    def block_copy(k, at, to):
        return pltpu.make_async_remote_copy(
            src_ref=sb.at[turn(k), at], dst_ref=rb.at[y, spot], send_sem=b_sems.at[0, k], recv_sem=b_sems.at[1, k],
            device_id=to, device_id_type=MESH,
        )

    def side_copy(k, at, to):
        return pltpu.make_async_remote_copy(
            src_ref=ss.at[turn(k), at], dst_ref=rs.at[y, spot], send_sem=e_sems.at[0, k], recv_sem=e_sems.at[1, k],
            device_id=to, device_id_type=MESH,
        )

    def all_copy(buf, sems, k):
        block = buf.at[ys[(4 - SHIFT[k]) % 4], pl.ds(0, 16 if k else 15)]
        return pltpu.make_async_remote_copy(
            src_ref=block, dst_ref=block, send_sem=sems.at[0, k], recv_sem=sems.at[1, k],
            device_id=sibling, device_id_type=MESH,
        )

    def scores(k):
        cols = pl.ds(pl.multiple_of(turn(k) * 256, 256), 256)

        @pl.loop(0, SLOTS // GROUP, init_carry=jnp.full((32, 128), LOW, F32))
        def most(group, most):
            for e in range(GROUP):
                n = group * GROUP + e
                i, rl, count = info[1, n], info[2, n], info[3, n]
                parts = [gq[of, i, pl.ds(rl, 16, stride=8), :].reshape(2, 8, 128) for of in range(2)]
                heads = jnp.concatenate(parts, axis=1).astype(BF16)
                first = jnp.concatenate([heads[0], blank], axis=1)
                second = jnp.concatenate([blank, heads[1]], axis=1)
                score = lax.dot_general(
                    jnp.concatenate([first, second], axis=0), kvb[n, :, cols],
                    (((1,), (1,)), ((), ())), preferred_element_type=F32,
                )
                score = jnp.where(lanes < count, score * SCALE, LOW)
                peak = jnp.max(score, axis=1, keepdims=True)
                wb[n] = jnp.exp(score - peak).astype(BF16)
                pk[n] = jnp.broadcast_to(peak, (32, 128))
                most = jnp.where(lanes == info[0, n], jnp.maximum(most, peak), most)
            return most

        return most

    def values(k, most):
        cols = pl.ds(pl.multiple_of(1024 + turn(k) * 256, 256), 256)
        dn[...] = jnp.dot(
            wb[...].reshape(SLOTS * 32, 128), jnp.ones((128, 128), BF16), preferred_element_type=F32
        ).reshape(SLOTS, 32, 128)

        @pl.loop(0, SLOTS // GROUP, init_carry=jnp.zeros((32, 128), F32))
        def den(group, den):
            for e in range(GROUP):
                n = group * GROUP + e
                r = info[0, n]
                best = jnp.max(jnp.where(lanes == r, most, LOW), axis=1, keepdims=True)
                factor = jnp.exp(pk[n] - best)
                both = jnp.dot(wb[n], kvb[n, :, cols], preferred_element_type=F32)
                num = jnp.concatenate([both[:16, :128], both[16:, 128:]], axis=0)
                earlier = jnp.where(info[4, n] >= 0, cb[info[5, n]], 0.0)
                cb[n] = num * factor + earlier
                den = den + jnp.where(lanes == r, factor * dn[n], 0.0)
            return den

        mx[k, 0] = most
        mx[k, 1] = den
        peak_copy(k).start()

    def hand_on(k):
        for i in range(4):
            for rl in range(8):
                sums = jnp.where(info[6, i * 8 + rl] >= 0, cb[info[7, i * 8 + rl]], 0.0)
                for xh in range(2):
                    for of in range(2):
                        at = pl.ds(xh * 64 + rl, 8, stride=8)
                        s32[k, of, i, at, :] = sums[xh * 16 + of * 8 : xh * 16 + of * 8 + 8]

        chunk_copy(k).start()

    def merge(k):
        kt = turn(k)
        peak_copy(k).wait_recv()
        top, other = mx[k, 0], mxr[k, 0]
        chip_top = jnp.maximum(top, other)
        mine_f, other_f = jnp.exp(top - chip_top), jnp.exp(other - chip_top)
        chip_den = mx[k, 1] * mine_f + mxr[k, 1] * other_f
        mt[0:32, :] = chip_top
        mt[32:64, :] = chip_den
        for w in range(2):
            for xh in range(2):
                row = pl.multiple_of(w * 32 + xh * 16 + core * 8, 8)
                uw[w * 16 + xh * 8 : w * 16 + xh * 8 + 8, :] = mt[pl.ds(row, 8), :]
        lane4 = iota((4, 128), 1)
        packed = [jnp.zeros((4, 128), F32) for _ in range(4)]
        for w in range(2):
            for t in range(4):
                got = uw[pl.ds(w * 16 + t, 4, stride=4), :]
                to = w * 32 + t * 8
                for i in range(4):
                    there = pltpu.roll(got, (to - 8 * i) % 128, 1)
                    packed[i] = jnp.where((lane4 >= to) & (lane4 < to + 8), there, packed[i])
        for i in range(4):
            for j in range(4):
                ss[kt, i * 4 + j] = packed[i][j : j + 1, :]
        both_f = jnp.concatenate([mine_f, other_f, jnp.zeros((64, 128), F32)], axis=0).T
        lift[...] = pltpu.roll(both_f[0:32], (128 - core * 8) % 128, 1)
        chunk_copy(k).wait_recv()

        for i in range(4):
            factors = lift[i * 8 : i * 8 + 8, :]
            for j in range(4):
                total = []
                for t in range(4):
                    lane = (j // 2) * 16 + (j % 2) * 4 + t
                    at = slice(j * 32 + t * 8, j * 32 + t * 8 + 8)
                    total.append(
                        s32[k, core, i, at, :] * factors[:, lane : lane + 1]
                        + r32[k, i, at, :] * factors[:, 32 + lane : 33 + lane]
                    )
                sb[kt, i * 4 + j] = jnp.concatenate(total, axis=0).astype(BF16)

    def send(k):
        kt = turn(k)

        def one(e):
            pz, _, px = beside(e, kt)
            at, to = pz * 4 + px, place(pz, kt, px)
            block_copy(k, at, to).start()
            side_copy(k, at, to).start()

        for e in PLACES:
            one(e)

        @pl.when(k > 0)
        def _():
            one(0)

    def spread_fresh():
        @pl.when(core == 0)
        def _():
            fresh_wait(7).wait_recv()

        @pl.when(core == 1)
        def _():
            fresh_wait(8).wait_recv()

        for m in range(1, 4):
            fresh_plane(m).start()

    def pass_fresh():
        fresh_planes().wait_recv()
        sib_fresh(core).start()

    @pl.loop(0, 5)
    def _(k):
        @pl.when(k < 4)
        def _():
            sib_copy(k, sib).wait_recv()

            kt = turn(k)
            for of in range(2):
                for i in range(4):
                    for j in range(4):
                        gq[of, i, j * 32 : j * 32 + 32, :] = gat[of, kt, i * 4 + j].astype(F32)

            most = scores(k)

            @pl.when(k == 0)
            def _():
                arrived(1, ys[2], 15).wait_recv()
                sib_copy(1, core).start()

            @pl.when(k == 1)
            def _():
                for phase in (2, 3):
                    arrived(phase, ys[SHIFT[phase]], 16).wait_recv()
                    sib_copy(phase, core).start()

            @pl.when(k == 0)
            def _():
                @pl.loop(0, KV_PARTS)
                def _(part):
                    value_copy(part).wait()

            values(k, most)
            hand_on(k)

        @pl.when(k > 0)
        def _():
            merge(k - 1)
            send(k - 1)

        @pl.when(k == 1)
        def _():
            spread_fresh()

        @pl.when(k == 3)
        def _():
            pass_fresh()

    rb[y, spot] = sb[y, spot]
    rs[y, spot] = ss[y, spot]

    sib_fresh(sib).wait_recv()

    @pl.loop(0, 4)
    def _(i):
        for j in range(16):
            fresh = gnt[j // 4, j % 2, i * 2 + (j % 4) // 2].astype(F32)
            for of in range(2):
                gn[of, i, j * 8 : j * 8 + 8, :] = fresh[of * 8 : of * 8 + 8]

    @pl.loop(0, 4)
    def _(e):
        found_row = smeta[SLOTS + e, 0]
        which = jnp.maximum(found_row - 1, 0)
        late, r = which >> 5, which & 31
        pair = [gn[of, r >> 3, pl.ds(r & 7, 16, stride=8), :] for of in range(2)]
        tl[pl.ds(pl.multiple_of(e * 16, 16), 16), :] = jnp.where(found_row > 0, halves(pair[0], pair[1], late > 0), 0.0)
    for j in range(16):
        tail[:, j * 128 : j * 128 + 128] = tl[pl.ds(j, 4, stride=16), :].astype(BF16)

    head = y * 2 + x // 2
    new_rows = []
    for at in (head, head + 8):
        pair = [gn[of, z, pl.ds(pl.multiple_of(at * 8, 8), 8), :] for of in range(2)]
        new_rows.append([halves(pair[0], pair[1], late) for late in (False, True)])
    new_m, new_den, new_num = [], [], []
    for t in range(4):
        mine_q = q[t // 2].astype(F32)[:, (t % 2) * 128 : (t % 2) * 128 + 128]
        found_scores = [
            jnp.sum(mine_q * new_rows[0][j], axis=1, keepdims=True) * SCALE for j in range(t // 2 + 1)
        ]
        peak = found_scores[0]
        for more in found_scores[1:]:
            peak = jnp.maximum(peak, more)
        ws = [jnp.exp(v - peak).astype(BF16).astype(F32) for v in found_scores]
        new_m.append(peak)
        new_den.append(sum(ws[1:], ws[0]))
        num = ws[0] * new_rows[1][0]
        for j in range(1, len(ws)):
            num = num + ws[j] * new_rows[1][j]
        new_num.append(num)
    new_m = jnp.concatenate(new_m, axis=0)
    new_den = jnp.concatenate(new_den, axis=0)
    new_num = jnp.concatenate(new_num, axis=0)

    def take_in(phases, top, den, total):
        planes = [ys[(4 - SHIFT[k]) % 4] for k in phases]
        count = 16 * len(phases)
        for k in phases:
            all_copy(rs, e_sems, k).wait_recv()
        side = [rs[plane].reshape(16, 128) for plane in planes]
        side = jnp.concatenate(side + [jnp.zeros((128 - count, 128), F32)], axis=0).T
        side_m, side_den = side[0:32, :count], side[32:64, :count]
        new_top = jnp.maximum(jnp.max(side_m, axis=1, keepdims=True), top)
        scales = jnp.exp(side_m - new_top)
        old_scale = jnp.exp(top - new_top)
        den = jnp.sum(scales * side_den, axis=1, keepdims=True) + den * old_scale
        total = total * old_scale
        for k, plane in enumerate(planes):
            all_copy(rb, b_sems, phases[k]).wait_recv()
            for e in range(16):
                total = total + scales[:, k * 16 + e : k * 16 + e + 1] * rb[plane, e].astype(F32)
        return new_top, den, total

    state = take_in((0, 1, 2), new_m, new_den, new_num)
    _, final_den, total = take_in((3,), *state)
    result = total / final_den
    for t in range(4):
        out[t // 2, :, (t % 2) * 128 : (t % 2) * 128 + 128] = result[t * 8 : t * 8 + 8].astype(BF16)

    stores = [
        pltpu.make_async_copy(src, dst, io_sem.at[k])
        for k, (src, dst) in enumerate([(out, out_at), (tail, tail_at)])
    ]
    for store in stores:
        store.start()

    for k in range(4):
        all_copy(sb, b_sems, k).wait_send()
        all_copy(ss, e_sems, k).wait_send()
    across_copy().wait_send()
    arrived(0, y, 15).wait_send()
    arrived(1, y, 15).wait_send()
    for m in (3, 1):
        next_copy(m).wait_send()
    for k in range(4):
        sib_copy(k, core).wait_send()
        peak_copy(k).wait_send()
        chunk_copy(k).wait_send()
    pair_rows.wait_send()

    @pl.when(core == 0)
    def _():
        fresh_wait(7).wait_send()

    @pl.when(core == 1)
    def _():
        fresh_wait(8).wait_send()

    fresh_planes().wait_send()
    sib_fresh(core).wait_send()
    for store in stores:
        store.wait()


def hand_over(result, rows, out, tail, sems):
    copies = [
        pltpu.make_async_copy(result, out, sems.at[0]),
        pltpu.make_async_copy(rows, tail, sems.at[1]),
    ]
    for copy in copies:
        copy.start()
    for copy in copies:
        copy.wait()


def per_device(kv_pool, queries, new_kv, lengths, block_dev, block_slot, owner_dev, owner_row):
    anywhere = pl.BlockSpec(memory_space=pltpu.HBM)
    dma = pltpu.SemaphoreType.DMA
    result, tail = pl.pallas_call(
        kernel,
        out_shape=(
            jax.ShapeDtypeStruct((2, 8, 256), BF16),
            jax.ShapeDtypeStruct((4, 2048), BF16),
        ),
        in_specs=[anywhere] * 8,
        out_specs=(anywhere, anywhere),
        scratch_shapes=[
            pltpu.VMEM((2, 8, 256), BF16),
            pltpu.VMEM((2, 8, 64), BF16),
            pltpu.VMEM((REQS, 128), I32),
            pltpu.VMEM((REQS, 128), I32),
            pltpu.VMEM((2, REQS), I32),
            pltpu.VMEM((2, REQS), I32),
            pltpu.SMEM((REQS,), I32),
            pltpu.VMEM((2, 8, 256), BF16),
            pltpu.VMEM((4, 2048), BF16),
            pltpu.SMEM((8, SLOTS), I32),
            pltpu.VMEM((SLOTS, 128, 2048), BF16),
            pltpu.VMEM((2, 4, 16, 32, 128), BF16),
            pltpu.VMEM((2, 8, 128), F32),
            pltpu.VMEM((16, 128), BF16),
            pltpu.VMEM((4, 2, 8, 16, 128), BF16),
            pltpu.VMEM((2, 4, 128, 128), F32),
            pltpu.VMEM((2, 4, 128, 128), F32),
            pltpu.VMEM((SLOTS, 32, 128), BF16),
            pltpu.VMEM((SLOTS, 32, 128), F32),
            pltpu.VMEM((SLOTS, 32, 128), F32),
            pltpu.VMEM((SLOTS, 32, 128), F32),
            pltpu.VMEM((4, 2, 32, 128), F32),
            pltpu.VMEM((4, 2, 32, 128), F32),
            pltpu.VMEM((64, 128), F32),
            pltpu.VMEM((32, 128), F32),
            pltpu.VMEM((32, 128), F32),
            pltpu.VMEM((4, 2, 4, 128, 128), F32),
            pltpu.VMEM((4, 4, 128, 128), F32),
            pltpu.VMEM((4, 16, 32, 128), BF16),
            pltpu.VMEM((4, 16, 32, 128), BF16),
            pltpu.VMEM((4, 16, 1, 128), F32),
            pltpu.VMEM((4, 16, 1, 128), F32),
            pltpu.VMEM((64, 128), F32),
            pltpu.VMEM((40, 128), I32),
            pltpu.SMEM((40, 128), I32),
            pltpu.VMEM((40, 128), I32),
            dma((KV_PARTS,)),
            dma((KV_PARTS,)),
            dma((5,)),
            dma((5,)),
            dma((4,)),
            dma((4,)),
            dma((8,)),
            dma((4,)),
            dma((4,)),
            dma((4,)),
            dma((4,)),
            dma((2, 4)),
            dma((2, 4)),
            dma,
            dma((7,)),
        ],
        compiler_params=pltpu.CompilerParams(
            collective_id=0, has_side_effects=True, vmem_limit_bytes=56 * 1024 * 1024
        ),
    )(kv_pool, queries, new_kv, block_dev, block_slot, owner_dev, owner_row, lengths)
    return pl.pallas_call(
        hand_over,
        out_shape=(
            jax.ShapeDtypeStruct((2, 8, 256), BF16),
            jax.ShapeDtypeStruct((4, 2048), BF16),
        ),
        in_specs=[anywhere] * 2,
        out_specs=(anywhere, anywhere),
        scratch_shapes=[dma((2,))],
    )(result, tail)


def solution(mesh):
    placed = (
        P(("inst", "seq"), None, None),
        P(None, "inst", "seq"),
        P(None, "inst", "seq"),
        P(),
        P(),
        P(),
        P(),
        P(),
    )
    return jax.shard_map(
        per_device,
        mesh=mesh,
        in_specs=placed,
        out_specs=(P(None, "inst", "seq"), P(("inst", "seq"), None)),
        check_vma=False,
    )
```

```python
import math

import jax
import jax.numpy as jnp
from jax import lax
from jax.experimental import pallas as pl
from jax.experimental.pallas import tpu as pltpu
from jax.sharding import PartitionSpec as P

MESH = pl.DeviceIdType.MESH
F32 = jnp.float32
BF16 = jnp.bfloat16
I32 = jnp.int32

N = 4
CHIPS = 64
SLOTS = 32
REQS = 32
LOW = -1e30
SCALE = 1.0 / math.sqrt(128)
UNROLL = 4
GROUP = 32
SHIFT = (0, 2, 1, 3)
PLACES = (10, 9, 11, 6, 14, 2, 8, 5, 7, 13, 15, 1, 3, 4, 12)
KV_PARTS = SLOTS // UNROLL


def iota(shape, dim):
    return lax.broadcasted_iota(I32, shape, dim)


def halves(first, second, late):
    lane = iota(first.shape, 1)
    if late is True:
        return jnp.where(lane < 64, pltpu.roll(first, 64, 1), second)
    if late is False:
        return jnp.where(lane < 64, first, pltpu.roll(second, 64, 1))
    low = jnp.where(late, pltpu.roll(first, 64, 1), first)
    high = jnp.where(late, second, pltpu.roll(second, 64, 1))
    return jnp.where(lane < 64, low, high)


def kernel(
    kv, q_in, nk_in, dev_in, slot_in, own_dev_in, own_row_in, lens_in, out_at, tail_at,
    q, nk, dev, slot, own_dev, own_row, lens, out, tail,
    info, kvb, gat, nx, tile, gnt, gq, gn, wb, pk, dn, cb, cb2, mx, mxr, mt, lift, uw, s32, r32, sb, rb, ss, rs, tl, meta, smeta, codes,
    k_sem, v_sem, sg, rg, s_sib, r_sib, n_sems, s_m, r_m, s_chunk, r_chunk, b_sems, e_sems, meta_sem, io_sem,
):
    z = lax.axis_index("inst")
    c = lax.axis_index("seq")
    y, x, core = c >> 3, (c >> 1) & 3, c & 1
    zs, ys, xs = [[(v + d) & 3 for d in range(4)] for v in (z, y, x)]
    me = z * 32 + c
    chip = z * 16 + y * 4 + x
    sib = 1 - core
    sibling = (z, y * 8 + x * 2 + sib)

    def place(pz, py, px):
        return (pz, py * 8 + px * 2 + core)

    loads = [
        pltpu.make_async_copy(src, dst, io_sem.at[k])
        for k, (src, dst) in enumerate([
            (q_in, q), (nk_in, nk), (dev_in, dev), (slot_in, slot),
            (own_dev_in, own_dev), (own_row_in, own_row), (lens_in, lens),
        ])
    ]
    for load in loads[:2]:
        load.start()

    def beside(e, py):
        return zs[e // 4], py, xs[e % 4]

    barrier = pltpu.get_barrier_semaphore()

    for e in PLACES:
        pl.semaphore_signal(barrier, inc=1, device_id=place(*beside(e, y)), device_id_type=MESH)
    for m in range(1, 4):
        pl.semaphore_signal(barrier, inc=1, device_id=place(z, ys[m], x), device_id_type=MESH)
    pl.semaphore_signal(barrier, inc=1, device_id=sibling, device_id_type=MESH)
    for load in loads[2:]:
        load.start()

    def key_copy(part):
        span = pl.ds(part * UNROLL, UNROLL)
        cols = pl.ds(0, 1024)
        return pltpu.make_async_copy(kv.at[span, :, cols], kvb.at[span, :, cols], k_sem.at[part])

    def value_copy(part):
        span = pl.ds(part * UNROLL, UNROLL)
        cols = pl.ds(1024, 1024)
        return pltpu.make_async_copy(kv.at[span, :, cols], kvb.at[span, :, cols], v_sem.at[part])

    spot = z * 4 + x
    for load in loads[:2]:
        load.wait()
    own = [q[s].astype(F32) for s in range(2)]
    gat[core, y, spot] = jnp.concatenate(
        [own[0][:, :128], own[0][:, 128:], own[1][:, :128], own[1][:, 128:]], axis=0
    ).astype(BF16)
    nx[0] = jnp.concatenate([nk[0].astype(F32), nk[1].astype(F32)], axis=1)

    pl.semaphore_wait(barrier, 19)

    def turn(k):
        return (y + ((k & 1) << 1) + (k >> 1)) & 3

    def push(block, k, to):
        return pltpu.make_async_remote_copy(
            src_ref=block, dst_ref=block, send_sem=sg.at[k], recv_sem=rg.at[k],
            device_id=to, device_id_type=MESH,
        )

    def plane_copy(e):
        return push(gat.at[core, y, spot], 0, place(*beside(e, y)))

    def across_copy():
        return push(gat.at[core, y, spot], 4, place(z, ys[2], x))

    def relay_copy(e):
        return push(gat.at[core, ys[2], spot], 1, place(*beside(e, y)))

    def next_copy(m):
        return push(gat.at[core, y], 2 if m == 3 else 3, place(z, ys[m], x))

    def arrived(k, plane, blocks):
        return push(gat.at[core, plane, pl.ds(0, blocks)], k, sibling)

    def sib_copy(k, of):
        block = gat.at[of, turn(k)]
        return pltpu.make_async_remote_copy(
            src_ref=block, dst_ref=block, send_sem=s_sib.at[k], recv_sem=r_sib.at[k],
            device_id=sibling, device_id_type=MESH,
        )

    across_copy().start()

    for e in PLACES:
        plane_copy(e).start()

    @pl.loop(0, KV_PARTS)
    def _(part):
        key_copy(part).start()

    pair_rows = pltpu.make_async_remote_copy(
        src_ref=nx.at[0], dst_ref=nx.at[1], send_sem=n_sems.at[0], recv_sem=n_sems.at[1],
        device_id=sibling, device_id_type=MESH,
    )
    pair_rows.start()
    shelf = z * 2 + (x >> 1)
    side_of = (x + core) & 1

    def fresh_copy(e):
        return pltpu.make_async_remote_copy(
            src_ref=tile, dst_ref=gnt.at[y, x & 1, shelf], send_sem=n_sems.at[2], recv_sem=n_sems.at[3],
            device_id=place(*beside(e, y)), device_id_type=MESH,
        )

    def fresh_wait(tiles):
        block = gnt.at[y, side_of, pl.ds(0, tiles)]
        return pltpu.make_async_remote_copy(
            src_ref=block, dst_ref=block, send_sem=n_sems.at[2], recv_sem=n_sems.at[3],
            device_id=sibling, device_id_type=MESH,
        )

    def fresh_plane(m):
        block = gnt.at[y, side_of]
        return pltpu.make_async_remote_copy(
            src_ref=block, dst_ref=block, send_sem=n_sems.at[4], recv_sem=n_sems.at[5],
            device_id=place(z, ys[m], x), device_id_type=MESH,
        )

    def fresh_planes():
        block = gnt.at[pl.ds(0, 3), side_of]
        return pltpu.make_async_remote_copy(
            src_ref=block, dst_ref=block, send_sem=n_sems.at[4], recv_sem=n_sems.at[5],
            device_id=sibling, device_id_type=MESH,
        )

    def sib_fresh(of):
        block = gnt.at[:, (x + of) & 1]
        return pltpu.make_async_remote_copy(
            src_ref=block, dst_ref=block, send_sem=n_sems.at[6], recv_sem=n_sems.at[7],
            device_id=sibling, device_id_type=MESH,
        )

    @pl.loop(0, KV_PARTS)
    def _(part):
        value_copy(part).start()

    for load in loads[2:]:
        load.wait()
    mine = jnp.where(dev[...] == me, slot[...], -1)
    code = iota((REQS, 128), 0) * 128 + iota((REQS, 128), 1) + 1

    @pl.loop(0, SLOTS // 4)
    def _(group):
        for e in range(4):
            n = group * 4 + e
            codes[pl.ds(n, 1), :] = jnp.sum(jnp.where(mine == n, code, 0), axis=0, keepdims=True)

    owned = jnp.where(own_dev[...] == me, own_row[...], -1)
    row_code = iota((2, REQS), 0) * REQS + iota((2, REQS), 1) + 1
    pad_row = jnp.zeros((1, 96), I32)
    for e in range(4):
        hit = jnp.sum(jnp.where(owned == e, row_code, 0), axis=0, keepdims=True)
        codes[SLOTS + e : SLOTS + e + 1, :] = jnp.concatenate([hit, pad_row], axis=1)
    codes[SLOTS + 4 :, :] = jnp.zeros((4, 128), I32)

    found = jnp.broadcast_to(jnp.sum(codes[...], axis=1, keepdims=True), (40, 128))
    held = found[:SLOTS]
    req_col = jnp.where(held > 0, jnp.minimum((held - 1) >> 7, REQS - 1), -1)
    rows, lanes = iota((SLOTS, 128), 0), iota((SLOTS, 128), 1)
    req_row = jnp.sum(jnp.where(rows == lanes, req_col, 0), axis=0, keepdims=True)
    req_row = jnp.where(lanes < SLOTS, jnp.broadcast_to(req_row, (SLOTS, 128)), -2)
    same_half = (lanes >> 4) == (rows >> 4)
    before = jnp.where((req_row == req_col) & (lanes < rows) & same_half, lanes, -1)
    before = jnp.max(before, axis=1, keepdims=True)
    low = jnp.max(jnp.where((req_row == rows) & (lanes < 16), lanes, -1), axis=1, keepdims=True)
    high = jnp.max(jnp.where((req_row == rows) & (lanes >= 16), lanes - 16, -1), axis=1, keepdims=True)
    meta[:SLOTS] = jnp.where(
        lanes == 0, req_col, jnp.where(lanes == 1, held, jnp.where(lanes == 2, before, jnp.where(lanes == 3, low, high)))
    )
    meta[SLOTS:] = found[SLOTS:]
    meta_copy = pltpu.make_async_copy(meta, smeta, meta_sem)
    meta_copy.start()

    pair_rows.wait_recv()
    both_rows = [jnp.where(core == of, nx[0], nx[1]) for of in range(2)]
    tile[...] = jnp.concatenate(both_rows, axis=0).astype(BF16)

    @pl.when(core == 0)
    def _():
        gnt[y, x & 1, shelf] = tile[...]

    push(gat.at[core, ys[2], spot], 4, sibling).wait_recv()

    for e in PLACES:
        relay_copy(e).start()

    arrived(0, y, 15).wait_recv()
    sib_copy(0, core).start()
    for m in (3, 1):
        next_copy(m).start()

    for of in range(2):
        @pl.when(core == of)
        def _():
            for e in range(2 - of, 16, 2):
                fresh_copy(e).start()

    meta_copy.wait()

    @pl.loop(0, SLOTS)
    def _(n):
        req, held, prev, low, high = [smeta[n, w] for w in range(5)]
        r = jnp.maximum(req, 0)
        b = (jnp.maximum(held, 1) - 1) & 127
        info[0, n] = req
        info[1, n] = r >> 3
        info[2, n] = r & 7
        info[3, n] = jnp.where(held > 0, lens[r] - b * 128, 0)
        info[4, n] = prev
        info[5, n] = jnp.maximum(prev, 0) & 15
        info[6, n] = low
        info[7, n] = jnp.maximum(low, 0)
        info[8, n] = high
        info[9, n] = jnp.maximum(high, 0)


    @pl.loop(0, KV_PARTS)
    def _(part):
        key_copy(part).wait()

    lanes = iota((32, 128), 1)
    blank = jnp.zeros((16, 128), BF16)

    def chunk_copy(k):
        return pltpu.make_async_remote_copy(
            src_ref=s32.at[k, sib], dst_ref=r32.at[k],
            send_sem=s_chunk.at[k], recv_sem=r_chunk.at[k], device_id=sibling, device_id_type=MESH,
        )

    def peak_copy(k):
        return pltpu.make_async_remote_copy(
            src_ref=mx.at[k], dst_ref=mxr.at[k], send_sem=s_m.at[k], recv_sem=r_m.at[k],
            device_id=sibling, device_id_type=MESH,
        )

    def block_copy(k, at, to):
        return pltpu.make_async_remote_copy(
            src_ref=sb.at[turn(k), at], dst_ref=rb.at[y, spot], send_sem=b_sems.at[0, k], recv_sem=b_sems.at[1, k],
            device_id=to, device_id_type=MESH,
        )

    def side_copy(k, at, to):
        return pltpu.make_async_remote_copy(
            src_ref=ss.at[turn(k), at], dst_ref=rs.at[y, spot], send_sem=e_sems.at[0, k], recv_sem=e_sems.at[1, k],
            device_id=to, device_id_type=MESH,
        )

    def all_copy(buf, sems, k):
        block = buf.at[ys[(4 - SHIFT[k]) % 4], pl.ds(0, 16 if k else 15)]
        return pltpu.make_async_remote_copy(
            src_ref=block, dst_ref=block, send_sem=sems.at[0, k], recv_sem=sems.at[1, k],
            device_id=sibling, device_id_type=MESH,
        )

    def scores(k):
        cols = pl.ds(pl.multiple_of(turn(k) * 256, 256), 256)

        @pl.loop(0, SLOTS // GROUP, init_carry=jnp.full((32, 128), LOW, F32))
        def most(group, most):
            for e in range(GROUP):
                n = group * GROUP + e
                i, rl, count = info[1, n], info[2, n], info[3, n]
                parts = [gq[of, i, pl.ds(rl, 16, stride=8), :].reshape(2, 8, 128) for of in range(2)]
                heads = jnp.concatenate(parts, axis=1).astype(BF16)
                first = jnp.concatenate([heads[0], blank], axis=1)
                second = jnp.concatenate([blank, heads[1]], axis=1)
                score = lax.dot_general(
                    jnp.concatenate([first, second], axis=0), kvb[n, :, cols],
                    (((1,), (1,)), ((), ())), preferred_element_type=F32,
                )
                score = jnp.where(lanes < count, score * SCALE, LOW)
                peak = jnp.max(score, axis=1, keepdims=True)
                wb[n] = jnp.exp(score - peak).astype(BF16)
                pk[n] = jnp.broadcast_to(peak, (32, 128))
                most = jnp.where(lanes == info[0, n], jnp.maximum(most, peak), most)
            return most

        return most

    def values(k, most):
        cols = pl.ds(pl.multiple_of(1024 + turn(k) * 256, 256), 256)
        dn[...] = jnp.dot(
            wb[...].reshape(SLOTS * 32, 128), jnp.ones((128, 128), BF16), preferred_element_type=F32
        ).reshape(SLOTS, 32, 128)

        @pl.loop(0, SLOTS // GROUP, init_carry=jnp.zeros((32, 128), F32))
        def den(group, den):
            for e in [v for half in zip(range(16), range(16, 32)) for v in half]:
                n = group * GROUP + e
                r = info[0, n]
                best = jnp.max(jnp.where(lanes == r, most, LOW), axis=1, keepdims=True)
                factor = jnp.exp(pk[n] - best)
                both = jnp.dot(wb[n], kvb[n, :, cols], preferred_element_type=F32)
                num = jnp.concatenate([both[:16, :128], both[16:, 128:]], axis=0)
                into, at = (cb, e) if e < 16 else (cb2, e - 16)
                into[at] = num * factor + jnp.where(info[4, n] >= 0, into[info[5, n]], 0.0)
                den = den + jnp.where(lanes == r, factor * dn[n], 0.0)
            return den

        mx[k, 0] = most
        mx[k, 1] = den
        peak_copy(k).start()

    def hand_on(k):
        for i in range(4):
            for rl in range(8):
                r = i * 8 + rl
                sums = jnp.where(info[6, r] >= 0, cb[info[7, r]], 0.0) + jnp.where(
                    info[8, r] >= 0, cb2[info[9, r]], 0.0
                )
                for xh in range(2):
                    for of in range(2):
                        at = pl.ds(xh * 64 + rl, 8, stride=8)
                        s32[k, of, i, at, :] = sums[xh * 16 + of * 8 : xh * 16 + of * 8 + 8]

        chunk_copy(k).start()

    def merge(k):
        kt = turn(k)
        peak_copy(k).wait_recv()
        top, other = mx[k, 0], mxr[k, 0]
        chip_top = jnp.maximum(top, other)
        mine_f, other_f = jnp.exp(top - chip_top), jnp.exp(other - chip_top)
        chip_den = mx[k, 1] * mine_f + mxr[k, 1] * other_f
        mt[0:32, :] = chip_top
        mt[32:64, :] = chip_den
        for w in range(2):
            for xh in range(2):
                row = pl.multiple_of(w * 32 + xh * 16 + core * 8, 8)
                uw[w * 16 + xh * 8 : w * 16 + xh * 8 + 8, :] = mt[pl.ds(row, 8), :]
        lane4 = iota((4, 128), 1)
        packed = [jnp.zeros((4, 128), F32) for _ in range(4)]
        for w in range(2):
            for t in range(4):
                got = uw[pl.ds(w * 16 + t, 4, stride=4), :]
                to = w * 32 + t * 8
                for i in range(4):
                    there = pltpu.roll(got, (to - 8 * i) % 128, 1)
                    packed[i] = jnp.where((lane4 >= to) & (lane4 < to + 8), there, packed[i])
        for i in range(4):
            for j in range(4):
                ss[kt, i * 4 + j] = packed[i][j : j + 1, :]
        both_f = jnp.concatenate([mine_f, other_f, jnp.zeros((64, 128), F32)], axis=0).T
        lift[...] = pltpu.roll(both_f[0:32], (128 - core * 8) % 128, 1)
        chunk_copy(k).wait_recv()

        for i in range(4):
            factors = lift[i * 8 : i * 8 + 8, :]
            for j in range(4):
                total = []
                for t in range(4):
                    lane = (j // 2) * 16 + (j % 2) * 4 + t
                    at = slice(j * 32 + t * 8, j * 32 + t * 8 + 8)
                    total.append(
                        s32[k, core, i, at, :] * factors[:, lane : lane + 1]
                        + r32[k, i, at, :] * factors[:, 32 + lane : 33 + lane]
                    )
                sb[kt, i * 4 + j] = jnp.concatenate(total, axis=0).astype(BF16)

    def send(k):
        kt = turn(k)

        def one(e):
            pz, _, px = beside(e, kt)
            at, to = pz * 4 + px, place(pz, kt, px)
            block_copy(k, at, to).start()
            side_copy(k, at, to).start()

        for e in PLACES:
            one(e)

        @pl.when(k > 0)
        def _():
            one(0)

    def spread_fresh():
        @pl.when(core == 0)
        def _():
            fresh_wait(7).wait_recv()

        @pl.when(core == 1)
        def _():
            fresh_wait(8).wait_recv()

        for m in range(1, 4):
            fresh_plane(m).start()

    def pass_fresh():
        fresh_planes().wait_recv()
        sib_fresh(core).start()

    @pl.loop(0, 5)
    def _(k):
        @pl.when(k < 4)
        def _():
            sib_copy(k, sib).wait_recv()

            kt = turn(k)
            for of in range(2):
                for i in range(4):
                    for j in range(4):
                        gq[of, i, j * 32 : j * 32 + 32, :] = gat[of, kt, i * 4 + j].astype(F32)

            @pl.when(k == 1)
            def _():
                for phase in (2, 3):
                    arrived(phase, ys[SHIFT[phase]], 16).wait_recv()
                    sib_copy(phase, core).start()

            most = scores(k)

            @pl.when(k == 0)
            def _():
                arrived(1, ys[2], 15).wait_recv()
                sib_copy(1, core).start()

                @pl.loop(0, KV_PARTS)
                def _(part):
                    value_copy(part).wait()

            values(k, most)
            hand_on(k)

        @pl.when(k > 0)
        def _():
            merge(k - 1)
            send(k - 1)

        @pl.when(k == 1)
        def _():
            spread_fresh()

        @pl.when(k == 3)
        def _():
            pass_fresh()

    rb[y, spot] = sb[y, spot]
    rs[y, spot] = ss[y, spot]

    sib_fresh(sib).wait_recv()

    @pl.loop(0, 4)
    def _(i):
        for j in range(16):
            fresh = gnt[j // 4, j % 2, i * 2 + (j % 4) // 2].astype(F32)
            for of in range(2):
                gn[of, i, j * 8 : j * 8 + 8, :] = fresh[of * 8 : of * 8 + 8]

    @pl.loop(0, 4)
    def _(e):
        found_row = smeta[SLOTS + e, 0]
        which = jnp.maximum(found_row - 1, 0)
        late, r = which >> 5, which & 31
        pair = [gn[of, r >> 3, pl.ds(r & 7, 16, stride=8), :] for of in range(2)]
        tl[pl.ds(pl.multiple_of(e * 16, 16), 16), :] = jnp.where(found_row > 0, halves(pair[0], pair[1], late > 0), 0.0)
    for j in range(16):
        tail[:, j * 128 : j * 128 + 128] = tl[pl.ds(j, 4, stride=16), :].astype(BF16)

    head = y * 2 + x // 2
    new_rows = []
    for at in (head, head + 8):
        pair = [gn[of, z, pl.ds(pl.multiple_of(at * 8, 8), 8), :] for of in range(2)]
        new_rows.append([halves(pair[0], pair[1], late) for late in (False, True)])
    new_m, new_den, new_num = [], [], []
    for t in range(4):
        mine_q = q[t // 2].astype(F32)[:, (t % 2) * 128 : (t % 2) * 128 + 128]
        found_scores = [
            jnp.sum(mine_q * new_rows[0][j], axis=1, keepdims=True) * SCALE for j in range(t // 2 + 1)
        ]
        peak = found_scores[0]
        for more in found_scores[1:]:
            peak = jnp.maximum(peak, more)
        ws = [jnp.exp(v - peak).astype(BF16).astype(F32) for v in found_scores]
        new_m.append(peak)
        new_den.append(sum(ws[1:], ws[0]))
        num = ws[0] * new_rows[1][0]
        for j in range(1, len(ws)):
            num = num + ws[j] * new_rows[1][j]
        new_num.append(num)
    new_m = jnp.concatenate(new_m, axis=0)
    new_den = jnp.concatenate(new_den, axis=0)
    new_num = jnp.concatenate(new_num, axis=0)

    def take_in(phases, top, den, total):
        planes = [ys[(4 - SHIFT[k]) % 4] for k in phases]
        count = 16 * len(phases)
        for k in phases:
            all_copy(rs, e_sems, k).wait_recv()
        side = [rs[plane].reshape(16, 128) for plane in planes]
        side = jnp.concatenate(side + [jnp.zeros((128 - count, 128), F32)], axis=0).T
        side_m, side_den = side[0:32, :count], side[32:64, :count]
        new_top = jnp.maximum(jnp.max(side_m, axis=1, keepdims=True), top)
        scales = jnp.exp(side_m - new_top)
        old_scale = jnp.exp(top - new_top)
        den = jnp.sum(scales * side_den, axis=1, keepdims=True) + den * old_scale
        total = total * old_scale
        for k, plane in enumerate(planes):
            all_copy(rb, b_sems, phases[k]).wait_recv()
            for e in range(16):
                total = total + scales[:, k * 16 + e : k * 16 + e + 1] * rb[plane, e].astype(F32)
        return new_top, den, total

    state = take_in((0, 1, 2), new_m, new_den, new_num)
    _, final_den, total = take_in((3,), *state)
    result = total / final_den
    for t in range(4):
        out[t // 2, :, (t % 2) * 128 : (t % 2) * 128 + 128] = result[t * 8 : t * 8 + 8].astype(BF16)

    stores = [
        pltpu.make_async_copy(src, dst, io_sem.at[k])
        for k, (src, dst) in enumerate([(out, out_at), (tail, tail_at)])
    ]
    for store in stores:
        store.start()

    for k in range(4):
        all_copy(sb, b_sems, k).wait_send()
        all_copy(ss, e_sems, k).wait_send()
    across_copy().wait_send()
    arrived(0, y, 15).wait_send()
    arrived(1, y, 15).wait_send()
    for m in (3, 1):
        next_copy(m).wait_send()
    for k in range(4):
        sib_copy(k, core).wait_send()
        peak_copy(k).wait_send()
        chunk_copy(k).wait_send()
    pair_rows.wait_send()

    @pl.when(core == 0)
    def _():
        fresh_wait(7).wait_send()

    @pl.when(core == 1)
    def _():
        fresh_wait(8).wait_send()

    fresh_planes().wait_send()
    sib_fresh(core).wait_send()
    for store in stores:
        store.wait()


def hand_over(result, rows, out, tail, out_near, tail_near, sems):
    ways = [(result, out_near, out), (rows, tail_near, tail)]
    arrive = [pltpu.make_async_copy(a, b, sems.at[k]) for k, (a, b, _) in enumerate(ways)]
    leave = [pltpu.make_async_copy(b, c, sems.at[k]) for k, (_, b, c) in enumerate(ways)]
    for copy in arrive:
        copy.start()
    for first, second in zip(arrive, leave):
        first.wait()
        second.start()
    for copy in leave:
        copy.wait()


def per_device(kv_pool, queries, new_kv, lengths, block_dev, block_slot, owner_dev, owner_row):
    anywhere = pl.BlockSpec(memory_space=pltpu.HBM)
    dma = pltpu.SemaphoreType.DMA
    result, tail = pl.pallas_call(
        kernel,
        out_shape=(
            jax.ShapeDtypeStruct((2, 8, 256), BF16),
            jax.ShapeDtypeStruct((4, 2048), BF16),
        ),
        in_specs=[anywhere] * 8,
        out_specs=(anywhere, anywhere),
        scratch_shapes=[
            pltpu.VMEM((2, 8, 256), BF16),
            pltpu.VMEM((2, 8, 64), BF16),
            pltpu.VMEM((REQS, 128), I32),
            pltpu.VMEM((REQS, 128), I32),
            pltpu.VMEM((2, REQS), I32),
            pltpu.VMEM((2, REQS), I32),
            pltpu.SMEM((REQS,), I32),
            pltpu.VMEM((2, 8, 256), BF16),
            pltpu.VMEM((4, 2048), BF16),
            pltpu.SMEM((10, SLOTS), I32),
            pltpu.VMEM((SLOTS, 128, 2048), BF16),
            pltpu.VMEM((2, 4, 16, 32, 128), BF16),
            pltpu.VMEM((2, 8, 128), F32),
            pltpu.VMEM((16, 128), BF16),
            pltpu.VMEM((4, 2, 8, 16, 128), BF16),
            pltpu.VMEM((2, 4, 128, 128), F32),
            pltpu.VMEM((2, 4, 128, 128), F32),
            pltpu.VMEM((SLOTS, 32, 128), BF16),
            pltpu.VMEM((SLOTS, 32, 128), F32),
            pltpu.VMEM((SLOTS, 32, 128), F32),
            pltpu.VMEM((16, 32, 128), F32),
            pltpu.VMEM((16, 32, 128), F32),
            pltpu.VMEM((4, 2, 32, 128), F32),
            pltpu.VMEM((4, 2, 32, 128), F32),
            pltpu.VMEM((64, 128), F32),
            pltpu.VMEM((32, 128), F32),
            pltpu.VMEM((32, 128), F32),
            pltpu.VMEM((4, 2, 4, 128, 128), F32),
            pltpu.VMEM((4, 4, 128, 128), F32),
            pltpu.VMEM((4, 16, 32, 128), BF16),
            pltpu.VMEM((4, 16, 32, 128), BF16),
            pltpu.VMEM((4, 16, 1, 128), F32),
            pltpu.VMEM((4, 16, 1, 128), F32),
            pltpu.VMEM((64, 128), F32),
            pltpu.VMEM((40, 128), I32),
            pltpu.SMEM((40, 128), I32),
            pltpu.VMEM((40, 128), I32),
            dma((KV_PARTS,)),
            dma((KV_PARTS,)),
            dma((5,)),
            dma((5,)),
            dma((4,)),
            dma((4,)),
            dma((8,)),
            dma((4,)),
            dma((4,)),
            dma((4,)),
            dma((4,)),
            dma((2, 4)),
            dma((2, 4)),
            dma,
            dma((7,)),
        ],
        compiler_params=pltpu.CompilerParams(
            collective_id=0, has_side_effects=True, vmem_limit_bytes=56 * 1024 * 1024
        ),
    )(kv_pool, queries, new_kv, block_dev, block_slot, owner_dev, owner_row, lengths)
    return pl.pallas_call(
        hand_over,
        out_shape=(
            jax.ShapeDtypeStruct((2, 8, 256), BF16),
            jax.ShapeDtypeStruct((4, 2048), BF16),
        ),
        in_specs=[anywhere] * 2,
        out_specs=(anywhere, anywhere),
        scratch_shapes=[pltpu.VMEM((2, 8, 256), BF16), pltpu.VMEM((4, 2048), BF16), dma((2,))],
    )(result, tail)


def solution(mesh):
    placed = (
        P(("inst", "seq"), None, None),
        P(None, "inst", "seq"),
        P(None, "inst", "seq"),
        P(),
        P(),
        P(),
        P(),
        P(),
    )
    return jax.shard_map(
        per_device,
        mesh=mesh,
        in_specs=placed,
        out_specs=(P(None, "inst", "seq"), P(("inst", "seq"), None)),
        check_vma=False,
    )
```

```python
import math

import jax
import jax.numpy as jnp
from jax import lax
from jax.experimental import pallas as pl
from jax.experimental.pallas import tpu as pltpu
from jax.sharding import PartitionSpec as P

MESH = pl.DeviceIdType.MESH
F32 = jnp.float32
BF16 = jnp.bfloat16
I32 = jnp.int32

N = 4
CHIPS = 64
SLOTS = 32
REQS = 32
LOW = -1e30
SCALE = 1.0 / math.sqrt(128)
UNROLL = 4
GROUP = 32
SHIFT = (0, 2, 3, 1)
PLACES = (10, 9, 11, 6, 14, 2, 8, 5, 7, 13, 15, 1, 3, 4, 12)
KV_PARTS = SLOTS // UNROLL


def iota(shape, dim):
    return lax.broadcasted_iota(I32, shape, dim)


def halves(first, second, late):
    lane = iota(first.shape, 1)
    if late is True:
        return jnp.where(lane < 64, pltpu.roll(first, 64, 1), second)
    if late is False:
        return jnp.where(lane < 64, first, pltpu.roll(second, 64, 1))
    low = jnp.where(late, pltpu.roll(first, 64, 1), first)
    high = jnp.where(late, second, pltpu.roll(second, 64, 1))
    return jnp.where(lane < 64, low, high)


def kernel(
    kv, q_in, nk_in, dev_in, slot_in, own_dev_in, own_row_in, lens_in, out_at, tail_at,
    q, nk, dev, slot, own_dev, own_row, lens, out, tail,
    info, kvb, gat, nx, tile, gnt, gq, gn, wb, pk, dn, cb, mx, mxr, mt, lift, uw, s32, r32, sb, rb, ss, rs, tl, meta, smeta, codes,
    k_sem, v_sem, sg, rg, s_sib, r_sib, n_sems, s_m, r_m, s_chunk, r_chunk, b_sems, e_sems, meta_sem, io_sem,
):
    z = lax.axis_index("inst")
    c = lax.axis_index("seq")
    y, x, core = c >> 3, (c >> 1) & 3, c & 1
    zs, ys, xs = [[(v + d) & 3 for d in range(4)] for v in (z, y, x)]
    me = z * 32 + c
    chip = z * 16 + y * 4 + x
    sib = 1 - core
    sibling = (z, y * 8 + x * 2 + sib)

    def place(pz, py, px):
        return (pz, py * 8 + px * 2 + core)

    loads = [
        pltpu.make_async_copy(src, dst, io_sem.at[k])
        for k, (src, dst) in enumerate([
            (q_in, q), (nk_in, nk), (dev_in, dev), (slot_in, slot),
            (own_dev_in, own_dev), (own_row_in, own_row), (lens_in, lens),
        ])
    ]
    for load in loads[:2]:
        load.start()

    def beside(e, py):
        return zs[e // 4], py, xs[e % 4]

    barrier = pltpu.get_barrier_semaphore()

    for e in PLACES:
        pl.semaphore_signal(barrier, inc=1, device_id=place(*beside(e, y)), device_id_type=MESH)
    for m in range(1, 4):
        pl.semaphore_signal(barrier, inc=1, device_id=place(z, ys[m], x), device_id_type=MESH)
    pl.semaphore_signal(barrier, inc=1, device_id=sibling, device_id_type=MESH)
    for load in loads[2:]:
        load.start()

    def key_copy(part):
        span = pl.ds(part * UNROLL, UNROLL)
        cols = pl.ds(0, 1024)
        return pltpu.make_async_copy(kv.at[span, :, cols], kvb.at[span, :, cols], k_sem.at[part])

    def value_copy(part):
        span = pl.ds(part * UNROLL, UNROLL)
        cols = pl.ds(1024, 1024)
        return pltpu.make_async_copy(kv.at[span, :, cols], kvb.at[span, :, cols], v_sem.at[part])

    spot = z * 4 + x
    for load in loads[:2]:
        load.wait()
    own = [q[s].astype(F32) for s in range(2)]
    gat[core, y, spot] = jnp.concatenate(
        [own[0][:, :128], own[0][:, 128:], own[1][:, :128], own[1][:, 128:]], axis=0
    ).astype(BF16)
    nx[0] = jnp.concatenate([nk[0].astype(F32), nk[1].astype(F32)], axis=1)

    pl.semaphore_wait(barrier, 19)

    def turn(k):
        return (y + 2 * (k & 1) + 3 * (k >> 1)) & 3

    def push(block, k, to):
        return pltpu.make_async_remote_copy(
            src_ref=block, dst_ref=block, send_sem=sg.at[k], recv_sem=rg.at[k],
            device_id=to, device_id_type=MESH,
        )

    def plane_copy(e):
        return push(gat.at[core, y, spot], 0, place(*beside(e, y)))

    def across_copy():
        return push(gat.at[core, y, spot], 4, place(z, ys[2], x))

    def relay_copy(e):
        return push(gat.at[core, ys[2], spot], 1, place(*beside(e, y)))

    def next_copy(m):
        return push(gat.at[core, y], 3 if m == 3 else 2, place(z, ys[m], x))

    def arrived(k, plane, blocks):
        return push(gat.at[core, plane, pl.ds(0, blocks)], k, sibling)

    def sib_copy(k, of):
        block = gat.at[of, turn(k)]
        return pltpu.make_async_remote_copy(
            src_ref=block, dst_ref=block, send_sem=s_sib.at[k], recv_sem=r_sib.at[k],
            device_id=sibling, device_id_type=MESH,
        )

    across_copy().start()

    for e in PLACES:
        plane_copy(e).start()

    @pl.loop(0, KV_PARTS)
    def _(part):
        key_copy(part).start()

    pair_rows = pltpu.make_async_remote_copy(
        src_ref=nx.at[0], dst_ref=nx.at[1], send_sem=n_sems.at[0], recv_sem=n_sems.at[1],
        device_id=sibling, device_id_type=MESH,
    )
    pair_rows.start()
    shelf = z * 2 + (x >> 1)
    side_of = (x + core) & 1

    def fresh_copy(e):
        return pltpu.make_async_remote_copy(
            src_ref=tile, dst_ref=gnt.at[y, x & 1, shelf], send_sem=n_sems.at[2], recv_sem=n_sems.at[3],
            device_id=place(*beside(e, y)), device_id_type=MESH,
        )

    def fresh_wait(tiles):
        block = gnt.at[y, side_of, pl.ds(0, tiles)]
        return pltpu.make_async_remote_copy(
            src_ref=block, dst_ref=block, send_sem=n_sems.at[2], recv_sem=n_sems.at[3],
            device_id=sibling, device_id_type=MESH,
        )

    def fresh_plane(m):
        block = gnt.at[y, side_of]
        return pltpu.make_async_remote_copy(
            src_ref=block, dst_ref=block, send_sem=n_sems.at[4], recv_sem=n_sems.at[5],
            device_id=place(z, ys[m], x), device_id_type=MESH,
        )

    def fresh_planes():
        block = gnt.at[pl.ds(0, 3), side_of]
        return pltpu.make_async_remote_copy(
            src_ref=block, dst_ref=block, send_sem=n_sems.at[4], recv_sem=n_sems.at[5],
            device_id=sibling, device_id_type=MESH,
        )

    def sib_fresh(of):
        block = gnt.at[:, (x + of) & 1]
        return pltpu.make_async_remote_copy(
            src_ref=block, dst_ref=block, send_sem=n_sems.at[6], recv_sem=n_sems.at[7],
            device_id=sibling, device_id_type=MESH,
        )

    @pl.loop(0, KV_PARTS)
    def _(part):
        value_copy(part).start()

    for load in loads[2:]:
        load.wait()
    mine = jnp.where(dev[...] == me, slot[...], -1)
    code = iota((REQS, 128), 0) * 128 + iota((REQS, 128), 1) + 1

    @pl.loop(0, SLOTS // 4)
    def _(group):
        for e in range(4):
            n = group * 4 + e
            codes[pl.ds(n, 1), :] = jnp.sum(jnp.where(mine == n, code, 0), axis=0, keepdims=True)

    owned = jnp.where(own_dev[...] == me, own_row[...], -1)
    row_code = iota((2, REQS), 0) * REQS + iota((2, REQS), 1) + 1
    pad_row = jnp.zeros((1, 96), I32)
    for e in range(4):
        hit = jnp.sum(jnp.where(owned == e, row_code, 0), axis=0, keepdims=True)
        codes[SLOTS + e : SLOTS + e + 1, :] = jnp.concatenate([hit, pad_row], axis=1)
    codes[SLOTS + 4 :, :] = jnp.zeros((4, 128), I32)

    found = jnp.broadcast_to(jnp.sum(codes[...], axis=1, keepdims=True), (40, 128))
    held = found[:SLOTS]
    req_col = jnp.where(held > 0, jnp.minimum((held - 1) >> 7, REQS - 1), -1)
    rows, lanes = iota((SLOTS, 128), 0), iota((SLOTS, 128), 1)
    req_row = jnp.sum(jnp.where(rows == lanes, req_col, 0), axis=0, keepdims=True)
    req_row = jnp.where(lanes < SLOTS, jnp.broadcast_to(req_row, (SLOTS, 128)), -2)
    before = jnp.max(jnp.where((req_row == req_col) & (lanes < rows), lanes, -1), axis=1, keepdims=True)
    last = jnp.max(jnp.where(req_row == rows, lanes, -1), axis=1, keepdims=True)
    meta[:SLOTS] = jnp.where(
        lanes == 0, req_col, jnp.where(lanes == 1, held, jnp.where(lanes == 2, before, last))
    )
    meta[SLOTS:] = found[SLOTS:]
    meta_copy = pltpu.make_async_copy(meta, smeta, meta_sem)
    meta_copy.start()

    pair_rows.wait_recv()
    both_rows = [jnp.where(core == of, nx[0], nx[1]) for of in range(2)]
    tile[...] = jnp.concatenate(both_rows, axis=0).astype(BF16)

    @pl.when(core == 0)
    def _():
        gnt[y, x & 1, shelf] = tile[...]

    push(gat.at[core, ys[2], spot], 4, sibling).wait_recv()

    for e in PLACES:
        relay_copy(e).start()

    arrived(0, y, 15).wait_recv()
    sib_copy(0, core).start()
    for m in (1, 3):
        next_copy(m).start()

    for of in range(2):
        @pl.when(core == of)
        def _():
            for e in range(2 - of, 16, 2):
                fresh_copy(e).start()

    meta_copy.wait()

    @pl.loop(0, SLOTS)
    def _(n):
        req, held, prev, end = smeta[n, 0], smeta[n, 1], smeta[n, 2], smeta[n, 3]
        r = jnp.maximum(req, 0)
        b = (jnp.maximum(held, 1) - 1) & 127
        info[0, n] = req
        info[1, n] = r >> 3
        info[2, n] = r & 7
        info[3, n] = jnp.where(held > 0, lens[r] - b * 128, 0)
        info[4, n] = prev
        info[5, n] = jnp.maximum(prev, 0)
        info[6, n] = end
        info[7, n] = jnp.maximum(end, 0)


    @pl.loop(0, KV_PARTS)
    def _(part):
        key_copy(part).wait()

    lanes = iota((32, 128), 1)
    blank = jnp.zeros((16, 128), BF16)

    def chunk_copy(k):
        return pltpu.make_async_remote_copy(
            src_ref=s32.at[k, sib], dst_ref=r32.at[k],
            send_sem=s_chunk.at[k], recv_sem=r_chunk.at[k], device_id=sibling, device_id_type=MESH,
        )

    def peak_copy(k):
        return pltpu.make_async_remote_copy(
            src_ref=mx.at[k], dst_ref=mxr.at[k], send_sem=s_m.at[k], recv_sem=r_m.at[k],
            device_id=sibling, device_id_type=MESH,
        )

    def block_copy(k, at, to):
        return pltpu.make_async_remote_copy(
            src_ref=sb.at[turn(k), at], dst_ref=rb.at[y, spot], send_sem=b_sems.at[0, k], recv_sem=b_sems.at[1, k],
            device_id=to, device_id_type=MESH,
        )

    def side_copy(k, at, to):
        return pltpu.make_async_remote_copy(
            src_ref=ss.at[turn(k), at], dst_ref=rs.at[y, spot], send_sem=e_sems.at[0, k], recv_sem=e_sems.at[1, k],
            device_id=to, device_id_type=MESH,
        )

    def all_copy(buf, sems, k):
        block = buf.at[ys[(4 - SHIFT[k]) % 4], pl.ds(0, 16 if k else 15)]
        return pltpu.make_async_remote_copy(
            src_ref=block, dst_ref=block, send_sem=sems.at[0, k], recv_sem=sems.at[1, k],
            device_id=sibling, device_id_type=MESH,
        )

    def scores(k):
        cols = pl.ds(pl.multiple_of(turn(k) * 256, 256), 256)

        @pl.loop(0, SLOTS // GROUP, init_carry=jnp.full((32, 128), LOW, F32))
        def most(group, most):
            for e in range(GROUP):
                n = group * GROUP + e
                i, rl, count = info[1, n], info[2, n], info[3, n]
                parts = [gq[of, i, pl.ds(rl, 16, stride=8), :].reshape(2, 8, 128) for of in range(2)]
                heads = jnp.concatenate(parts, axis=1).astype(BF16)
                first = jnp.concatenate([heads[0], blank], axis=1)
                second = jnp.concatenate([blank, heads[1]], axis=1)
                score = lax.dot_general(
                    jnp.concatenate([first, second], axis=0), kvb[n, :, cols],
                    (((1,), (1,)), ((), ())), preferred_element_type=F32,
                )
                score = jnp.where(lanes < count, score * SCALE, LOW)
                peak = jnp.max(score, axis=1, keepdims=True)
                wb[n] = jnp.exp(score - peak).astype(BF16)
                pk[n] = jnp.broadcast_to(peak, (32, 128))
                most = jnp.where(lanes == info[0, n], jnp.maximum(most, peak), most)
            return most

        return most

    def values(k, most):
        cols = pl.ds(pl.multiple_of(1024 + turn(k) * 256, 256), 256)
        dn[...] = jnp.dot(
            wb[...].reshape(SLOTS * 32, 128), jnp.ones((128, 128), BF16), preferred_element_type=F32
        ).reshape(SLOTS, 32, 128)

        @pl.loop(0, SLOTS // GROUP, init_carry=jnp.zeros((32, 128), F32))
        def den(group, den):
            for e in range(GROUP):
                n = group * GROUP + e
                r = info[0, n]
                best = jnp.max(jnp.where(lanes == r, most, LOW), axis=1, keepdims=True)
                factor = jnp.exp(pk[n] - best)
                both = jnp.dot(wb[n], kvb[n, :, cols], preferred_element_type=F32)
                num = jnp.concatenate([both[:16, :128], both[16:, 128:]], axis=0)
                earlier = jnp.where(info[4, n] >= 0, cb[info[5, n]], 0.0)
                cb[n] = num * factor + earlier
                den = den + jnp.where(lanes == r, factor * dn[n], 0.0)
            return den

        mx[k, 0] = most
        mx[k, 1] = den
        peak_copy(k).start()

    def hand_on(k):
        for i in range(4):
            for rl in range(8):
                sums = jnp.where(info[6, i * 8 + rl] >= 0, cb[info[7, i * 8 + rl]], 0.0)
                for xh in range(2):
                    for of in range(2):
                        at = pl.ds(xh * 64 + rl, 8, stride=8)
                        s32[k, of, i, at, :] = sums[xh * 16 + of * 8 : xh * 16 + of * 8 + 8]

        chunk_copy(k).start()

    def merge(k):
        kt = turn(k)
        peak_copy(k).wait_recv()
        top, other = mx[k, 0], mxr[k, 0]
        chip_top = jnp.maximum(top, other)
        mine_f, other_f = jnp.exp(top - chip_top), jnp.exp(other - chip_top)
        chip_den = mx[k, 1] * mine_f + mxr[k, 1] * other_f
        mt[0:32, :] = chip_top
        mt[32:64, :] = chip_den
        for w in range(2):
            for xh in range(2):
                row = pl.multiple_of(w * 32 + xh * 16 + core * 8, 8)
                uw[w * 16 + xh * 8 : w * 16 + xh * 8 + 8, :] = mt[pl.ds(row, 8), :]
        lane4 = iota((4, 128), 1)
        packed = [jnp.zeros((4, 128), F32) for _ in range(4)]
        for w in range(2):
            for t in range(4):
                got = uw[pl.ds(w * 16 + t, 4, stride=4), :]
                to = w * 32 + t * 8
                for i in range(4):
                    there = pltpu.roll(got, (to - 8 * i) % 128, 1)
                    packed[i] = jnp.where((lane4 >= to) & (lane4 < to + 8), there, packed[i])
        for i in range(4):
            for j in range(4):
                ss[kt, i * 4 + j] = packed[i][j : j + 1, :]
        both_f = jnp.concatenate([mine_f, other_f, jnp.zeros((64, 128), F32)], axis=0).T
        lift[...] = pltpu.roll(both_f[0:32], (128 - core * 8) % 128, 1)
        chunk_copy(k).wait_recv()

        for i in range(4):
            factors = lift[i * 8 : i * 8 + 8, :]
            for j in range(4):
                total = []
                for t in range(4):
                    lane = (j // 2) * 16 + (j % 2) * 4 + t
                    at = slice(j * 32 + t * 8, j * 32 + t * 8 + 8)
                    total.append(
                        s32[k, core, i, at, :] * factors[:, lane : lane + 1]
                        + r32[k, i, at, :] * factors[:, 32 + lane : 33 + lane]
                    )
                sb[kt, i * 4 + j] = jnp.concatenate(total, axis=0).astype(BF16)

    def send(k):
        kt = turn(k)

        def one(e):
            pz, _, px = beside(e, kt)
            at, to = pz * 4 + px, place(pz, kt, px)
            block_copy(k, at, to).start()
            side_copy(k, at, to).start()

        for e in PLACES:
            one(e)

        @pl.when(k > 0)
        def _():
            one(0)

    def spread_fresh():
        @pl.when(core == 0)
        def _():
            fresh_wait(7).wait_recv()

        @pl.when(core == 1)
        def _():
            fresh_wait(8).wait_recv()

        for m in range(1, 4):
            fresh_plane(m).start()

    def pass_fresh():
        fresh_planes().wait_recv()
        sib_fresh(core).start()

    @pl.loop(0, 5)
    def _(k):
        @pl.when(k < 4)
        def _():
            sib_copy(k, sib).wait_recv()

            kt = turn(k)
            for of in range(2):
                for i in range(4):
                    for j in range(4):
                        gq[of, i, j * 32 : j * 32 + 32, :] = gat[of, kt, i * 4 + j].astype(F32)

            most = scores(k)

            @pl.when(k == 0)
            def _():
                arrived(1, ys[2], 15).wait_recv()
                sib_copy(1, core).start()

            @pl.when(k == 1)
            def _():
                for phase in (2, 3):
                    arrived(phase, ys[SHIFT[phase]], 16).wait_recv()
                    sib_copy(phase, core).start()

            @pl.when(k == 0)
            def _():
                @pl.loop(0, KV_PARTS)
                def _(part):
                    value_copy(part).wait()

            values(k, most)
            hand_on(k)

        @pl.when(k > 0)
        def _():
            merge(k - 1)
            send(k - 1)

        @pl.when(k == 1)
        def _():
            spread_fresh()

        @pl.when(k == 3)
        def _():
            pass_fresh()

    rb[y, spot] = sb[y, spot]
    rs[y, spot] = ss[y, spot]

    sib_fresh(sib).wait_recv()

    @pl.loop(0, 4)
    def _(i):
        for j in range(16):
            fresh = gnt[j // 4, j % 2, i * 2 + (j % 4) // 2].astype(F32)
            for of in range(2):
                gn[of, i, j * 8 : j * 8 + 8, :] = fresh[of * 8 : of * 8 + 8]

    @pl.loop(0, 4)
    def _(e):
        found_row = smeta[SLOTS + e, 0]
        which = jnp.maximum(found_row - 1, 0)
        late, r = which >> 5, which & 31
        pair = [gn[of, r >> 3, pl.ds(r & 7, 16, stride=8), :] for of in range(2)]
        tl[pl.ds(pl.multiple_of(e * 16, 16), 16), :] = jnp.where(found_row > 0, halves(pair[0], pair[1], late > 0), 0.0)
    for j in range(16):
        tail[:, j * 128 : j * 128 + 128] = tl[pl.ds(j, 4, stride=16), :].astype(BF16)

    head = y * 2 + x // 2
    new_rows = []
    for at in (head, head + 8):
        pair = [gn[of, z, pl.ds(pl.multiple_of(at * 8, 8), 8), :] for of in range(2)]
        new_rows.append([halves(pair[0], pair[1], late) for late in (False, True)])
    new_m, new_den, new_num = [], [], []
    for t in range(4):
        mine_q = q[t // 2].astype(F32)[:, (t % 2) * 128 : (t % 2) * 128 + 128]
        found_scores = [
            jnp.sum(mine_q * new_rows[0][j], axis=1, keepdims=True) * SCALE for j in range(t // 2 + 1)
        ]
        peak = found_scores[0]
        for more in found_scores[1:]:
            peak = jnp.maximum(peak, more)
        ws = [jnp.exp(v - peak).astype(BF16).astype(F32) for v in found_scores]
        new_m.append(peak)
        new_den.append(sum(ws[1:], ws[0]))
        num = ws[0] * new_rows[1][0]
        for j in range(1, len(ws)):
            num = num + ws[j] * new_rows[1][j]
        new_num.append(num)
    new_m = jnp.concatenate(new_m, axis=0)
    new_den = jnp.concatenate(new_den, axis=0)
    new_num = jnp.concatenate(new_num, axis=0)

    def take_in(phases, top, den, total):
        planes = [ys[(4 - SHIFT[k]) % 4] for k in phases]
        count = 16 * len(phases)
        for k in phases:
            all_copy(rs, e_sems, k).wait_recv()
        side = [rs[plane].reshape(16, 128) for plane in planes]
        side = jnp.concatenate(side + [jnp.zeros((128 - count, 128), F32)], axis=0).T
        side_m, side_den = side[0:32, :count], side[32:64, :count]
        new_top = jnp.maximum(jnp.max(side_m, axis=1, keepdims=True), top)
        scales = jnp.exp(side_m - new_top)
        old_scale = jnp.exp(top - new_top)
        den = jnp.sum(scales * side_den, axis=1, keepdims=True) + den * old_scale
        total = total * old_scale
        for k, plane in enumerate(planes):
            all_copy(rb, b_sems, phases[k]).wait_recv()
            for e in range(16):
                total = total + scales[:, k * 16 + e : k * 16 + e + 1] * rb[plane, e].astype(F32)
        return new_top, den, total

    state = take_in((0, 1, 2), new_m, new_den, new_num)
    _, final_den, total = take_in((3,), *state)
    result = total / final_den
    for t in range(4):
        out[t // 2, :, (t % 2) * 128 : (t % 2) * 128 + 128] = result[t * 8 : t * 8 + 8].astype(BF16)

    stores = [
        pltpu.make_async_copy(src, dst, io_sem.at[k])
        for k, (src, dst) in enumerate([(out, out_at), (tail, tail_at)])
    ]
    for store in stores:
        store.start()

    for k in range(4):
        all_copy(sb, b_sems, k).wait_send()
        all_copy(ss, e_sems, k).wait_send()
    across_copy().wait_send()
    arrived(0, y, 15).wait_send()
    arrived(1, y, 15).wait_send()
    for m in (1, 3):
        next_copy(m).wait_send()
    for k in range(4):
        sib_copy(k, core).wait_send()
        peak_copy(k).wait_send()
        chunk_copy(k).wait_send()
    pair_rows.wait_send()

    @pl.when(core == 0)
    def _():
        fresh_wait(7).wait_send()

    @pl.when(core == 1)
    def _():
        fresh_wait(8).wait_send()

    fresh_planes().wait_send()
    sib_fresh(core).wait_send()
    for store in stores:
        store.wait()


def hand_over(result, rows, out, tail, out_near, tail_near, sems):
    ways = [(result, out_near, out), (rows, tail_near, tail)]
    arrive = [pltpu.make_async_copy(a, b, sems.at[k]) for k, (a, b, _) in enumerate(ways)]
    leave = [pltpu.make_async_copy(b, c, sems.at[k]) for k, (_, b, c) in enumerate(ways)]
    for copy in arrive:
        copy.start()
    for first, second in zip(arrive, leave):
        first.wait()
        second.start()
    for copy in leave:
        copy.wait()


def per_device(kv_pool, queries, new_kv, lengths, block_dev, block_slot, owner_dev, owner_row):
    anywhere = pl.BlockSpec(memory_space=pltpu.HBM)
    dma = pltpu.SemaphoreType.DMA
    result, tail = pl.pallas_call(
        kernel,
        out_shape=(
            jax.ShapeDtypeStruct((2, 8, 256), BF16),
            jax.ShapeDtypeStruct((4, 2048), BF16),
        ),
        in_specs=[anywhere] * 8,
        out_specs=(anywhere, anywhere),
        scratch_shapes=[
            pltpu.VMEM((2, 8, 256), BF16),
            pltpu.VMEM((2, 8, 64), BF16),
            pltpu.VMEM((REQS, 128), I32),
            pltpu.VMEM((REQS, 128), I32),
            pltpu.VMEM((2, REQS), I32),
            pltpu.VMEM((2, REQS), I32),
            pltpu.SMEM((REQS,), I32),
            pltpu.VMEM((2, 8, 256), BF16),
            pltpu.VMEM((4, 2048), BF16),
            pltpu.SMEM((8, SLOTS), I32),
            pltpu.VMEM((SLOTS, 128, 2048), BF16),
            pltpu.VMEM((2, 4, 16, 32, 128), BF16),
            pltpu.VMEM((2, 8, 128), F32),
            pltpu.VMEM((16, 128), BF16),
            pltpu.VMEM((4, 2, 8, 16, 128), BF16),
            pltpu.VMEM((2, 4, 128, 128), F32),
            pltpu.VMEM((2, 4, 128, 128), F32),
            pltpu.VMEM((SLOTS, 32, 128), BF16),
            pltpu.VMEM((SLOTS, 32, 128), F32),
            pltpu.VMEM((SLOTS, 32, 128), F32),
            pltpu.VMEM((SLOTS, 32, 128), F32),
            pltpu.VMEM((4, 2, 32, 128), F32),
            pltpu.VMEM((4, 2, 32, 128), F32),
            pltpu.VMEM((64, 128), F32),
            pltpu.VMEM((32, 128), F32),
            pltpu.VMEM((32, 128), F32),
            pltpu.VMEM((4, 2, 4, 128, 128), F32),
            pltpu.VMEM((4, 4, 128, 128), F32),
            pltpu.VMEM((4, 16, 32, 128), BF16),
            pltpu.VMEM((4, 16, 32, 128), BF16),
            pltpu.VMEM((4, 16, 1, 128), F32),
            pltpu.VMEM((4, 16, 1, 128), F32),
            pltpu.VMEM((64, 128), F32),
            pltpu.VMEM((40, 128), I32),
            pltpu.SMEM((40, 128), I32),
            pltpu.VMEM((40, 128), I32),
            dma((KV_PARTS,)),
            dma((KV_PARTS,)),
            dma((5,)),
            dma((5,)),
            dma((4,)),
            dma((4,)),
            dma((8,)),
            dma((4,)),
            dma((4,)),
            dma((4,)),
            dma((4,)),
            dma((2, 4)),
            dma((2, 4)),
            dma,
            dma((7,)),
        ],
        compiler_params=pltpu.CompilerParams(
            collective_id=0, has_side_effects=True, vmem_limit_bytes=56 * 1024 * 1024
        ),
    )(kv_pool, queries, new_kv, block_dev, block_slot, owner_dev, owner_row, lengths)
    return pl.pallas_call(
        hand_over,
        out_shape=(
            jax.ShapeDtypeStruct((2, 8, 256), BF16),
            jax.ShapeDtypeStruct((4, 2048), BF16),
        ),
        in_specs=[anywhere] * 2,
        out_specs=(anywhere, anywhere),
        scratch_shapes=[pltpu.VMEM((2, 8, 256), BF16), pltpu.VMEM((4, 2048), BF16), dma((2,))],
    )(result, tail)


def solution(mesh):
    placed = (
        P(("inst", "seq"), None, None),
        P(None, "inst", "seq"),
        P(None, "inst", "seq"),
        P(),
        P(),
        P(),
        P(),
        P(),
    )
    return jax.shard_map(
        per_device,
        mesh=mesh,
        in_specs=placed,
        out_specs=(P(None, "inst", "seq"), P(("inst", "seq"), None)),
        check_vma=False,
    )
```

```python
import math

import jax
import jax.numpy as jnp
from jax import lax
from jax.experimental import pallas as pl
from jax.experimental.pallas import tpu as pltpu
from jax.sharding import PartitionSpec as P

MESH = pl.DeviceIdType.MESH
F32 = jnp.float32
BF16 = jnp.bfloat16
I32 = jnp.int32

N = 4
CHIPS = 64
SLOTS = 32
REQS = 32
LOW = -1e30
SCALE = 1.0 / math.sqrt(128)
UNROLL = 4
GROUP = 32
SHIFT = (0, 2, 1, 3)
PLACES = (10, 9, 11, 6, 14, 2, 8, 5, 7, 13, 15, 1, 3, 4, 12)
KV_PARTS = SLOTS // UNROLL


def iota(shape, dim):
    return lax.broadcasted_iota(I32, shape, dim)


def halves(first, second, late):
    lane = iota(first.shape, 1)
    if late is True:
        return jnp.where(lane < 64, pltpu.roll(first, 64, 1), second)
    if late is False:
        return jnp.where(lane < 64, first, pltpu.roll(second, 64, 1))
    low = jnp.where(late, pltpu.roll(first, 64, 1), first)
    high = jnp.where(late, second, pltpu.roll(second, 64, 1))
    return jnp.where(lane < 64, low, high)


def kernel(
    kv, q_in, nk_in, dev_in, slot_in, own_dev_in, own_row_in, lens_in, out_at, tail_at,
    q, nk, dev, slot, own_dev, own_row, lens, out, tail,
    info, kvb, gat, nx, tile, gnt, gq, gn, wb, pk, dn, cb, mx, mxr, mt, lift, uw, s32, r32, sb, rb, ss, rs, tl, meta, smeta, codes,
    k_sem, v_sem, sg, rg, s_sib, r_sib, n_sems, s_m, r_m, s_chunk, r_chunk, b_sems, e_sems, meta_sem, io_sem,
):
    z = lax.axis_index("inst")
    c = lax.axis_index("seq")
    y, x, core = c >> 3, (c >> 1) & 3, c & 1
    zs, ys, xs = [[(v + d) & 3 for d in range(4)] for v in (z, y, x)]
    me = z * 32 + c
    chip = z * 16 + y * 4 + x
    sib = 1 - core
    sibling = (z, y * 8 + x * 2 + sib)

    def place(pz, py, px):
        return (pz, py * 8 + px * 2 + core)

    loads = [
        pltpu.make_async_copy(src, dst, io_sem.at[k])
        for k, (src, dst) in enumerate([
            (q_in, q), (nk_in, nk), (dev_in, dev), (slot_in, slot),
            (own_dev_in, own_dev), (own_row_in, own_row), (lens_in, lens),
        ])
    ]
    for load in loads[:2]:
        load.start()

    def beside(e, py):
        return zs[e // 4], py, xs[e % 4]

    barrier = pltpu.get_barrier_semaphore()

    for e in PLACES:
        pl.semaphore_signal(barrier, inc=1, device_id=place(*beside(e, y)), device_id_type=MESH)
    for m in range(1, 4):
        pl.semaphore_signal(barrier, inc=1, device_id=place(z, ys[m], x), device_id_type=MESH)
    pl.semaphore_signal(barrier, inc=1, device_id=sibling, device_id_type=MESH)
    for load in loads[2:]:
        load.start()

    def key_copy(part):
        span = pl.ds(part * UNROLL, UNROLL)
        cols = pl.ds(0, 1024)
        return pltpu.make_async_copy(kv.at[span, :, cols], kvb.at[span, :, cols], k_sem.at[part])

    def value_copy(part):
        span = pl.ds(part * UNROLL, UNROLL)
        cols = pl.ds(1024, 1024)
        return pltpu.make_async_copy(kv.at[span, :, cols], kvb.at[span, :, cols], v_sem.at[part])

    spot = z * 4 + x
    for load in loads[:2]:
        load.wait()
    own = [q[s].astype(F32) for s in range(2)]
    gat[core, y, spot] = jnp.concatenate(
        [own[0][:, :128], own[0][:, 128:], own[1][:, :128], own[1][:, 128:]], axis=0
    ).astype(BF16)
    nx[0] = jnp.concatenate([nk[0].astype(F32), nk[1].astype(F32)], axis=1)

    pl.semaphore_wait(barrier, 19)

    def turn(k):
        return (y + ((k & 1) << 1) + (k >> 1)) & 3

    def push(block, k, to):
        return pltpu.make_async_remote_copy(
            src_ref=block, dst_ref=block, send_sem=sg.at[k], recv_sem=rg.at[k],
            device_id=to, device_id_type=MESH,
        )

    def plane_copy(e):
        return push(gat.at[core, y, spot], 0, place(*beside(e, y)))

    def across_copy():
        return push(gat.at[core, y, spot], 4, place(z, ys[2], x))

    def relay_copy(e):
        return push(gat.at[core, ys[2], spot], 1, place(*beside(e, y)))

    def next_copy(m):
        return push(gat.at[core, y], 2 if m == 3 else 3, place(z, ys[m], x))

    def arrived(k, plane, blocks):
        return push(gat.at[core, plane, pl.ds(0, blocks)], k, sibling)

    def sib_copy(k, of):
        block = gat.at[of, turn(k)]
        return pltpu.make_async_remote_copy(
            src_ref=block, dst_ref=block, send_sem=s_sib.at[k], recv_sem=r_sib.at[k],
            device_id=sibling, device_id_type=MESH,
        )

    across_copy().start()

    for e in PLACES:
        plane_copy(e).start()

    @pl.loop(0, KV_PARTS)
    def _(part):
        key_copy(part).start()

    pair_rows = pltpu.make_async_remote_copy(
        src_ref=nx.at[0], dst_ref=nx.at[1], send_sem=n_sems.at[0], recv_sem=n_sems.at[1],
        device_id=sibling, device_id_type=MESH,
    )
    pair_rows.start()
    shelf = z * 2 + (x >> 1)
    side_of = (x + core) & 1

    def fresh_copy(e):
        return pltpu.make_async_remote_copy(
            src_ref=tile, dst_ref=gnt.at[y, x & 1, shelf], send_sem=n_sems.at[2], recv_sem=n_sems.at[3],
            device_id=place(*beside(e, y)), device_id_type=MESH,
        )

    def fresh_wait(tiles):
        block = gnt.at[y, side_of, pl.ds(0, tiles)]
        return pltpu.make_async_remote_copy(
            src_ref=block, dst_ref=block, send_sem=n_sems.at[2], recv_sem=n_sems.at[3],
            device_id=sibling, device_id_type=MESH,
        )

    def fresh_plane(m):
        block = gnt.at[y, side_of]
        return pltpu.make_async_remote_copy(
            src_ref=block, dst_ref=block, send_sem=n_sems.at[4], recv_sem=n_sems.at[5],
            device_id=place(z, ys[m], x), device_id_type=MESH,
        )

    def fresh_planes():
        block = gnt.at[pl.ds(0, 3), side_of]
        return pltpu.make_async_remote_copy(
            src_ref=block, dst_ref=block, send_sem=n_sems.at[4], recv_sem=n_sems.at[5],
            device_id=sibling, device_id_type=MESH,
        )

    def sib_fresh(of):
        block = gnt.at[:, (x + of) & 1]
        return pltpu.make_async_remote_copy(
            src_ref=block, dst_ref=block, send_sem=n_sems.at[6], recv_sem=n_sems.at[7],
            device_id=sibling, device_id_type=MESH,
        )

    @pl.loop(0, KV_PARTS)
    def _(part):
        value_copy(part).start()

    for load in loads[2:]:
        load.wait()
    mine = jnp.where(dev[...] == me, slot[...], -1)
    code = iota((REQS, 128), 0) * 128 + iota((REQS, 128), 1) + 1

    @pl.loop(0, SLOTS // 4)
    def _(group):
        for e in range(4):
            n = group * 4 + e
            codes[pl.ds(n, 1), :] = jnp.sum(jnp.where(mine == n, code, 0), axis=0, keepdims=True)

    owned = jnp.where(own_dev[...] == me, own_row[...], -1)
    row_code = iota((2, REQS), 0) * REQS + iota((2, REQS), 1) + 1
    pad_row = jnp.zeros((1, 96), I32)
    for e in range(4):
        hit = jnp.sum(jnp.where(owned == e, row_code, 0), axis=0, keepdims=True)
        codes[SLOTS + e : SLOTS + e + 1, :] = jnp.concatenate([hit, pad_row], axis=1)
    codes[SLOTS + 4 :, :] = jnp.zeros((4, 128), I32)

    found = jnp.broadcast_to(jnp.sum(codes[...], axis=1, keepdims=True), (40, 128))
    held = found[:SLOTS]
    req_col = jnp.where(held > 0, jnp.minimum((held - 1) >> 7, REQS - 1), -1)
    rows, lanes = iota((SLOTS, 128), 0), iota((SLOTS, 128), 1)
    req_row = jnp.sum(jnp.where(rows == lanes, req_col, 0), axis=0, keepdims=True)
    req_row = jnp.where(lanes < SLOTS, jnp.broadcast_to(req_row, (SLOTS, 128)), -2)
    before = jnp.max(jnp.where((req_row == req_col) & (lanes < rows), lanes, -1), axis=1, keepdims=True)
    last = jnp.max(jnp.where(req_row == rows, lanes, -1), axis=1, keepdims=True)
    meta[:SLOTS] = jnp.where(
        lanes == 0, req_col, jnp.where(lanes == 1, held, jnp.where(lanes == 2, before, last))
    )
    meta[SLOTS:] = found[SLOTS:]
    meta_copy = pltpu.make_async_copy(meta, smeta, meta_sem)
    meta_copy.start()

    pair_rows.wait_recv()
    both_rows = [jnp.where(core == of, nx[0], nx[1]) for of in range(2)]
    tile[...] = jnp.concatenate(both_rows, axis=0).astype(BF16)

    @pl.when(core == 0)
    def _():
        gnt[y, x & 1, shelf] = tile[...]

    push(gat.at[core, ys[2], spot], 4, sibling).wait_recv()

    for e in PLACES:
        relay_copy(e).start()

    arrived(0, y, 15).wait_recv()
    sib_copy(0, core).start()
    for m in (3, 1):
        next_copy(m).start()

    for of in range(2):
        @pl.when(core == of)
        def _():
            for e in range(2 - of, 16, 2):
                fresh_copy(e).start()

    meta_copy.wait()

    @pl.loop(0, SLOTS)
    def _(n):
        req, held, prev, end = smeta[n, 0], smeta[n, 1], smeta[n, 2], smeta[n, 3]
        r = jnp.maximum(req, 0)
        b = (jnp.maximum(held, 1) - 1) & 127
        info[0, n] = req
        info[1, n] = r >> 3
        info[2, n] = r & 7
        info[3, n] = jnp.where(held > 0, lens[r] - b * 128, 0)
        info[4, n] = prev
        info[5, n] = jnp.maximum(prev, 0)
        info[6, n] = end
        info[7, n] = jnp.maximum(end, 0)


    @pl.loop(0, KV_PARTS)
    def _(part):
        key_copy(part).wait()

    lanes = iota((32, 128), 1)
    blank = jnp.zeros((16, 128), BF16)

    def chunk_copy(k):
        return pltpu.make_async_remote_copy(
            src_ref=s32.at[k, sib], dst_ref=r32.at[k],
            send_sem=s_chunk.at[k], recv_sem=r_chunk.at[k], device_id=sibling, device_id_type=MESH,
        )

    def peak_copy(k):
        return pltpu.make_async_remote_copy(
            src_ref=mx.at[k], dst_ref=mxr.at[k], send_sem=s_m.at[k], recv_sem=r_m.at[k],
            device_id=sibling, device_id_type=MESH,
        )

    def block_copy(k, at, to):
        return pltpu.make_async_remote_copy(
            src_ref=sb.at[turn(k), at], dst_ref=rb.at[y, spot], send_sem=b_sems.at[0, k], recv_sem=b_sems.at[1, k],
            device_id=to, device_id_type=MESH,
        )

    def side_copy(k, at, to):
        return pltpu.make_async_remote_copy(
            src_ref=ss.at[turn(k), at], dst_ref=rs.at[y, spot], send_sem=e_sems.at[0, k], recv_sem=e_sems.at[1, k],
            device_id=to, device_id_type=MESH,
        )

    def all_copy(buf, sems, k):
        block = buf.at[ys[(4 - SHIFT[k]) % 4], pl.ds(0, 16 if k else 15)]
        return pltpu.make_async_remote_copy(
            src_ref=block, dst_ref=block, send_sem=sems.at[0, k], recv_sem=sems.at[1, k],
            device_id=sibling, device_id_type=MESH,
        )

    def scores(k):
        cols = pl.ds(pl.multiple_of(turn(k) * 256, 256), 256)

        @pl.loop(0, SLOTS // GROUP, init_carry=jnp.full((32, 128), LOW, F32))
        def most(group, most):
            for e in range(GROUP):
                n = group * GROUP + e
                i, rl, count = info[1, n], info[2, n], info[3, n]
                parts = [gq[of, i, pl.ds(rl, 16, stride=8), :].reshape(2, 8, 128) for of in range(2)]
                heads = jnp.concatenate(parts, axis=1).astype(BF16)
                first = jnp.concatenate([heads[0], blank], axis=1)
                second = jnp.concatenate([blank, heads[1]], axis=1)
                score = lax.dot_general(
                    jnp.concatenate([first, second], axis=0), kvb[n, :, cols],
                    (((1,), (1,)), ((), ())), preferred_element_type=F32,
                )
                score = jnp.where(lanes < count, score * SCALE, LOW)
                peak = jnp.max(score, axis=1, keepdims=True)
                wb[n] = jnp.exp(score - peak).astype(BF16)
                pk[n] = jnp.broadcast_to(peak, (32, 128))
                most = jnp.where(lanes == info[0, n], jnp.maximum(most, peak), most)
            return most

        return most

    def values(k, most):
        cols = pl.ds(pl.multiple_of(1024 + turn(k) * 256, 256), 256)
        dn[...] = jnp.dot(
            wb[...].reshape(SLOTS * 32, 128), jnp.ones((128, 128), BF16), preferred_element_type=F32
        ).reshape(SLOTS, 32, 128)

        @pl.loop(0, SLOTS // GROUP, init_carry=jnp.zeros((32, 128), F32))
        def den(group, den):
            for e in range(GROUP):
                n = group * GROUP + e
                r = info[0, n]
                best = jnp.max(jnp.where(lanes == r, most, LOW), axis=1, keepdims=True)
                factor = jnp.exp(pk[n] - best)
                both = jnp.dot(wb[n], kvb[n, :, cols], preferred_element_type=F32)
                num = jnp.concatenate([both[:16, :128], both[16:, 128:]], axis=0)
                earlier = jnp.where(info[4, n] >= 0, cb[info[5, n]], 0.0)
                cb[n] = num * factor + earlier
                den = den + jnp.where(lanes == r, factor * dn[n], 0.0)
            return den

        mx[k, 0] = most
        mx[k, 1] = den
        peak_copy(k).start()

    def hand_on(k):
        for i in range(4):
            for rl in range(8):
                sums = jnp.where(info[6, i * 8 + rl] >= 0, cb[info[7, i * 8 + rl]], 0.0)
                for xh in range(2):
                    for of in range(2):
                        at = pl.ds(xh * 64 + rl, 8, stride=8)
                        s32[k, of, i, at, :] = sums[xh * 16 + of * 8 : xh * 16 + of * 8 + 8]

        chunk_copy(k).start()

    def merge(k):
        kt = turn(k)
        peak_copy(k).wait_recv()
        top, other = mx[k, 0], mxr[k, 0]
        chip_top = jnp.maximum(top, other)
        mine_f, other_f = jnp.exp(top - chip_top), jnp.exp(other - chip_top)
        chip_den = mx[k, 1] * mine_f + mxr[k, 1] * other_f
        mt[0:32, :] = chip_top
        mt[32:64, :] = chip_den
        for w in range(2):
            for xh in range(2):
                row = pl.multiple_of(w * 32 + xh * 16 + core * 8, 8)
                uw[w * 16 + xh * 8 : w * 16 + xh * 8 + 8, :] = mt[pl.ds(row, 8), :]
        lane4 = iota((4, 128), 1)
        packed = [jnp.zeros((4, 128), F32) for _ in range(4)]
        for w in range(2):
            for t in range(4):
                got = uw[pl.ds(w * 16 + t, 4, stride=4), :]
                to = w * 32 + t * 8
                for i in range(4):
                    there = pltpu.roll(got, (to - 8 * i) % 128, 1)
                    packed[i] = jnp.where((lane4 >= to) & (lane4 < to + 8), there, packed[i])
        for i in range(4):
            for j in range(4):
                ss[kt, i * 4 + j] = packed[i][j : j + 1, :]
        both_f = jnp.concatenate([mine_f, other_f, jnp.zeros((64, 128), F32)], axis=0).T
        lift[...] = pltpu.roll(both_f[0:32], (128 - core * 8) % 128, 1)
        chunk_copy(k).wait_recv()

        for i in range(4):
            factors = lift[i * 8 : i * 8 + 8, :]
            for j in range(4):
                total = []
                for t in range(4):
                    lane = (j // 2) * 16 + (j % 2) * 4 + t
                    at = slice(j * 32 + t * 8, j * 32 + t * 8 + 8)
                    total.append(
                        s32[k, core, i, at, :] * factors[:, lane : lane + 1]
                        + r32[k, i, at, :] * factors[:, 32 + lane : 33 + lane]
                    )
                sb[kt, i * 4 + j] = jnp.concatenate(total, axis=0).astype(BF16)

    def send(k):
        kt = turn(k)

        def one(e):
            pz, _, px = beside(e, kt)
            at, to = pz * 4 + px, place(pz, kt, px)
            block_copy(k, at, to).start()
            side_copy(k, at, to).start()

        for e in PLACES:
            one(e)

        @pl.when(k > 0)
        def _():
            one(0)

    def spread_fresh():
        @pl.when(core == 0)
        def _():
            fresh_wait(7).wait_recv()

        @pl.when(core == 1)
        def _():
            fresh_wait(8).wait_recv()

        for m in range(1, 4):
            fresh_plane(m).start()

    def pass_fresh():
        fresh_planes().wait_recv()
        sib_fresh(core).start()

    @pl.loop(0, 5)
    def _(k):
        @pl.when(k < 4)
        def _():
            sib_copy(k, sib).wait_recv()

            kt = turn(k)
            for of in range(2):
                for i in range(4):
                    for j in range(4):
                        gq[of, i, j * 32 : j * 32 + 32, :] = gat[of, kt, i * 4 + j].astype(F32)

            most = scores(k)

            @pl.when(k == 0)
            def _():
                arrived(1, ys[2], 15).wait_recv()
                sib_copy(1, core).start()

            @pl.when(k == 1)
            def _():
                for phase in (2, 3):
                    arrived(phase, ys[SHIFT[phase]], 16).wait_recv()
                    sib_copy(phase, core).start()

            @pl.when(k == 0)
            def _():
                @pl.loop(0, KV_PARTS)
                def _(part):
                    value_copy(part).wait()

            values(k, most)
            hand_on(k)

        @pl.when(k > 0)
        def _():
            merge(k - 1)
            send(k - 1)

        @pl.when(k == 1)
        def _():
            spread_fresh()

        @pl.when(k == 3)
        def _():
            pass_fresh()

    rb[y, spot] = sb[y, spot]
    rs[y, spot] = ss[y, spot]

    sib_fresh(sib).wait_recv()

    @pl.loop(0, 4)
    def _(i):
        for j in range(16):
            fresh = gnt[j // 4, j % 2, i * 2 + (j % 4) // 2].astype(F32)
            for of in range(2):
                gn[of, i, j * 8 : j * 8 + 8, :] = fresh[of * 8 : of * 8 + 8]

    @pl.loop(0, 4)
    def _(e):
        found_row = smeta[SLOTS + e, 0]
        which = jnp.maximum(found_row - 1, 0)
        late, r = which >> 5, which & 31
        pair = [gn[of, r >> 3, pl.ds(r & 7, 16, stride=8), :] for of in range(2)]
        tl[pl.ds(pl.multiple_of(e * 16, 16), 16), :] = jnp.where(found_row > 0, halves(pair[0], pair[1], late > 0), 0.0)
    for j in range(16):
        tail[:, j * 128 : j * 128 + 128] = tl[pl.ds(j, 4, stride=16), :].astype(BF16)

    head = y * 2 + x // 2
    new_rows = []
    for at in (head, head + 8):
        pair = [gn[of, z, pl.ds(pl.multiple_of(at * 8, 8), 8), :] for of in range(2)]
        new_rows.append([halves(pair[0], pair[1], late) for late in (False, True)])
    new_m, new_den, new_num = [], [], []
    for t in range(4):
        mine_q = q[t // 2].astype(F32)[:, (t % 2) * 128 : (t % 2) * 128 + 128]
        found_scores = [
            jnp.sum(mine_q * new_rows[0][j], axis=1, keepdims=True) * SCALE for j in range(t // 2 + 1)
        ]
        peak = found_scores[0]
        for more in found_scores[1:]:
            peak = jnp.maximum(peak, more)
        ws = [jnp.exp(v - peak).astype(BF16).astype(F32) for v in found_scores]
        new_m.append(peak)
        new_den.append(sum(ws[1:], ws[0]))
        num = ws[0] * new_rows[1][0]
        for j in range(1, len(ws)):
            num = num + ws[j] * new_rows[1][j]
        new_num.append(num)
    new_m = jnp.concatenate(new_m, axis=0)
    new_den = jnp.concatenate(new_den, axis=0)
    new_num = jnp.concatenate(new_num, axis=0)

    def take_in(phases, top, den, total):
        planes = [ys[(4 - SHIFT[k]) % 4] for k in phases]
        count = 16 * len(phases)
        for k in phases:
            all_copy(rs, e_sems, k).wait_recv()
        side = [rs[plane].reshape(16, 128) for plane in planes]
        side = jnp.concatenate(side + [jnp.zeros((128 - count, 128), F32)], axis=0).T
        side_m, side_den = side[0:32, :count], side[32:64, :count]
        new_top = jnp.maximum(jnp.max(side_m, axis=1, keepdims=True), top)
        scales = jnp.exp(side_m - new_top)
        old_scale = jnp.exp(top - new_top)
        den = jnp.sum(scales * side_den, axis=1, keepdims=True) + den * old_scale
        total = total * old_scale
        for k, plane in enumerate(planes):
            all_copy(rb, b_sems, phases[k]).wait_recv()
            for e in range(16):
                total = total + scales[:, k * 16 + e : k * 16 + e + 1] * rb[plane, e].astype(F32)
        return new_top, den, total

    state = take_in((0, 1, 2), new_m, new_den, new_num)
    _, final_den, total = take_in((3,), *state)
    result = total / final_den
    for t in range(4):
        out[t // 2, :, (t % 2) * 128 : (t % 2) * 128 + 128] = result[t * 8 : t * 8 + 8].astype(BF16)

    stores = [
        pltpu.make_async_copy(src, dst, io_sem.at[k])
        for k, (src, dst) in enumerate([(out, out_at), (tail, tail_at)])
    ]
    for store in stores:
        store.start()

    for k in range(4):
        all_copy(sb, b_sems, k).wait_send()
        all_copy(ss, e_sems, k).wait_send()
    across_copy().wait_send()
    arrived(0, y, 15).wait_send()
    arrived(1, y, 15).wait_send()
    for m in (3, 1):
        next_copy(m).wait_send()
    for k in range(4):
        sib_copy(k, core).wait_send()
        peak_copy(k).wait_send()
        chunk_copy(k).wait_send()
    pair_rows.wait_send()

    @pl.when(core == 0)
    def _():
        fresh_wait(7).wait_send()

    @pl.when(core == 1)
    def _():
        fresh_wait(8).wait_send()

    fresh_planes().wait_send()
    sib_fresh(core).wait_send()
    for store in stores:
        store.wait()


def hand_over(result, rows, out, tail, out_near, tail_near, sems):
    ways = [(result, out_near, out), (rows, tail_near, tail)]
    arrive = [pltpu.make_async_copy(a, b, sems.at[k]) for k, (a, b, _) in enumerate(ways)]
    leave = [pltpu.make_async_copy(b, c, sems.at[k]) for k, (_, b, c) in enumerate(ways)]
    for copy in arrive:
        copy.start()
    for first, second in zip(arrive, leave):
        first.wait()
        second.start()
    for copy in leave:
        copy.wait()


def per_device(kv_pool, queries, new_kv, lengths, block_dev, block_slot, owner_dev, owner_row):
    anywhere = pl.BlockSpec(memory_space=pltpu.HBM)
    dma = pltpu.SemaphoreType.DMA
    result, tail = pl.pallas_call(
        kernel,
        out_shape=(
            jax.ShapeDtypeStruct((2, 8, 256), BF16),
            jax.ShapeDtypeStruct((4, 2048), BF16),
        ),
        in_specs=[anywhere] * 8,
        out_specs=(anywhere, anywhere),
        scratch_shapes=[
            pltpu.VMEM((2, 8, 256), BF16),
            pltpu.VMEM((2, 8, 64), BF16),
            pltpu.VMEM((REQS, 128), I32),
            pltpu.VMEM((REQS, 128), I32),
            pltpu.VMEM((2, REQS), I32),
            pltpu.VMEM((2, REQS), I32),
            pltpu.SMEM((REQS,), I32),
            pltpu.VMEM((2, 8, 256), BF16),
            pltpu.VMEM((4, 2048), BF16),
            pltpu.SMEM((8, SLOTS), I32),
            pltpu.VMEM((SLOTS, 128, 2048), BF16),
            pltpu.VMEM((2, 4, 16, 32, 128), BF16),
            pltpu.VMEM((2, 8, 128), F32),
            pltpu.VMEM((16, 128), BF16),
            pltpu.VMEM((4, 2, 8, 16, 128), BF16),
            pltpu.VMEM((2, 4, 128, 128), F32),
            pltpu.VMEM((2, 4, 128, 128), F32),
            pltpu.VMEM((SLOTS, 32, 128), BF16),
            pltpu.VMEM((SLOTS, 32, 128), F32),
            pltpu.VMEM((SLOTS, 32, 128), F32),
            pltpu.VMEM((SLOTS, 32, 128), F32),
            pltpu.VMEM((4, 2, 32, 128), F32),
            pltpu.VMEM((4, 2, 32, 128), F32),
            pltpu.VMEM((64, 128), F32),
            pltpu.VMEM((32, 128), F32),
            pltpu.VMEM((32, 128), F32),
            pltpu.VMEM((4, 2, 4, 128, 128), F32),
            pltpu.VMEM((4, 4, 128, 128), F32),
            pltpu.VMEM((4, 16, 32, 128), BF16),
            pltpu.VMEM((4, 16, 32, 128), BF16),
            pltpu.VMEM((4, 16, 1, 128), F32),
            pltpu.VMEM((4, 16, 1, 128), F32),
            pltpu.VMEM((64, 128), F32),
            pltpu.VMEM((40, 128), I32),
            pltpu.SMEM((40, 128), I32),
            pltpu.VMEM((40, 128), I32),
            dma((KV_PARTS,)),
            dma((KV_PARTS,)),
            dma((5,)),
            dma((5,)),
            dma((4,)),
            dma((4,)),
            dma((8,)),
            dma((4,)),
            dma((4,)),
            dma((4,)),
            dma((4,)),
            dma((2, 4)),
            dma((2, 4)),
            dma,
            dma((7,)),
        ],
        compiler_params=pltpu.CompilerParams(
            collective_id=0, has_side_effects=True, vmem_limit_bytes=56 * 1024 * 1024
        ),
    )(kv_pool, queries, new_kv, block_dev, block_slot, owner_dev, owner_row, lengths)
    return pl.pallas_call(
        hand_over,
        out_shape=(
            jax.ShapeDtypeStruct((2, 8, 256), BF16),
            jax.ShapeDtypeStruct((4, 2048), BF16),
        ),
        in_specs=[anywhere] * 2,
        out_specs=(anywhere, anywhere),
        scratch_shapes=[pltpu.VMEM((2, 8, 256), BF16), pltpu.VMEM((4, 2048), BF16), dma((2,))],
    )(result, tail)


def solution(mesh):
    placed = (
        P(("inst", "seq"), None, None),
        P(None, "inst", "seq"),
        P(None, "inst", "seq"),
        P(),
        P(),
        P(),
        P(),
        P(),
    )
    return jax.shard_map(
        per_device,
        mesh=mesh,
        in_specs=placed,
        out_specs=(P(None, "inst", "seq"), P(("inst", "seq"), None)),
        check_vma=False,
    )
```

```python
import math

import jax
import jax.numpy as jnp
from jax import lax
from jax.experimental import pallas as pl
from jax.experimental.pallas import tpu as pltpu
from jax.sharding import PartitionSpec as P

MESH = pl.DeviceIdType.MESH
F32 = jnp.float32
BF16 = jnp.bfloat16
I32 = jnp.int32

N = 4
CHIPS = 64
SLOTS = 32
REQS = 32
LOW = -1e30
SCALE = 1.0 / math.sqrt(128)
UNROLL = 4
GROUP = 32
SHIFT = (0, 2, 1, 3)
PLACES = (10, 9, 11, 6, 14, 2, 8, 5, 7, 13, 15, 1, 3, 4, 12)
KV_PARTS = SLOTS // UNROLL


def iota(shape, dim):
    return lax.broadcasted_iota(I32, shape, dim)


def halves(first, second, late):
    lane = iota(first.shape, 1)
    if late is True:
        return jnp.where(lane < 64, pltpu.roll(first, 64, 1), second)
    if late is False:
        return jnp.where(lane < 64, first, pltpu.roll(second, 64, 1))
    low = jnp.where(late, pltpu.roll(first, 64, 1), first)
    high = jnp.where(late, second, pltpu.roll(second, 64, 1))
    return jnp.where(lane < 64, low, high)


def kernel(
    kv, q_in, nk_in, dev_in, slot_in, own_dev_in, own_row_in, lens_in, out_at, tail_at,
    q, nk, dev, slot, own_dev, own_row, lens, out, tail,
    info, kvb, gat, nx, tile, gnt, gq, gn, wb, pk, dn, cb, mx, mxr, mt, lift, uw, s32, r32, sb, rb, ss, rs, tl, meta, smeta, codes,
    k_sem, v_sem, sg, rg, s_sib, r_sib, n_sems, s_m, r_m, s_chunk, r_chunk, b_sems, e_sems, meta_sem, io_sem,
):
    z = lax.axis_index("inst")
    c = lax.axis_index("seq")
    y, x, core = c >> 3, (c >> 1) & 3, c & 1
    zs, ys, xs = [[(v + d) & 3 for d in range(4)] for v in (z, y, x)]
    me = z * 32 + c
    chip = z * 16 + y * 4 + x
    sib = 1 - core
    sibling = (z, y * 8 + x * 2 + sib)

    def place(pz, py, px):
        return (pz, py * 8 + px * 2 + core)

    loads = [
        pltpu.make_async_copy(src, dst, io_sem.at[k])
        for k, (src, dst) in enumerate([
            (q_in, q), (nk_in, nk), (dev_in, dev), (slot_in, slot),
            (own_dev_in, own_dev), (own_row_in, own_row), (lens_in, lens),
        ])
    ]
    for load in loads[:2]:
        load.start()

    def beside(e, py):
        return zs[e // 4], py, xs[e % 4]

    barrier = pltpu.get_barrier_semaphore()

    for e in PLACES:
        pl.semaphore_signal(barrier, inc=1, device_id=place(*beside(e, y)), device_id_type=MESH)
    for m in range(1, 4):
        pl.semaphore_signal(barrier, inc=1, device_id=place(z, ys[m], x), device_id_type=MESH)
    pl.semaphore_signal(barrier, inc=1, device_id=sibling, device_id_type=MESH)
    for load in loads[2:]:
        load.start()

    def key_copy(part):
        span = pl.ds(part * UNROLL, UNROLL)
        cols = pl.ds(0, 1024)
        return pltpu.make_async_copy(kv.at[span, :, cols], kvb.at[span, :, cols], k_sem.at[part])

    def value_copy(part):
        span = pl.ds(part * UNROLL, UNROLL)
        cols = pl.ds(1024, 1024)
        return pltpu.make_async_copy(kv.at[span, :, cols], kvb.at[span, :, cols], v_sem.at[part])

    spot = z * 4 + x
    for load in loads[:2]:
        load.wait()
    own = [q[s].astype(F32) for s in range(2)]
    gat[core, y, spot] = jnp.concatenate(
        [own[0][:, :128], own[0][:, 128:], own[1][:, :128], own[1][:, 128:]], axis=0
    ).astype(BF16)
    nx[0] = jnp.concatenate([nk[0].astype(F32), nk[1].astype(F32)], axis=1)

    pl.semaphore_wait(barrier, 19)

    def turn(k):
        return (y + ((k & 1) << 1) + (k >> 1)) & 3

    def push(block, k, to):
        return pltpu.make_async_remote_copy(
            src_ref=block, dst_ref=block, send_sem=sg.at[k], recv_sem=rg.at[k],
            device_id=to, device_id_type=MESH,
        )

    def plane_copy(e):
        return push(gat.at[core, y, spot], 0, place(*beside(e, y)))

    def across_copy():
        return push(gat.at[core, y, spot], 4, place(z, ys[2], x))

    def relay_copy(e):
        return push(gat.at[core, ys[2], spot], 1, place(*beside(e, y)))

    def next_copy(m):
        return push(gat.at[core, y], 2 if m == 3 else 3, place(z, ys[m], x))

    def arrived(k, plane, blocks):
        return push(gat.at[core, plane, pl.ds(0, blocks)], k, sibling)

    def sib_copy(k, of):
        block = gat.at[of, turn(k)]
        return pltpu.make_async_remote_copy(
            src_ref=block, dst_ref=block, send_sem=s_sib.at[k], recv_sem=r_sib.at[k],
            device_id=sibling, device_id_type=MESH,
        )

    across_copy().start()

    for e in PLACES:
        plane_copy(e).start()

    @pl.loop(0, KV_PARTS)
    def _(part):
        key_copy(part).start()

    pair_rows = pltpu.make_async_remote_copy(
        src_ref=nx.at[0], dst_ref=nx.at[1], send_sem=n_sems.at[0], recv_sem=n_sems.at[1],
        device_id=sibling, device_id_type=MESH,
    )
    pair_rows.start()
    shelf = z * 2 + (x >> 1)
    side_of = (x + core) & 1

    def fresh_copy(e):
        return pltpu.make_async_remote_copy(
            src_ref=tile, dst_ref=gnt.at[y, x & 1, shelf], send_sem=n_sems.at[2], recv_sem=n_sems.at[3],
            device_id=place(*beside(e, y)), device_id_type=MESH,
        )

    def fresh_wait(tiles):
        block = gnt.at[y, side_of, pl.ds(0, tiles)]
        return pltpu.make_async_remote_copy(
            src_ref=block, dst_ref=block, send_sem=n_sems.at[2], recv_sem=n_sems.at[3],
            device_id=sibling, device_id_type=MESH,
        )

    def fresh_plane(m):
        block = gnt.at[y, side_of]
        return pltpu.make_async_remote_copy(
            src_ref=block, dst_ref=block, send_sem=n_sems.at[4], recv_sem=n_sems.at[5],
            device_id=place(z, ys[m], x), device_id_type=MESH,
        )

    def fresh_planes():
        block = gnt.at[pl.ds(0, 3), side_of]
        return pltpu.make_async_remote_copy(
            src_ref=block, dst_ref=block, send_sem=n_sems.at[4], recv_sem=n_sems.at[5],
            device_id=sibling, device_id_type=MESH,
        )

    def sib_fresh(of):
        block = gnt.at[:, (x + of) & 1]
        return pltpu.make_async_remote_copy(
            src_ref=block, dst_ref=block, send_sem=n_sems.at[6], recv_sem=n_sems.at[7],
            device_id=sibling, device_id_type=MESH,
        )

    @pl.loop(0, KV_PARTS)
    def _(part):
        value_copy(part).start()

    for load in loads[2:]:
        load.wait()
    mine = jnp.where(dev[...] == me, slot[...], -1)
    code = iota((REQS, 128), 0) * 128 + iota((REQS, 128), 1) + 1

    @pl.loop(0, SLOTS // 4)
    def _(group):
        for e in range(4):
            n = group * 4 + e
            codes[pl.ds(n, 1), :] = jnp.sum(jnp.where(mine == n, code, 0), axis=0, keepdims=True)

    owned = jnp.where(own_dev[...] == me, own_row[...], -1)
    row_code = iota((2, REQS), 0) * REQS + iota((2, REQS), 1) + 1
    pad_row = jnp.zeros((1, 96), I32)
    for e in range(4):
        hit = jnp.sum(jnp.where(owned == e, row_code, 0), axis=0, keepdims=True)
        codes[SLOTS + e : SLOTS + e + 1, :] = jnp.concatenate([hit, pad_row], axis=1)
    codes[SLOTS + 4 :, :] = jnp.zeros((4, 128), I32)

    found = jnp.broadcast_to(jnp.sum(codes[...], axis=1, keepdims=True), (40, 128))
    held = found[:SLOTS]
    req_col = jnp.where(held > 0, jnp.minimum((held - 1) >> 7, REQS - 1), -1)
    rows, lanes = iota((SLOTS, 128), 0), iota((SLOTS, 128), 1)
    req_row = jnp.sum(jnp.where(rows == lanes, req_col, 0), axis=0, keepdims=True)
    req_row = jnp.where(lanes < SLOTS, jnp.broadcast_to(req_row, (SLOTS, 128)), -2)
    before = jnp.max(jnp.where((req_row == req_col) & (lanes < rows), lanes, -1), axis=1, keepdims=True)
    last = jnp.max(jnp.where(req_row == rows, lanes, -1), axis=1, keepdims=True)
    meta[:SLOTS] = jnp.where(
        lanes == 0, req_col, jnp.where(lanes == 1, held, jnp.where(lanes == 2, before, last))
    )
    meta[SLOTS:] = found[SLOTS:]
    meta_copy = pltpu.make_async_copy(meta, smeta, meta_sem)
    meta_copy.start()

    pair_rows.wait_recv()
    both_rows = [jnp.where(core == of, nx[0], nx[1]) for of in range(2)]
    tile[...] = jnp.concatenate(both_rows, axis=0).astype(BF16)

    @pl.when(core == 0)
    def _():
        gnt[y, x & 1, shelf] = tile[...]

    push(gat.at[core, ys[2], spot], 4, sibling).wait_recv()

    for e in PLACES:
        relay_copy(e).start()

    arrived(0, y, 15).wait_recv()
    sib_copy(0, core).start()
    for m in (3, 1):
        next_copy(m).start()

    for of in range(2):
        @pl.when(core == of)
        def _():
            for e in range(2 - of, 16, 2):
                fresh_copy(e).start()

    meta_copy.wait()

    @pl.loop(0, SLOTS)
    def _(n):
        req, held, prev, end = smeta[n, 0], smeta[n, 1], smeta[n, 2], smeta[n, 3]
        r = jnp.maximum(req, 0)
        b = (jnp.maximum(held, 1) - 1) & 127
        info[0, n] = req
        info[1, n] = r >> 3
        info[2, n] = r & 7
        info[3, n] = jnp.where(held > 0, lens[r] - b * 128, 0)
        info[4, n] = prev
        info[5, n] = jnp.maximum(prev, 0)
        info[6, n] = end
        info[7, n] = jnp.maximum(end, 0)


    @pl.loop(0, KV_PARTS)
    def _(part):
        key_copy(part).wait()

    lanes = iota((32, 128), 1)
    blank = jnp.zeros((16, 128), BF16)

    def chunk_copy(k):
        return pltpu.make_async_remote_copy(
            src_ref=s32.at[k, sib], dst_ref=r32.at[k],
            send_sem=s_chunk.at[k], recv_sem=r_chunk.at[k], device_id=sibling, device_id_type=MESH,
        )

    def peak_copy(k):
        return pltpu.make_async_remote_copy(
            src_ref=mx.at[k], dst_ref=mxr.at[k], send_sem=s_m.at[k], recv_sem=r_m.at[k],
            device_id=sibling, device_id_type=MESH,
        )

    def block_copy(k, at, to):
        return pltpu.make_async_remote_copy(
            src_ref=sb.at[turn(k), at], dst_ref=rb.at[y, spot], send_sem=b_sems.at[0, k], recv_sem=b_sems.at[1, k],
            device_id=to, device_id_type=MESH,
        )

    def side_copy(k, at, to):
        return pltpu.make_async_remote_copy(
            src_ref=ss.at[turn(k), at], dst_ref=rs.at[y, spot], send_sem=e_sems.at[0, k], recv_sem=e_sems.at[1, k],
            device_id=to, device_id_type=MESH,
        )

    def all_copy(buf, sems, k):
        block = buf.at[ys[(4 - SHIFT[k]) % 4], pl.ds(0, 16 if k else 15)]
        return pltpu.make_async_remote_copy(
            src_ref=block, dst_ref=block, send_sem=sems.at[0, k], recv_sem=sems.at[1, k],
            device_id=sibling, device_id_type=MESH,
        )

    def scores(k):
        cols = pl.ds(pl.multiple_of(turn(k) * 256, 256), 256)

        @pl.loop(0, SLOTS // GROUP, init_carry=jnp.full((32, 128), LOW, F32))
        def most(group, most):
            for e in range(GROUP):
                n = group * GROUP + e
                i, rl, count = info[1, n], info[2, n], info[3, n]
                parts = [gq[of, i, pl.ds(rl, 16, stride=8), :].reshape(2, 8, 128) for of in range(2)]
                heads = jnp.concatenate(parts, axis=1).astype(BF16)
                first = jnp.concatenate([heads[0], blank], axis=1)
                second = jnp.concatenate([blank, heads[1]], axis=1)
                score = lax.dot_general(
                    jnp.concatenate([first, second], axis=0), kvb[n, :, cols],
                    (((1,), (1,)), ((), ())), preferred_element_type=F32,
                )
                score = jnp.where(lanes < count, score * SCALE, LOW)
                peak = jnp.max(score, axis=1, keepdims=True)
                wb[n] = jnp.exp(score - peak).astype(BF16)
                pk[n] = jnp.broadcast_to(peak, (32, 128))
                most = jnp.where(lanes == info[0, n], jnp.maximum(most, peak), most)
            return most

        return most

    def values(k, most):
        cols = pl.ds(pl.multiple_of(1024 + turn(k) * 256, 256), 256)
        dn[...] = jnp.dot(
            wb[...].reshape(SLOTS * 32, 128), jnp.ones((128, 128), BF16), preferred_element_type=F32
        ).reshape(SLOTS, 32, 128)

        @pl.loop(0, SLOTS // GROUP, init_carry=jnp.zeros((32, 128), F32))
        def den(group, den):
            for e in range(GROUP):
                n = group * GROUP + e
                r = info[0, n]
                best = jnp.max(jnp.where(lanes == r, most, LOW), axis=1, keepdims=True)
                factor = jnp.exp(pk[n] - best)
                both = jnp.dot(wb[n], kvb[n, :, cols], preferred_element_type=F32)
                num = jnp.concatenate([both[:16, :128], both[16:, 128:]], axis=0)
                earlier = jnp.where(info[4, n] >= 0, cb[info[5, n]], 0.0)
                cb[n] = num * factor + earlier
                den = den + jnp.where(lanes == r, factor * dn[n], 0.0)
            return den

        mx[k, 0] = most
        mx[k, 1] = den
        peak_copy(k).start()

    def hand_on(k):
        for i in range(4):
            for rl in range(8):
                sums = jnp.where(info[6, i * 8 + rl] >= 0, cb[info[7, i * 8 + rl]], 0.0)
                for xh in range(2):
                    for of in range(2):
                        at = pl.ds(xh * 64 + rl, 8, stride=8)
                        s32[k, of, i, at, :] = sums[xh * 16 + of * 8 : xh * 16 + of * 8 + 8]

        chunk_copy(k).start()

    def merge(k):
        kt = turn(k)
        peak_copy(k).wait_recv()
        top, other = mx[k, 0], mxr[k, 0]
        chip_top = jnp.maximum(top, other)
        mine_f, other_f = jnp.exp(top - chip_top), jnp.exp(other - chip_top)
        chip_den = mx[k, 1] * mine_f + mxr[k, 1] * other_f
        mt[0:32, :] = chip_top
        mt[32:64, :] = chip_den
        for w in range(2):
            for xh in range(2):
                row = pl.multiple_of(w * 32 + xh * 16 + core * 8, 8)
                uw[w * 16 + xh * 8 : w * 16 + xh * 8 + 8, :] = mt[pl.ds(row, 8), :]
        lane4 = iota((4, 128), 1)
        packed = [jnp.zeros((4, 128), F32) for _ in range(4)]
        for w in range(2):
            for t in range(4):
                got = uw[pl.ds(w * 16 + t, 4, stride=4), :]
                to = w * 32 + t * 8
                for i in range(4):
                    there = pltpu.roll(got, (to - 8 * i) % 128, 1)
                    packed[i] = jnp.where((lane4 >= to) & (lane4 < to + 8), there, packed[i])
        for i in range(4):
            for j in range(4):
                ss[kt, i * 4 + j] = packed[i][j : j + 1, :]
        both_f = jnp.concatenate([mine_f, other_f, jnp.zeros((64, 128), F32)], axis=0).T
        lift[...] = pltpu.roll(both_f[0:32], (128 - core * 8) % 128, 1)
        chunk_copy(k).wait_recv()

        for i in range(4):
            factors = lift[i * 8 : i * 8 + 8, :]
            for j in range(4):
                total = []
                for t in range(4):
                    lane = (j // 2) * 16 + (j % 2) * 4 + t
                    at = slice(j * 32 + t * 8, j * 32 + t * 8 + 8)
                    total.append(
                        s32[k, core, i, at, :] * factors[:, lane : lane + 1]
                        + r32[k, i, at, :] * factors[:, 32 + lane : 33 + lane]
                    )
                sb[kt, i * 4 + j] = jnp.concatenate(total, axis=0).astype(BF16)

    def send(k):
        kt = turn(k)

        def one(e):
            pz, _, px = beside(e, kt)
            at, to = pz * 4 + px, place(pz, kt, px)
            block_copy(k, at, to).start()
            side_copy(k, at, to).start()

        for e in PLACES:
            one(e)

        @pl.when(k > 0)
        def _():
            one(0)

    def spread_fresh():
        @pl.when(core == 0)
        def _():
            fresh_wait(7).wait_recv()

        @pl.when(core == 1)
        def _():
            fresh_wait(8).wait_recv()

        for m in range(1, 4):
            fresh_plane(m).start()

    def pass_fresh():
        fresh_planes().wait_recv()
        sib_fresh(core).start()

    @pl.loop(0, 5)
    def _(k):
        @pl.when(k < 4)
        def _():
            kt = turn(k)

            def widen(of):
                for i in range(4):
                    for j in range(4):
                        gq[of, i, j * 32 : j * 32 + 32, :] = gat[of, kt, i * 4 + j].astype(F32)

            widen(core)
            sib_copy(k, sib).wait_recv()
            widen(sib)
            most = scores(k)

            @pl.when(k == 0)
            def _():
                arrived(1, ys[2], 15).wait_recv()
                sib_copy(1, core).start()

            @pl.when(k == 1)
            def _():
                for phase in (2, 3):
                    arrived(phase, ys[SHIFT[phase]], 16).wait_recv()
                    sib_copy(phase, core).start()

            @pl.when(k == 0)
            def _():
                @pl.loop(0, KV_PARTS)
                def _(part):
                    value_copy(part).wait()

            values(k, most)
            hand_on(k)

        @pl.when(k > 0)
        def _():
            merge(k - 1)
            send(k - 1)

        @pl.when(k == 1)
        def _():
            spread_fresh()

        @pl.when(k == 3)
        def _():
            pass_fresh()

    rb[y, spot] = sb[y, spot]
    rs[y, spot] = ss[y, spot]

    sib_fresh(sib).wait_recv()

    @pl.loop(0, 4)
    def _(i):
        for j in range(16):
            fresh = gnt[j // 4, j % 2, i * 2 + (j % 4) // 2].astype(F32)
            for of in range(2):
                gn[of, i, j * 8 : j * 8 + 8, :] = fresh[of * 8 : of * 8 + 8]

    @pl.loop(0, 4)
    def _(e):
        found_row = smeta[SLOTS + e, 0]
        which = jnp.maximum(found_row - 1, 0)
        late, r = which >> 5, which & 31
        pair = [gn[of, r >> 3, pl.ds(r & 7, 16, stride=8), :] for of in range(2)]
        tl[pl.ds(pl.multiple_of(e * 16, 16), 16), :] = jnp.where(found_row > 0, halves(pair[0], pair[1], late > 0), 0.0)
    for j in range(16):
        tail[:, j * 128 : j * 128 + 128] = tl[pl.ds(j, 4, stride=16), :].astype(BF16)

    head = y * 2 + x // 2
    new_rows = []
    for at in (head, head + 8):
        pair = [gn[of, z, pl.ds(pl.multiple_of(at * 8, 8), 8), :] for of in range(2)]
        new_rows.append([halves(pair[0], pair[1], late) for late in (False, True)])
    new_m, new_den, new_num = [], [], []
    for t in range(4):
        mine_q = q[t // 2].astype(F32)[:, (t % 2) * 128 : (t % 2) * 128 + 128]
        found_scores = [
            jnp.sum(mine_q * new_rows[0][j], axis=1, keepdims=True) * SCALE for j in range(t // 2 + 1)
        ]
        peak = found_scores[0]
        for more in found_scores[1:]:
            peak = jnp.maximum(peak, more)
        ws = [jnp.exp(v - peak).astype(BF16).astype(F32) for v in found_scores]
        new_m.append(peak)
        new_den.append(sum(ws[1:], ws[0]))
        num = ws[0] * new_rows[1][0]
        for j in range(1, len(ws)):
            num = num + ws[j] * new_rows[1][j]
        new_num.append(num)
    new_m = jnp.concatenate(new_m, axis=0)
    new_den = jnp.concatenate(new_den, axis=0)
    new_num = jnp.concatenate(new_num, axis=0)

    def take_in(phases, top, den, total):
        planes = [ys[(4 - SHIFT[k]) % 4] for k in phases]
        count = 16 * len(phases)
        for k in phases:
            all_copy(rs, e_sems, k).wait_recv()
        side = [rs[plane].reshape(16, 128) for plane in planes]
        side = jnp.concatenate(side + [jnp.zeros((128 - count, 128), F32)], axis=0).T
        side_m, side_den = side[0:32, :count], side[32:64, :count]
        new_top = jnp.maximum(jnp.max(side_m, axis=1, keepdims=True), top)
        scales = jnp.exp(side_m - new_top)
        old_scale = jnp.exp(top - new_top)
        den = jnp.sum(scales * side_den, axis=1, keepdims=True) + den * old_scale
        total = total * old_scale
        for k, plane in enumerate(planes):
            all_copy(rb, b_sems, phases[k]).wait_recv()
            for e in range(16):
                total = total + scales[:, k * 16 + e : k * 16 + e + 1] * rb[plane, e].astype(F32)
        return new_top, den, total

    state = take_in((0, 1, 2), new_m, new_den, new_num)
    _, final_den, total = take_in((3,), *state)
    result = total / final_den
    for t in range(4):
        out[t // 2, :, (t % 2) * 128 : (t % 2) * 128 + 128] = result[t * 8 : t * 8 + 8].astype(BF16)

    stores = [
        pltpu.make_async_copy(src, dst, io_sem.at[k])
        for k, (src, dst) in enumerate([(out, out_at), (tail, tail_at)])
    ]
    for store in stores:
        store.start()

    for k in range(4):
        all_copy(sb, b_sems, k).wait_send()
        all_copy(ss, e_sems, k).wait_send()
    across_copy().wait_send()
    arrived(0, y, 15).wait_send()
    arrived(1, y, 15).wait_send()
    for m in (3, 1):
        next_copy(m).wait_send()
    for k in range(4):
        sib_copy(k, core).wait_send()
        peak_copy(k).wait_send()
        chunk_copy(k).wait_send()
    pair_rows.wait_send()

    @pl.when(core == 0)
    def _():
        fresh_wait(7).wait_send()

    @pl.when(core == 1)
    def _():
        fresh_wait(8).wait_send()

    fresh_planes().wait_send()
    sib_fresh(core).wait_send()
    for store in stores:
        store.wait()


def hand_over(result, rows, out, tail, out_near, tail_near, sems):
    ways = [(result, out_near, out), (rows, tail_near, tail)]
    arrive = [pltpu.make_async_copy(a, b, sems.at[k]) for k, (a, b, _) in enumerate(ways)]
    leave = [pltpu.make_async_copy(b, c, sems.at[k]) for k, (_, b, c) in enumerate(ways)]
    for copy in arrive:
        copy.start()
    for first, second in zip(arrive, leave):
        first.wait()
        second.start()
    for copy in leave:
        copy.wait()


def per_device(kv_pool, queries, new_kv, lengths, block_dev, block_slot, owner_dev, owner_row):
    anywhere = pl.BlockSpec(memory_space=pltpu.HBM)
    dma = pltpu.SemaphoreType.DMA
    result, tail = pl.pallas_call(
        kernel,
        out_shape=(
            jax.ShapeDtypeStruct((2, 8, 256), BF16),
            jax.ShapeDtypeStruct((4, 2048), BF16),
        ),
        in_specs=[anywhere] * 8,
        out_specs=(anywhere, anywhere),
        scratch_shapes=[
            pltpu.VMEM((2, 8, 256), BF16),
            pltpu.VMEM((2, 8, 64), BF16),
            pltpu.VMEM((REQS, 128), I32),
            pltpu.VMEM((REQS, 128), I32),
            pltpu.VMEM((2, REQS), I32),
            pltpu.VMEM((2, REQS), I32),
            pltpu.SMEM((REQS,), I32),
            pltpu.VMEM((2, 8, 256), BF16),
            pltpu.VMEM((4, 2048), BF16),
            pltpu.SMEM((8, SLOTS), I32),
            pltpu.VMEM((SLOTS, 128, 2048), BF16),
            pltpu.VMEM((2, 4, 16, 32, 128), BF16),
            pltpu.VMEM((2, 8, 128), F32),
            pltpu.VMEM((16, 128), BF16),
            pltpu.VMEM((4, 2, 8, 16, 128), BF16),
            pltpu.VMEM((2, 4, 128, 128), F32),
            pltpu.VMEM((2, 4, 128, 128), F32),
            pltpu.VMEM((SLOTS, 32, 128), BF16),
            pltpu.VMEM((SLOTS, 32, 128), F32),
            pltpu.VMEM((SLOTS, 32, 128), F32),
            pltpu.VMEM((SLOTS, 32, 128), F32),
            pltpu.VMEM((4, 2, 32, 128), F32),
            pltpu.VMEM((4, 2, 32, 128), F32),
            pltpu.VMEM((64, 128), F32),
            pltpu.VMEM((32, 128), F32),
            pltpu.VMEM((32, 128), F32),
            pltpu.VMEM((4, 2, 4, 128, 128), F32),
            pltpu.VMEM((4, 4, 128, 128), F32),
            pltpu.VMEM((4, 16, 32, 128), BF16),
            pltpu.VMEM((4, 16, 32, 128), BF16),
            pltpu.VMEM((4, 16, 1, 128), F32),
            pltpu.VMEM((4, 16, 1, 128), F32),
            pltpu.VMEM((64, 128), F32),
            pltpu.VMEM((40, 128), I32),
            pltpu.SMEM((40, 128), I32),
            pltpu.VMEM((40, 128), I32),
            dma((KV_PARTS,)),
            dma((KV_PARTS,)),
            dma((5,)),
            dma((5,)),
            dma((4,)),
            dma((4,)),
            dma((8,)),
            dma((4,)),
            dma((4,)),
            dma((4,)),
            dma((4,)),
            dma((2, 4)),
            dma((2, 4)),
            dma,
            dma((7,)),
        ],
        compiler_params=pltpu.CompilerParams(
            collective_id=0, has_side_effects=True, vmem_limit_bytes=56 * 1024 * 1024
        ),
    )(kv_pool, queries, new_kv, block_dev, block_slot, owner_dev, owner_row, lengths)
    return pl.pallas_call(
        hand_over,
        out_shape=(
            jax.ShapeDtypeStruct((2, 8, 256), BF16),
            jax.ShapeDtypeStruct((4, 2048), BF16),
        ),
        in_specs=[anywhere] * 2,
        out_specs=(anywhere, anywhere),
        scratch_shapes=[pltpu.VMEM((2, 8, 256), BF16), pltpu.VMEM((4, 2048), BF16), dma((2,))],
    )(result, tail)


def solution(mesh):
    placed = (
        P(("inst", "seq"), None, None),
        P(None, "inst", "seq"),
        P(None, "inst", "seq"),
        P(),
        P(),
        P(),
        P(),
        P(),
    )
    return jax.shard_map(
        per_device,
        mesh=mesh,
        in_specs=placed,
        out_specs=(P(None, "inst", "seq"), P(("inst", "seq"), None)),
        check_vma=False,
    )
```

```python
import math

import jax
import jax.numpy as jnp
from jax import lax
from jax.experimental import pallas as pl
from jax.experimental.pallas import tpu as pltpu
from jax.sharding import PartitionSpec as P

MESH = pl.DeviceIdType.MESH
F32 = jnp.float32
BF16 = jnp.bfloat16
I32 = jnp.int32

N = 4
CHIPS = 64
SLOTS = 32
REQS = 32
LOW = -1e30
SCALE = 1.0 / math.sqrt(128)
UNROLL = 4
GROUP = 32
SHIFT = (0, 2, 1, 3)
PLACES = (10, 9, 11, 6, 14, 2, 8, 5, 7, 13, 15, 1, 3, 4, 12)
KV_PARTS = SLOTS // UNROLL


def iota(shape, dim):
    return lax.broadcasted_iota(I32, shape, dim)


def halves(first, second, late):
    lane = iota(first.shape, 1)
    if late is True:
        return jnp.where(lane < 64, pltpu.roll(first, 64, 1), second)
    if late is False:
        return jnp.where(lane < 64, first, pltpu.roll(second, 64, 1))
    low = jnp.where(late, pltpu.roll(first, 64, 1), first)
    high = jnp.where(late, second, pltpu.roll(second, 64, 1))
    return jnp.where(lane < 64, low, high)


def kernel(
    kv, q_in, nk_in, dev_in, slot_in, own_dev_in, own_row_in, lens_in, out_at, tail_at,
    q, nk, dev, slot, own_dev, own_row, lens, out, tail,
    info, kvb, gat, nx, tile, gnt, gq, gn, wb, pk, dn, cb, cb2, mx, mxr, mt, lift, uw, s32, r32, sb, rb, ss, rs, tl, meta, smeta, codes,
    k_sem, v_sem, sg, rg, s_sib, r_sib, n_sems, s_m, r_m, s_chunk, r_chunk, b_sems, e_sems, meta_sem, io_sem,
):
    z = lax.axis_index("inst")
    c = lax.axis_index("seq")
    y, x, core = c >> 3, (c >> 1) & 3, c & 1
    zs, ys, xs = [[(v + d) & 3 for d in range(4)] for v in (z, y, x)]
    me = z * 32 + c
    chip = z * 16 + y * 4 + x
    sib = 1 - core
    sibling = (z, y * 8 + x * 2 + sib)

    def place(pz, py, px):
        return (pz, py * 8 + px * 2 + core)

    loads = [
        pltpu.make_async_copy(src, dst, io_sem.at[k])
        for k, (src, dst) in enumerate([
            (q_in, q), (nk_in, nk), (dev_in, dev), (slot_in, slot),
            (own_dev_in, own_dev), (own_row_in, own_row), (lens_in, lens),
        ])
    ]
    for load in loads[:2]:
        load.start()

    def beside(e, py):
        return zs[e // 4], py, xs[e % 4]

    barrier = pltpu.get_barrier_semaphore()

    for e in PLACES:
        pl.semaphore_signal(barrier, inc=1, device_id=place(*beside(e, y)), device_id_type=MESH)
    for m in range(1, 4):
        pl.semaphore_signal(barrier, inc=1, device_id=place(z, ys[m], x), device_id_type=MESH)
    pl.semaphore_signal(barrier, inc=1, device_id=sibling, device_id_type=MESH)
    for load in loads[2:]:
        load.start()

    def key_copy(part):
        span = pl.ds(part * UNROLL, UNROLL)
        cols = pl.ds(0, 1024)
        return pltpu.make_async_copy(kv.at[span, :, cols], kvb.at[span, :, cols], k_sem.at[part])

    def value_copy(part):
        span = pl.ds(part * UNROLL, UNROLL)
        cols = pl.ds(1024, 1024)
        return pltpu.make_async_copy(kv.at[span, :, cols], kvb.at[span, :, cols], v_sem.at[part])

    spot = z * 4 + x
    for load in loads[:2]:
        load.wait()
    own = [q[s].astype(F32) for s in range(2)]
    gat[core, y, spot] = jnp.concatenate(
        [own[0][:, :128], own[0][:, 128:], own[1][:, :128], own[1][:, 128:]], axis=0
    ).astype(BF16)
    nx[0] = jnp.concatenate([nk[0].astype(F32), nk[1].astype(F32)], axis=1)

    pl.semaphore_wait(barrier, 19)

    def turn(k):
        return (y + ((k & 1) << 1) + (k >> 1)) & 3

    def push(block, k, to):
        return pltpu.make_async_remote_copy(
            src_ref=block, dst_ref=block, send_sem=sg.at[k], recv_sem=rg.at[k],
            device_id=to, device_id_type=MESH,
        )

    def plane_copy(e):
        return push(gat.at[core, y, spot], 0, place(*beside(e, y)))

    def across_copy():
        return push(gat.at[core, y, spot], 4, place(z, ys[2], x))

    def relay_copy(e):
        return push(gat.at[core, ys[2], spot], 1, place(*beside(e, y)))

    def next_copy(m):
        return push(gat.at[core, y], 2 if m == 3 else 3, place(z, ys[m], x))

    def arrived(k, plane, blocks):
        return push(gat.at[core, plane, pl.ds(0, blocks)], k, sibling)

    def sib_copy(k, of):
        block = gat.at[of, turn(k)]
        return pltpu.make_async_remote_copy(
            src_ref=block, dst_ref=block, send_sem=s_sib.at[k], recv_sem=r_sib.at[k],
            device_id=sibling, device_id_type=MESH,
        )

    across_copy().start()

    for e in PLACES:
        plane_copy(e).start()

    @pl.loop(0, KV_PARTS)
    def _(part):
        key_copy(part).start()

    pair_rows = pltpu.make_async_remote_copy(
        src_ref=nx.at[0], dst_ref=nx.at[1], send_sem=n_sems.at[0], recv_sem=n_sems.at[1],
        device_id=sibling, device_id_type=MESH,
    )
    pair_rows.start()
    shelf = z * 2 + (x >> 1)
    side_of = (x + core) & 1

    def fresh_copy(e):
        return pltpu.make_async_remote_copy(
            src_ref=tile, dst_ref=gnt.at[y, x & 1, shelf], send_sem=n_sems.at[2], recv_sem=n_sems.at[3],
            device_id=place(*beside(e, y)), device_id_type=MESH,
        )

    def fresh_wait(tiles):
        block = gnt.at[y, side_of, pl.ds(0, tiles)]
        return pltpu.make_async_remote_copy(
            src_ref=block, dst_ref=block, send_sem=n_sems.at[2], recv_sem=n_sems.at[3],
            device_id=sibling, device_id_type=MESH,
        )

    def fresh_plane(m):
        block = gnt.at[y, side_of]
        return pltpu.make_async_remote_copy(
            src_ref=block, dst_ref=block, send_sem=n_sems.at[4], recv_sem=n_sems.at[5],
            device_id=place(z, ys[m], x), device_id_type=MESH,
        )

    def fresh_planes():
        block = gnt.at[pl.ds(0, 3), side_of]
        return pltpu.make_async_remote_copy(
            src_ref=block, dst_ref=block, send_sem=n_sems.at[4], recv_sem=n_sems.at[5],
            device_id=sibling, device_id_type=MESH,
        )

    def sib_fresh(of):
        block = gnt.at[:, (x + of) & 1]
        return pltpu.make_async_remote_copy(
            src_ref=block, dst_ref=block, send_sem=n_sems.at[6], recv_sem=n_sems.at[7],
            device_id=sibling, device_id_type=MESH,
        )

    @pl.loop(0, KV_PARTS)
    def _(part):
        value_copy(part).start()

    for load in loads[2:]:
        load.wait()
    mine = jnp.where(dev[...] == me, slot[...], -1)
    code = iota((REQS, 128), 0) * 128 + iota((REQS, 128), 1) + 1

    @pl.loop(0, SLOTS // 4)
    def _(group):
        for e in range(4):
            n = group * 4 + e
            codes[pl.ds(n, 1), :] = jnp.sum(jnp.where(mine == n, code, 0), axis=0, keepdims=True)

    owned = jnp.where(own_dev[...] == me, own_row[...], -1)
    row_code = iota((2, REQS), 0) * REQS + iota((2, REQS), 1) + 1
    pad_row = jnp.zeros((1, 96), I32)
    for e in range(4):
        hit = jnp.sum(jnp.where(owned == e, row_code, 0), axis=0, keepdims=True)
        codes[SLOTS + e : SLOTS + e + 1, :] = jnp.concatenate([hit, pad_row], axis=1)
    codes[SLOTS + 4 :, :] = jnp.zeros((4, 128), I32)

    found = jnp.broadcast_to(jnp.sum(codes[...], axis=1, keepdims=True), (40, 128))
    held = found[:SLOTS]
    req_col = jnp.where(held > 0, jnp.minimum((held - 1) >> 7, REQS - 1), -1)
    rows, lanes = iota((SLOTS, 128), 0), iota((SLOTS, 128), 1)
    req_row = jnp.sum(jnp.where(rows == lanes, req_col, 0), axis=0, keepdims=True)
    req_row = jnp.where(lanes < SLOTS, jnp.broadcast_to(req_row, (SLOTS, 128)), -2)
    same_half = (lanes >> 4) == (rows >> 4)
    before = jnp.where((req_row == req_col) & (lanes < rows) & same_half, lanes, -1)
    before = jnp.max(before, axis=1, keepdims=True)
    low = jnp.max(jnp.where((req_row == rows) & (lanes < 16), lanes, -1), axis=1, keepdims=True)
    high = jnp.max(jnp.where((req_row == rows) & (lanes >= 16), lanes - 16, -1), axis=1, keepdims=True)
    meta[:SLOTS] = jnp.where(
        lanes == 0, req_col, jnp.where(lanes == 1, held, jnp.where(lanes == 2, before, jnp.where(lanes == 3, low, high)))
    )
    meta[SLOTS:] = found[SLOTS:]
    meta_copy = pltpu.make_async_copy(meta, smeta, meta_sem)
    meta_copy.start()

    pair_rows.wait_recv()
    both_rows = [jnp.where(core == of, nx[0], nx[1]) for of in range(2)]
    tile[...] = jnp.concatenate(both_rows, axis=0).astype(BF16)

    @pl.when(core == 0)
    def _():
        gnt[y, x & 1, shelf] = tile[...]

    push(gat.at[core, ys[2], spot], 4, sibling).wait_recv()

    for e in PLACES:
        relay_copy(e).start()

    arrived(0, y, 15).wait_recv()
    sib_copy(0, core).start()
    for m in (3, 1):
        next_copy(m).start()

    for of in range(2):
        @pl.when(core == of)
        def _():
            for e in range(2 - of, 16, 2):
                fresh_copy(e).start()

    meta_copy.wait()

    @pl.loop(0, SLOTS)
    def _(n):
        req, held, prev, low, high = [smeta[n, w] for w in range(5)]
        r = jnp.maximum(req, 0)
        b = (jnp.maximum(held, 1) - 1) & 127
        info[0, n] = req
        info[1, n] = r >> 3
        info[2, n] = r & 7
        info[3, n] = jnp.where(held > 0, lens[r] - b * 128, 0)
        info[4, n] = prev
        info[5, n] = jnp.maximum(prev, 0) & 15
        info[6, n] = low
        info[7, n] = jnp.maximum(low, 0)
        info[8, n] = high
        info[9, n] = jnp.maximum(high, 0)


    @pl.loop(0, KV_PARTS)
    def _(part):
        key_copy(part).wait()

    lanes = iota((32, 128), 1)
    blank = jnp.zeros((16, 128), BF16)

    def chunk_copy(k):
        return pltpu.make_async_remote_copy(
            src_ref=s32.at[k, sib], dst_ref=r32.at[k],
            send_sem=s_chunk.at[k], recv_sem=r_chunk.at[k], device_id=sibling, device_id_type=MESH,
        )

    def peak_copy(k):
        return pltpu.make_async_remote_copy(
            src_ref=mx.at[k], dst_ref=mxr.at[k], send_sem=s_m.at[k], recv_sem=r_m.at[k],
            device_id=sibling, device_id_type=MESH,
        )

    def block_copy(k, at, to):
        return pltpu.make_async_remote_copy(
            src_ref=sb.at[turn(k), at], dst_ref=rb.at[y, spot], send_sem=b_sems.at[0, k], recv_sem=b_sems.at[1, k],
            device_id=to, device_id_type=MESH,
        )

    def side_copy(k, at, to):
        return pltpu.make_async_remote_copy(
            src_ref=ss.at[turn(k), at], dst_ref=rs.at[y, spot], send_sem=e_sems.at[0, k], recv_sem=e_sems.at[1, k],
            device_id=to, device_id_type=MESH,
        )

    def all_copy(buf, sems, k):
        block = buf.at[ys[(4 - SHIFT[k]) % 4], pl.ds(0, 16 if k else 15)]
        return pltpu.make_async_remote_copy(
            src_ref=block, dst_ref=block, send_sem=sems.at[0, k], recv_sem=sems.at[1, k],
            device_id=sibling, device_id_type=MESH,
        )

    def scores(k):
        cols = pl.ds(pl.multiple_of(turn(k) * 256, 256), 256)

        @pl.loop(0, SLOTS // GROUP, init_carry=jnp.full((32, 128), LOW, F32))
        def most(group, most):
            for e in range(GROUP):
                n = group * GROUP + e
                i, rl, count = info[1, n], info[2, n], info[3, n]
                parts = [gq[of, i, pl.ds(rl, 16, stride=8), :].reshape(2, 8, 128) for of in range(2)]
                heads = jnp.concatenate(parts, axis=1).astype(BF16)
                first = jnp.concatenate([heads[0], blank], axis=1)
                second = jnp.concatenate([blank, heads[1]], axis=1)
                score = lax.dot_general(
                    jnp.concatenate([first, second], axis=0), kvb[n, :, cols],
                    (((1,), (1,)), ((), ())), preferred_element_type=F32,
                )
                score = jnp.where(lanes < count, score * SCALE, LOW)
                peak = jnp.max(score, axis=1, keepdims=True)
                wb[n] = jnp.exp(score - peak).astype(BF16)
                pk[n] = jnp.broadcast_to(peak, (32, 128))
                most = jnp.where(lanes == info[0, n], jnp.maximum(most, peak), most)
            return most

        return most

    def values(k, most):
        cols = pl.ds(pl.multiple_of(1024 + turn(k) * 256, 256), 256)
        dn[...] = jnp.dot(
            wb[...].reshape(SLOTS * 32, 128), jnp.ones((128, 128), BF16), preferred_element_type=F32
        ).reshape(SLOTS, 32, 128)

        @pl.loop(0, SLOTS // GROUP, init_carry=jnp.zeros((32, 128), F32))
        def den(group, den):
            for e in [v for half in zip(range(16), range(16, 32)) for v in half]:
                n = group * GROUP + e
                r = info[0, n]
                best = jnp.max(jnp.where(lanes == r, most, LOW), axis=1, keepdims=True)
                factor = jnp.exp(pk[n] - best)
                both = jnp.dot(wb[n], kvb[n, :, cols], preferred_element_type=F32)
                num = jnp.concatenate([both[:16, :128], both[16:, 128:]], axis=0)
                into, at = (cb, e) if e < 16 else (cb2, e - 16)
                into[at] = num * factor + jnp.where(info[4, n] >= 0, into[info[5, n]], 0.0)
                den = den + jnp.where(lanes == r, factor * dn[n], 0.0)
            return den

        mx[k, 0] = most
        mx[k, 1] = den
        peak_copy(k).start()

    def hand_on(k):
        for i in range(4):
            for rl in range(8):
                r = i * 8 + rl
                sums = jnp.where(info[6, r] >= 0, cb[info[7, r]], 0.0) + jnp.where(
                    info[8, r] >= 0, cb2[info[9, r]], 0.0
                )
                for xh in range(2):
                    for of in range(2):
                        at = pl.ds(xh * 64 + rl, 8, stride=8)
                        s32[k, of, i, at, :] = sums[xh * 16 + of * 8 : xh * 16 + of * 8 + 8]

        chunk_copy(k).start()

    def merge(k):
        kt = turn(k)
        peak_copy(k).wait_recv()
        top, other = mx[k, 0], mxr[k, 0]
        chip_top = jnp.maximum(top, other)
        mine_f, other_f = jnp.exp(top - chip_top), jnp.exp(other - chip_top)
        chip_den = mx[k, 1] * mine_f + mxr[k, 1] * other_f
        mt[0:32, :] = chip_top
        mt[32:64, :] = chip_den
        for w in range(2):
            for xh in range(2):
                row = pl.multiple_of(w * 32 + xh * 16 + core * 8, 8)
                uw[w * 16 + xh * 8 : w * 16 + xh * 8 + 8, :] = mt[pl.ds(row, 8), :]
        lane4 = iota((4, 128), 1)
        packed = [jnp.zeros((4, 128), F32) for _ in range(4)]
        for w in range(2):
            for t in range(4):
                got = uw[pl.ds(w * 16 + t, 4, stride=4), :]
                to = w * 32 + t * 8
                for i in range(4):
                    there = pltpu.roll(got, (to - 8 * i) % 128, 1)
                    packed[i] = jnp.where((lane4 >= to) & (lane4 < to + 8), there, packed[i])
        for i in range(4):
            for j in range(4):
                ss[kt, i * 4 + j] = packed[i][j : j + 1, :]
        both_f = jnp.concatenate([mine_f, other_f, jnp.zeros((64, 128), F32)], axis=0).T
        lift[...] = pltpu.roll(both_f[0:32], (128 - core * 8) % 128, 1)
        chunk_copy(k).wait_recv()

        for i in range(4):
            factors = lift[i * 8 : i * 8 + 8, :]
            for j in range(4):
                total = []
                for t in range(4):
                    lane = (j // 2) * 16 + (j % 2) * 4 + t
                    at = slice(j * 32 + t * 8, j * 32 + t * 8 + 8)
                    total.append(
                        s32[k, core, i, at, :] * factors[:, lane : lane + 1]
                        + r32[k, i, at, :] * factors[:, 32 + lane : 33 + lane]
                    )
                sb[kt, i * 4 + j] = jnp.concatenate(total, axis=0).astype(BF16)

    def send(k):
        kt = turn(k)

        def one(e):
            pz, _, px = beside(e, kt)
            at, to = pz * 4 + px, place(pz, kt, px)
            block_copy(k, at, to).start()
            side_copy(k, at, to).start()

        for e in PLACES:
            one(e)

        @pl.when(k > 0)
        def _():
            one(0)

    def spread_fresh():
        @pl.when(core == 0)
        def _():
            fresh_wait(7).wait_recv()

        @pl.when(core == 1)
        def _():
            fresh_wait(8).wait_recv()

        for m in range(1, 4):
            fresh_plane(m).start()

    def pass_fresh():
        fresh_planes().wait_recv()
        sib_fresh(core).start()

    @pl.loop(0, 5)
    def _(k):
        @pl.when(k < 4)
        def _():
            sib_copy(k, sib).wait_recv()

            kt = turn(k)
            for of in range(2):
                for i in range(4):
                    for j in range(4):
                        gq[of, i, j * 32 : j * 32 + 32, :] = gat[of, kt, i * 4 + j].astype(F32)

            most = scores(k)

            @pl.when(k == 0)
            def _():
                arrived(1, ys[2], 15).wait_recv()
                sib_copy(1, core).start()

            @pl.when(k == 1)
            def _():
                for phase in (2, 3):
                    arrived(phase, ys[SHIFT[phase]], 16).wait_recv()
                    sib_copy(phase, core).start()

            @pl.when(k == 0)
            def _():
                @pl.loop(0, KV_PARTS)
                def _(part):
                    value_copy(part).wait()

            values(k, most)
            hand_on(k)

        @pl.when(k > 0)
        def _():
            merge(k - 1)
            send(k - 1)

        @pl.when(k == 1)
        def _():
            spread_fresh()

        @pl.when(k == 3)
        def _():
            pass_fresh()

    rb[y, spot] = sb[y, spot]
    rs[y, spot] = ss[y, spot]

    sib_fresh(sib).wait_recv()

    @pl.loop(0, 4)
    def _(i):
        for j in range(16):
            fresh = gnt[j // 4, j % 2, i * 2 + (j % 4) // 2].astype(F32)
            for of in range(2):
                gn[of, i, j * 8 : j * 8 + 8, :] = fresh[of * 8 : of * 8 + 8]

    @pl.loop(0, 4)
    def _(e):
        found_row = smeta[SLOTS + e, 0]
        which = jnp.maximum(found_row - 1, 0)
        late, r = which >> 5, which & 31
        pair = [gn[of, r >> 3, pl.ds(r & 7, 16, stride=8), :] for of in range(2)]
        tl[pl.ds(pl.multiple_of(e * 16, 16), 16), :] = jnp.where(found_row > 0, halves(pair[0], pair[1], late > 0), 0.0)
    for j in range(16):
        tail[:, j * 128 : j * 128 + 128] = tl[pl.ds(j, 4, stride=16), :].astype(BF16)

    head = y * 2 + x // 2
    new_rows = []
    for at in (head, head + 8):
        pair = [gn[of, z, pl.ds(pl.multiple_of(at * 8, 8), 8), :] for of in range(2)]
        new_rows.append([halves(pair[0], pair[1], late) for late in (False, True)])
    new_m, new_den, new_num = [], [], []
    for t in range(4):
        mine_q = q[t // 2].astype(F32)[:, (t % 2) * 128 : (t % 2) * 128 + 128]
        found_scores = [
            jnp.sum(mine_q * new_rows[0][j], axis=1, keepdims=True) * SCALE for j in range(t // 2 + 1)
        ]
        peak = found_scores[0]
        for more in found_scores[1:]:
            peak = jnp.maximum(peak, more)
        ws = [jnp.exp(v - peak).astype(BF16).astype(F32) for v in found_scores]
        new_m.append(peak)
        new_den.append(sum(ws[1:], ws[0]))
        num = ws[0] * new_rows[1][0]
        for j in range(1, len(ws)):
            num = num + ws[j] * new_rows[1][j]
        new_num.append(num)
    new_m = jnp.concatenate(new_m, axis=0)
    new_den = jnp.concatenate(new_den, axis=0)
    new_num = jnp.concatenate(new_num, axis=0)

    def take_in(phases, top, den, total):
        planes = [ys[(4 - SHIFT[k]) % 4] for k in phases]
        count = 16 * len(phases)
        for k in phases:
            all_copy(rs, e_sems, k).wait_recv()
        side = [rs[plane].reshape(16, 128) for plane in planes]
        side = jnp.concatenate(side + [jnp.zeros((128 - count, 128), F32)], axis=0).T
        side_m, side_den = side[0:32, :count], side[32:64, :count]
        new_top = jnp.maximum(jnp.max(side_m, axis=1, keepdims=True), top)
        scales = jnp.exp(side_m - new_top)
        old_scale = jnp.exp(top - new_top)
        den = jnp.sum(scales * side_den, axis=1, keepdims=True) + den * old_scale
        total = total * old_scale
        for k, plane in enumerate(planes):
            all_copy(rb, b_sems, phases[k]).wait_recv()
            for e in range(16):
                total = total + scales[:, k * 16 + e : k * 16 + e + 1] * rb[plane, e].astype(F32)
        return new_top, den, total

    state = take_in((0, 1, 2), new_m, new_den, new_num)
    _, final_den, total = take_in((3,), *state)
    result = total / final_den
    for t in range(4):
        out[t // 2, :, (t % 2) * 128 : (t % 2) * 128 + 128] = result[t * 8 : t * 8 + 8].astype(BF16)

    stores = [
        pltpu.make_async_copy(src, dst, io_sem.at[k])
        for k, (src, dst) in enumerate([(out, out_at), (tail, tail_at)])
    ]
    for store in stores:
        store.start()

    for k in range(4):
        all_copy(sb, b_sems, k).wait_send()
        all_copy(ss, e_sems, k).wait_send()
    across_copy().wait_send()
    arrived(0, y, 15).wait_send()
    arrived(1, y, 15).wait_send()
    for m in (3, 1):
        next_copy(m).wait_send()
    for k in range(4):
        sib_copy(k, core).wait_send()
        peak_copy(k).wait_send()
        chunk_copy(k).wait_send()
    pair_rows.wait_send()

    @pl.when(core == 0)
    def _():
        fresh_wait(7).wait_send()

    @pl.when(core == 1)
    def _():
        fresh_wait(8).wait_send()

    fresh_planes().wait_send()
    sib_fresh(core).wait_send()
    for store in stores:
        store.wait()


def hand_over(result, rows, out, tail, out_near, tail_near, sems):
    ways = [(result, out_near, out), (rows, tail_near, tail)]
    arrive = [pltpu.make_async_copy(a, b, sems.at[k]) for k, (a, b, _) in enumerate(ways)]
    leave = [pltpu.make_async_copy(b, c, sems.at[k]) for k, (_, b, c) in enumerate(ways)]
    for copy in arrive:
        copy.start()
    for first, second in zip(arrive, leave):
        first.wait()
        second.start()
    for copy in leave:
        copy.wait()


def per_device(kv_pool, queries, new_kv, lengths, block_dev, block_slot, owner_dev, owner_row):
    anywhere = pl.BlockSpec(memory_space=pltpu.HBM)
    dma = pltpu.SemaphoreType.DMA
    result, tail = pl.pallas_call(
        kernel,
        out_shape=(
            jax.ShapeDtypeStruct((2, 8, 256), BF16),
            jax.ShapeDtypeStruct((4, 2048), BF16),
        ),
        in_specs=[anywhere] * 8,
        out_specs=(anywhere, anywhere),
        scratch_shapes=[
            pltpu.VMEM((2, 8, 256), BF16),
            pltpu.VMEM((2, 8, 64), BF16),
            pltpu.VMEM((REQS, 128), I32),
            pltpu.VMEM((REQS, 128), I32),
            pltpu.VMEM((2, REQS), I32),
            pltpu.VMEM((2, REQS), I32),
            pltpu.SMEM((REQS,), I32),
            pltpu.VMEM((2, 8, 256), BF16),
            pltpu.VMEM((4, 2048), BF16),
            pltpu.SMEM((10, SLOTS), I32),
            pltpu.VMEM((SLOTS, 128, 2048), BF16),
            pltpu.VMEM((2, 4, 16, 32, 128), BF16),
            pltpu.VMEM((2, 8, 128), F32),
            pltpu.VMEM((16, 128), BF16),
            pltpu.VMEM((4, 2, 8, 16, 128), BF16),
            pltpu.VMEM((2, 4, 128, 128), F32),
            pltpu.VMEM((2, 4, 128, 128), F32),
            pltpu.VMEM((SLOTS, 32, 128), BF16),
            pltpu.VMEM((SLOTS, 32, 128), F32),
            pltpu.VMEM((SLOTS, 32, 128), F32),
            pltpu.VMEM((16, 32, 128), F32),
            pltpu.VMEM((16, 32, 128), F32),
            pltpu.VMEM((4, 2, 32, 128), F32),
            pltpu.VMEM((4, 2, 32, 128), F32),
            pltpu.VMEM((64, 128), F32),
            pltpu.VMEM((32, 128), F32),
            pltpu.VMEM((32, 128), F32),
            pltpu.VMEM((4, 2, 4, 128, 128), F32),
            pltpu.VMEM((4, 4, 128, 128), F32),
            pltpu.VMEM((4, 16, 32, 128), BF16),
            pltpu.VMEM((4, 16, 32, 128), BF16),
            pltpu.VMEM((4, 16, 1, 128), F32),
            pltpu.VMEM((4, 16, 1, 128), F32),
            pltpu.VMEM((64, 128), F32),
            pltpu.VMEM((40, 128), I32),
            pltpu.SMEM((40, 128), I32),
            pltpu.VMEM((40, 128), I32),
            dma((KV_PARTS,)),
            dma((KV_PARTS,)),
            dma((5,)),
            dma((5,)),
            dma((4,)),
            dma((4,)),
            dma((8,)),
            dma((4,)),
            dma((4,)),
            dma((4,)),
            dma((4,)),
            dma((2, 4)),
            dma((2, 4)),
            dma,
            dma((7,)),
        ],
        compiler_params=pltpu.CompilerParams(
            collective_id=0, has_side_effects=True, vmem_limit_bytes=56 * 1024 * 1024
        ),
    )(kv_pool, queries, new_kv, block_dev, block_slot, owner_dev, owner_row, lengths)
    return pl.pallas_call(
        hand_over,
        out_shape=(
            jax.ShapeDtypeStruct((2, 8, 256), BF16),
            jax.ShapeDtypeStruct((4, 2048), BF16),
        ),
        in_specs=[anywhere] * 2,
        out_specs=(anywhere, anywhere),
        scratch_shapes=[pltpu.VMEM((2, 8, 256), BF16), pltpu.VMEM((4, 2048), BF16), dma((2,))],
    )(result, tail)


def solution(mesh):
    placed = (
        P(("inst", "seq"), None, None),
        P(None, "inst", "seq"),
        P(None, "inst", "seq"),
        P(),
        P(),
        P(),
        P(),
        P(),
    )
    return jax.shard_map(
        per_device,
        mesh=mesh,
        in_specs=placed,
        out_specs=(P(None, "inst", "seq"), P(("inst", "seq"), None)),
        check_vma=False,
    )
```
